32 devices in a mesh: tm: 16 (over z, x, core), clip: 2 (over y).
Axes of the slice: x: 2, y: 2, z: 4, core: 2. Of those that a mesh axis runs over, the one named last changes fastest.
Arguments:
- mel_frames: bfloat16 [640, 2, 16, 80], P('tm', 'clip'), may hold values from -6 to 6
- conv_first: bfloat16 [3, 80, 768], replicated, may hold values from -0.375 to 0.375
- conv_second: bfloat16 [3, 768, 768], replicated, may hold values from -0.125 to 0.125
- enc_projection: bfloat16 [768, 2304], replicated, may hold values from -0.21875 to 0.21875
- enc_output: bfloat16 [768, 768], replicated, may hold values from -4 to 4
- enc_expand: bfloat16 [768, 3072], replicated, may hold values from -0.21875 to 0.21875
- enc_narrow: bfloat16 [3072, 768], replicated, may hold values from -0.109375 to 0.109375
- dec_input: bfloat16 [2, 16, 448, 768], P('clip', 'tm'), may hold values from -6 to 6
- lengths: int32 [2, 16], P('clip', 'tm'), may hold values from 5 to 448, as said below
- self_query: bfloat16 [768, 768], replicated, may hold values from -0.21875 to 0.21875
- self_key: bfloat16 [768, 768], replicated, may hold values from -0.21875 to 0.21875
- self_value: bfloat16 [768, 768], replicated, may hold values from -0.21875 to 0.21875
- self_output: bfloat16 [768, 768], replicated, may hold values from -3.5 to 3.5
- cross_query: bfloat16 [768, 768], replicated, may hold values from -0.21875 to 0.21875
- cross_key: bfloat16 [768, 768], replicated, may hold values from -0.21875 to 0.21875
- cross_value: bfloat16 [768, 768], replicated, may hold values from -0.21875 to 0.21875
- cross_output: bfloat16 [768, 768], replicated, may hold values from -4 to 4
- mlp_expand: bfloat16 [768, 3072], replicated, may hold values from -0.21875 to 0.21875
- mlp_narrow: bfloat16 [3072, 768], replicated, may hold values from -0.109375 to 0.109375
- gain_self: float32 [768], replicated, may hold values from 0.25 to 1.75
- gain_cross: float32 [768], replicated, may hold values from 0.25 to 1.75
- gain_mlp: float32 [768], replicated, may hold values from 0.25 to 1.75
- cotangent: bfloat16 [2, 16, 448, 768], P('clip', 'tm'), may hold values from -6 to 6
Outputs:
- encoded: bfloat16 [2, 16, 320, 768], P('clip', 'tm')
- dec_output: bfloat16 [2, 16, 448, 768], P('clip', 'tm')
- dec_input_grad: float32 [2, 16, 448, 768], P('clip', 'tm')
- enc_state_grad: float32 [2, 16, 320, 768], P('clip', 'tm')
- grad_self_query: float32 [768, 768], P('tm')
- grad_self_key: float32 [768, 768], P('tm')
- grad_self_value: float32 [768, 768], P('tm')
- grad_self_output: float32 [768, 768], P('tm')
- grad_cross_query: float32 [768, 768], P('tm')
- grad_cross_key: float32 [768, 768], P('tm')
- grad_cross_value: float32 [768, 768], P('tm')
- grad_cross_output: float32 [768, 768], P('tm')
- grad_mlp_expand: float32 [768, 3072], P('tm')
- grad_mlp_narrow: float32 [3072, 768], P('tm')
- grad_gain_self: float32 [768], P('tm')
- grad_gain_cross: float32 [768], P('tm')
- grad_gain_mlp: float32 [768], P('tm')
The draws below stay inside these ranges and needn't reach their ends.
Inputs may be any that keep to these rules, and one draw needn't show every extreme that they name: `lengths`: in each group of 16 clips one clip has length exactly 448.
All inputs are finite; a program needn't handle non-finite values.
Results may differ from the reference program's by a relative error of at most 0.034.
Values may be sent and summed in bfloat16 or wider, within the bound.
A program may use at most 192 MiB of HBM per device.

```python
import math
import jax
import jax.numpy as jnp
from jax import lax

D = 768
HEADS = 12
HD = 64
FF = 3072
MEL = 80
DEC = 448
CLIP_SETS = 2
MEMBERS = 16
CLIPS = 32
ENC = 320
FRAMES = 640


def draw_lengths(key, part):
    key = jax.random.fold_in(key, 11)
    length_key, pick_key = jax.random.split(key)
    drawn = jax.random.randint(length_key, (CLIP_SETS, MEMBERS), 5, DEC + 1, dtype=jnp.int32)
    chosen = jax.random.randint(pick_key, (CLIP_SETS, 1), 0, MEMBERS, dtype=jnp.int32)
    members = jnp.arange(MEMBERS, dtype=jnp.int32)[None, :]
    return jnp.where(members == chosen, DEC, drawn).astype(jnp.int32)


def levels(key, shape, cuts, smallest, largest):
    factor_of = 1.0
    for position, parts in cuts:
        heights = jax.random.uniform(jax.random.fold_in(jax.random.fold_in(key, 6), position), (parts,), jnp.float32, smallest / len(cuts), largest / len(cuts))
        factor_of = factor_of * jnp.repeat(jnp.exp(heights), shape[position] // parts).reshape((-1,) + (1,) * (len(shape) - 1 - position))
    return factor_of


def bell_draw(key, extent, width, bound, cuts=(), kind=jnp.bfloat16):
    factor_of = levels(key, extent, cuts, -0.22, 0.18) if cuts else 1.0
    array = jax.random.normal(key, extent, jnp.float32) * width * factor_of
    return jnp.minimum(jnp.maximum(array, -bound), bound).astype(kind)


def setup_inputs(seed: int = 0) -> dict:
    splits = jax.random.split(jax.random.key(seed), 24)
    return {
        "mel_frames": bell_draw(splits[0], (FRAMES, CLIP_SETS, MEMBERS, MEL), 1.0, 6.0, ((0, 16), (1, 2))),
        "conv_first": bell_draw(splits[1], (3, MEL, D), (3 * MEL) ** -0.5, 0.375),
        "conv_second": bell_draw(splits[2], (3, D, D), (3 * D) ** -0.5, 0.125),
        "enc_projection": bell_draw(splits[3], (D, 3 * D), D ** -0.5, 0.21875),
        "enc_output": bell_draw(splits[4], (D, D), (max(1, D // ENC)) ** -0.5, 4.0),
        "enc_expand": bell_draw(splits[5], (D, FF), D ** -0.5, 0.21875),
        "enc_narrow": bell_draw(splits[6], (FF, D), FF ** -0.5, 0.109375),
        "dec_input": bell_draw(splits[7], (CLIP_SETS, MEMBERS, DEC, D), 1.0, 6.0, ((0, 2), (1, 16))),
        "lengths": draw_lengths(jax.random.fold_in(splits[23], 71), 0),
        "self_query": bell_draw(splits[9], (D, D), D ** -0.5, 0.21875),
        "self_key": bell_draw(splits[10], (D, D), D ** -0.5, 0.21875),
        "self_value": bell_draw(splits[11], (D, D), D ** -0.5, 0.21875),
        "self_output": bell_draw(splits[12], (D, D), (max(1, 2 * D // DEC)) ** -0.5, 3.5),
        "cross_query": bell_draw(splits[13], (D, D), D ** -0.5, 0.21875),
        "cross_key": bell_draw(splits[14], (D, D), D ** -0.5, 0.21875),
        "cross_value": bell_draw(splits[15], (D, D), D ** -0.5, 0.21875),
        "cross_output": bell_draw(splits[16], (D, D), (max(1, D // ENC)) ** -0.5, 4.0),
        "mlp_expand": bell_draw(splits[17], (D, FF), D ** -0.5, 0.21875),
        "mlp_narrow": bell_draw(splits[18], (FF, D), FF ** -0.5, 0.109375),
        "gain_self": jnp.clip(1.0 + 0.15 * jax.random.normal(splits[19], (D,), jnp.float32), 0.25, 1.75),
        "gain_cross": jnp.clip(1.0 + 0.15 * jax.random.normal(splits[20], (D,), jnp.float32), 0.25, 1.75),
        "gain_mlp": jnp.clip(1.0 + 0.15 * jax.random.normal(splits[21], (D,), jnp.float32), 0.25, 1.75),
        "cotangent": bell_draw(splits[22], (CLIP_SETS, MEMBERS, DEC, D), 1.0, 6.0, ((0, 2), (1, 16))),
    }


HIGH = lax.Precision.HIGHEST

@jax.custom_vjp
def low(v):
    return lax.optimization_barrier(v.astype(jnp.bfloat16)).astype(jnp.float32)

@jax.custom_vjp
def low_back(v):
    return v

def low_keep(v):
    return (low(v), None)

def low_pass(kept, grad):
    return (grad,)

def back_keep(v):
    return (v, None)

def back_low(kept, grad):
    return (low(grad),)
low.defvjp(low_keep, low_pass)
low_back.defvjp(back_keep, back_low)

def both_ways(values):
    return low(low_back(values))

def as_float(values):
    return values.astype(jnp.float32)

def layer_norm(values):
    centre = lax.optimization_barrier(jnp.mean(values, axis=-1, keepdims=True))
    shifted = values - centre
    spread = lax.optimization_barrier(jnp.mean(shifted * shifted, axis=-1, keepdims=True))
    return shifted * lax.rsqrt(spread + 1e-05)

def matmul(left, right):
    return jnp.dot(left, right, precision=HIGH, preferred_element_type=jnp.float32)

def gelu_exact(values):
    return jax.nn.gelu(values, approximate=False)

def sinusoids(length, features):
    halfway = features // 2
    factor = math.log(10000.0) / (halfway - 1)
    inverse = jnp.exp(-factor * jnp.arange(halfway, dtype=jnp.float32))
    moments = jnp.arange(length, dtype=jnp.int32).astype(jnp.float32)
    angles = moments[:, None] * inverse[None, :]
    return jnp.concatenate([jnp.sin(angles), jnp.cos(angles)], axis=1)

def encode_clip(mel_clip, weights):
    conv_first, conv_second, projection, output_w, expand_w, narrow_w = weights
    frames = mel_clip.shape[0]
    length = frames // 2
    padded = jnp.pad(mel_clip, ((1, 1), (0, 0)))
    first_conv = sum((matmul(padded[offset:offset + frames], conv_first[offset]) for offset in range(3)))
    stem_rows = low(gelu_exact(first_conv))
    padded = jnp.pad(stem_rows, ((1, 1), (0, 0)))
    second = sum((matmul(padded[offset:offset + frames:2], conv_second[offset]) for offset in range(3)))
    state = gelu_exact(second) + sinusoids(length, D)
    joint = matmul(low(layer_norm(state)), projection)
    queries = low(joint[:, :D]).reshape(length, HEADS, HD)
    key_part = low(joint[:, D:2 * D]).reshape(length, HEADS, HD)
    value_part = low(joint[:, 2 * D:]).reshape(length, HEADS, HD)
    scores = jnp.einsum('qhd,khd->hqk', queries, key_part, precision=HIGH) * HD ** (-0.5)
    highest = lax.optimization_barrier(jnp.max(scores, axis=-1, keepdims=True))
    raised = jnp.exp(scores - highest)
    mixed = jnp.einsum('hqk,khd->qhd', low(raised), value_part, precision=HIGH)
    mixed = mixed / jnp.transpose(lax.optimization_barrier(jnp.sum(raised, axis=-1)))[:, :, None]
    state = state + matmul(low(mixed.reshape(length, D)), output_w)
    widened = low(gelu_exact(matmul(low(layer_norm(state)), expand_w)))
    state = state + matmul(widened, narrow_w)
    return low(layer_norm(state))

def attend(queries, key_part, value_part, allowed):
    row_count = queries.shape[0]
    scores = jnp.einsum('qhd,khd->hqk', queries.reshape(row_count, HEADS, HD), key_part.reshape(-1, HEADS, HD), precision=HIGH)
    scores = low_back(scores * HD ** (-0.5))
    scores = jnp.where(allowed[None], scores, -1e+30)
    highest = lax.optimization_barrier(jnp.max(scores, axis=-1, keepdims=True))
    raised = jnp.exp(scores - highest)
    probs = raised / lax.optimization_barrier(jnp.sum(raised, axis=-1, keepdims=True))
    mixed = jnp.einsum('hqk,khd->qhd', low(probs), value_part.reshape(-1, HEADS, HD), precision=HIGH)
    return both_ways(mixed.reshape(row_count, D))

def decode_clip(inputs, states, length, weights):
    self_query, self_key, self_value, self_output, cross_query, cross_key, cross_value, cross_output, mlp_expand, mlp_narrow, gain_self, gain_cross, gain_mlp = weights
    row_count = inputs.shape[0]
    places = jnp.arange(row_count, dtype=jnp.int32)
    normed = low(layer_norm(inputs) * gain_self)
    queries = both_ways(matmul(normed, self_query))
    key_part = both_ways(matmul(normed, self_key))
    value_part = both_ways(matmul(normed, self_value))
    allowed = (places[None, :] <= places[:, None]) & (places[None, :] < length)
    after_self = inputs + low_back(matmul(attend(queries, key_part, value_part, allowed), self_output))
    normed = low(layer_norm(after_self) * gain_cross)
    queries = both_ways(matmul(normed, cross_query))
    key_part = both_ways(matmul(states, cross_key))
    value_part = both_ways(matmul(states, cross_value))
    everywhere = jnp.ones((row_count, states.shape[0]), dtype=jnp.bool_)
    after_cross = after_self + low_back(matmul(attend(queries, key_part, value_part, everywhere), cross_output))
    normed = low(layer_norm(after_cross) * gain_mlp)
    hidden = low_back(matmul(normed, mlp_expand))
    after_mlp = after_cross + low_back(matmul(low(gelu_exact(hidden)), mlp_narrow))
    return jnp.where((places < length)[:, None], after_mlp, 0.0)

def reference(mel_frames, conv_first, conv_second, enc_projection, enc_output, enc_expand, enc_narrow, dec_input, lengths, self_query, self_key, self_value, self_output, cross_query, cross_key, cross_value, cross_output, mlp_expand, mlp_narrow, gain_self, gain_cross, gain_mlp, cotangent):
    enc_weights = tuple((as_float(matrix) for matrix in (conv_first, conv_second, enc_projection, enc_output, enc_expand, enc_narrow)))
    mel_clips = jnp.moveaxis(as_float(mel_frames).reshape(FRAMES, CLIPS, MEL), 1, 0)
    dec_weights = tuple((as_float(matrix) for matrix in (self_query, self_key, self_value, self_output, cross_query, cross_key, cross_value, cross_output, mlp_expand, mlp_narrow, gain_self, gain_cross, gain_mlp)))
    inputs = as_float(dec_input).reshape(CLIPS, DEC, D)
    seed_grad = as_float(cotangent).reshape(CLIPS, DEC, D)
    clip_lengths = lengths.reshape(CLIPS)
    per_clip = jax.checkpoint(decode_clip)
    state_shift = jnp.zeros((CLIPS, ENC, D), jnp.float32)

    def forward(clip_inputs, shift, weights):
        encoded = lax.map(lambda single: encode_clip(single, enc_weights), mel_clips)
        clip_states = encoded + shift
        result = lax.map(lambda triple: per_clip(triple[0], triple[1], triple[2], weights), (clip_inputs, clip_states, clip_lengths))
        return (result, encoded)
    result, backward, encoded = jax.vjp(forward, inputs, state_shift, dec_weights, has_aux=True)
    input_grad, state_grad, weight_grads = backward(seed_grad)
    return (encoded.reshape(CLIP_SETS, MEMBERS, ENC, D).astype(jnp.bfloat16), result.reshape(CLIP_SETS, MEMBERS, DEC, D).astype(jnp.bfloat16), input_grad.reshape(CLIP_SETS, MEMBERS, DEC, D), state_grad.reshape(CLIP_SETS, MEMBERS, ENC, D), weight_grads[0], weight_grads[1], weight_grads[2], weight_grads[3], weight_grads[4], weight_grads[5], weight_grads[6], weight_grads[7], weight_grads[8], weight_grads[9], weight_grads[10], weight_grads[11], weight_grads[12])
```

```python
import functools
import math

import jax
import jax.numpy as jnp
from jax import lax
from jax.sharding import PartitionSpec as P

D = 768
HEADS = 12
HD = 64


def layer_norm(values):
    centre = jnp.mean(values, axis=-1, keepdims=True)
    shifted = values - centre
    spread = jnp.mean(shifted * shifted, axis=-1, keepdims=True)
    return shifted * lax.rsqrt(spread + 1e-05)


def scaled_norm(values, norm_gain):
    return layer_norm(values) * norm_gain


def gelu_exact(values):
    return jax.nn.gelu(values, approximate=False)


def project(activations, weight):
    return jnp.einsum("ctd,de->cte", activations, weight, preferred_element_type=jnp.float32)


def project_back(gradient, weight):
    return jnp.einsum("cte,de->ctd", gradient, weight, preferred_element_type=jnp.float32)


def weight_grad(activations, gradient):
    return jnp.einsum("ctd,cte->de", activations, gradient, preferred_element_type=jnp.float32)


def split_heads(values):
    return values.reshape(values.shape[0], values.shape[1], HEADS, HD)


def merge_heads(values):
    return values.reshape(values.shape[0], values.shape[1], HEADS * HD)


def pair_products(left, right):
    return jnp.einsum(
        "cqhd,ckhd->chqk", split_heads(left), split_heads(right), preferred_element_type=jnp.float32
    )


def apply_probs(probs, values):
    return merge_heads(
        jnp.einsum(
            "chqk,ckhd->cqhd", probs, split_heads(values), preferred_element_type=jnp.float32
        )
    )


def key_grads(probs, values):
    return merge_heads(
        jnp.einsum(
            "chqk,cqhd->ckhd", probs, split_heads(values), preferred_element_type=jnp.float32
        )
    )


def normalize(scores):
    highest = jnp.max(scores, axis=-1, keepdims=True)
    raised = jnp.exp(scores - highest)
    return raised / jnp.sum(raised, axis=-1, keepdims=True)


def score_grads(probs, products):
    weighted = jnp.sum(probs * products, axis=-1, keepdims=True)
    return (probs * (products - weighted)).astype(jnp.bfloat16)


def sinusoids(length, features):
    halfway = features // 2
    factor = math.log(10000.0) / (halfway - 1)
    inverse = jnp.exp(-factor * jnp.arange(halfway, dtype=jnp.float32))
    moments = jnp.arange(length, dtype=jnp.int32).astype(jnp.float32)
    angles = moments[:, None] * inverse[None, :]
    return jnp.concatenate([jnp.sin(angles), jnp.cos(angles)], axis=1)


def encode(mel_clips, conv_first, conv_second, enc_projection, enc_output, enc_expand, enc_narrow):
    frames = mel_clips.shape[1]
    length = frames // 2
    padded = jnp.pad(mel_clips, ((0, 0), (1, 1), (0, 0)))
    first_conv = sum(
        (project(padded[:, offset : offset + frames], conv_first[offset]) for offset in range(3))
    )
    stem_rows = gelu_exact(first_conv).astype(jnp.bfloat16)
    padded = jnp.pad(stem_rows, ((0, 0), (1, 1), (0, 0)))
    second = sum(
        (
            project(padded[:, offset : offset + frames : 2], conv_second[offset])
            for offset in range(3)
        )
    )
    state = gelu_exact(second) + sinusoids(length, D)[None]
    joint = project(layer_norm(state).astype(jnp.bfloat16), enc_projection)
    queries = joint[..., :D].astype(jnp.bfloat16)
    key_part = joint[..., D : 2 * D].astype(jnp.bfloat16)
    value_part = joint[..., 2 * D :].astype(jnp.bfloat16)
    scores = pair_products(queries, key_part) * HD ** (-0.5)
    highest = jnp.max(scores, axis=-1, keepdims=True)
    raised = jnp.exp(scores - highest)
    totals = jnp.transpose(jnp.sum(raised, axis=-1), (0, 2, 1))
    mixed = jnp.einsum(
        "chqk,ckhd->cqhd",
        raised.astype(jnp.bfloat16),
        split_heads(value_part),
        preferred_element_type=jnp.float32,
    )
    mixed = merge_heads(mixed / totals[..., None]).astype(jnp.bfloat16)
    state = state + project(mixed, enc_output)
    widened = gelu_exact(project(layer_norm(state).astype(jnp.bfloat16), enc_expand)).astype(
        jnp.bfloat16
    )
    state = state + project(widened, enc_narrow)
    return layer_norm(state).astype(jnp.bfloat16)


def trade(values, axis, size, bit):
    return lax.ppermute(values, axis, [(i, i ^ bit) for i in range(size)])


def add_rounded(left, right):
    return (left.astype(jnp.float32) + right.astype(jnp.float32)).astype(jnp.bfloat16)


def halve(values, dim, axis, size, bit):
    mine = (lax.axis_index(axis) // bit) % 2
    kept = lax.dynamic_index_in_dim(values, mine, dim, keepdims=False)
    sent = lax.dynamic_index_in_dim(values, 1 - mine, dim, keepdims=False)
    return add_rounded(kept, trade(sent, axis, size, bit))


def bits_of(size):
    return [1 << k for k in range(size.bit_length() - 1)]


def members_first(values, members, groups):
    for bit in bits_of(members):
        values = halve(values, len(values.shape) - 3, "tm", members, bit)
    for bit in bits_of(groups):
        values = add_rounded(values, trade(values, "clip", groups, bit))
    return values.astype(jnp.float32)


def groups_first(values, members, groups):
    values = halve(values, len(values.shape) - 3, "tm", members, 1)
    lead = values.shape[:-2]
    rows, columns = values.shape[-2:]
    for bit in bits_of(groups):
        values = values.reshape(lead + (2, values.shape[-2] // 2, columns))
        values = halve(values, len(lead), "clip", groups, bit)
    for bit in bits_of(members)[1:]:
        values = halve(values, len(values.shape) - 3, "tm", members, bit)
    for bit in bits_of(groups)[::-1]:
        mine = (lax.axis_index("clip") // bit) % 2
        other = trade(values, "clip", groups, bit)
        values = jnp.where(
            mine == 0, jnp.concatenate([values, other]), jnp.concatenate([other, values])
        )
    return values.astype(jnp.float32)


def reduce_grads(sets, members, groups):
    split = (2,) * (members.bit_length() - 1)
    results = []
    for matrices in sets:
        blocks = [
            matrix.astype(jnp.bfloat16).reshape(members, matrix.shape[0] // members, matrix.shape[1])
            for matrix in matrices
        ]
        widths = [matrix.shape[1] for matrix in matrices]
        if len(blocks) == 4:
            first, second = blocks[:2], blocks[2:]
        else:
            half = blocks[0].shape[2] // 2
            first, second = [blocks[0][:, :, :half]], [blocks[0][:, :, half:]]
        streams = []
        for parts, way in ((first, members_first), (second, groups_first)):
            joined = jnp.concatenate(parts, axis=2) if len(parts) > 1 else parts[0]
            streams.append(way(joined.reshape(split + joined.shape[1:]), members, groups))
        joined = jnp.concatenate(streams, axis=1)
        edges = [sum(widths[: k + 1]) for k in range(len(widths) - 1)]
        results.append(jnp.split(joined, edges, axis=1))
    return results


def body(
    members,
    groups,
    mel_frames,
    conv_first,
    conv_second,
    enc_projection,
    enc_output,
    enc_expand,
    enc_narrow,
    dec_input,
    lengths,
    self_query,
    self_key,
    self_value,
    self_output,
    cross_query,
    cross_key,
    cross_value,
    cross_output,
    mlp_expand,
    mlp_narrow,
    gain_self,
    gain_cross,
    gain_mlp,
    cotangent,
):
    arrived = lax.all_to_all(mel_frames, "tm", split_axis=2, concat_axis=0, tiled=True)
    mel_clips = jnp.transpose(arrived[:, 0], (1, 0, 2))
    encoded = encode(
        mel_clips, conv_first, conv_second, enc_projection, enc_output, enc_expand, enc_narrow
    )
    scale = HD ** (-0.5)
    inputs = dec_input[0].astype(jnp.float32)
    clip_lengths = lengths[0]
    places = jnp.arange(inputs.shape[1], dtype=jnp.int32)
    live_rows = places[None, :] < clip_lengths[:, None]
    h_self = scaled_norm(inputs, gain_self).astype(jnp.bfloat16)
    q_self = project(h_self, self_query).astype(jnp.bfloat16)
    k_self = project(h_self, self_key).astype(jnp.bfloat16)
    v_self = project(h_self, self_value).astype(jnp.bfloat16)
    allowed = (places[None, None, :] <= places[None, :, None]) & (
        places[None, None, :] < clip_lengths[:, None, None]
    )
    p_self = normalize(jnp.where(allowed[:, None], pair_products(q_self, k_self) * scale, -1e30))
    pb_self = p_self.astype(jnp.bfloat16)
    o_self = apply_probs(pb_self, v_self).astype(jnp.bfloat16)
    after_self = inputs + project(o_self, self_output)
    h_cross = scaled_norm(after_self, gain_cross).astype(jnp.bfloat16)
    q_cross = project(h_cross, cross_query).astype(jnp.bfloat16)
    k_cross = project(encoded, cross_key).astype(jnp.bfloat16)
    v_cross = project(encoded, cross_value).astype(jnp.bfloat16)
    p_cross = normalize(pair_products(q_cross, k_cross) * scale)
    pb_cross = p_cross.astype(jnp.bfloat16)
    o_cross = apply_probs(pb_cross, v_cross).astype(jnp.bfloat16)
    after_cross = after_self + project(o_cross, cross_output)
    h_mlp = scaled_norm(after_cross, gain_mlp).astype(jnp.bfloat16)
    hidden = project(h_mlp, mlp_expand)
    activated = gelu_exact(hidden).astype(jnp.bfloat16)
    after_mlp = after_cross + project(activated, mlp_narrow)
    dec_output = jnp.where(live_rows[..., None], after_mlp, 0.0).astype(jnp.bfloat16)
    grad_three = jnp.where(live_rows[..., None], cotangent[0].astype(jnp.float32), 0.0)
    branch_three = grad_three.astype(jnp.bfloat16)
    g_narrow = weight_grad(activated, branch_three)
    d_active = project_back(branch_three, mlp_narrow)
    gelu_value, gelu_back = jax.vjp(gelu_exact, hidden)
    d_hidden = gelu_back(d_active)[0].astype(jnp.bfloat16)
    g_expand = weight_grad(h_mlp, d_hidden)
    d_h_mlp = project_back(d_hidden, mlp_expand)
    norm_value, norm_back = jax.vjp(scaled_norm, after_cross, gain_mlp)
    d_part, g_gain_mlp = norm_back(d_h_mlp)
    grad_two = grad_three + d_part
    branch_two = grad_two.astype(jnp.bfloat16)
    g_cross_out = weight_grad(o_cross, branch_two)
    d_o_cross = project_back(branch_two, cross_output).astype(jnp.bfloat16)
    ds_cross = score_grads(p_cross, pair_products(d_o_cross, v_cross))
    d_q_cross = (apply_probs(ds_cross, k_cross) * scale).astype(jnp.bfloat16)
    d_k_cross = (key_grads(ds_cross, q_cross) * scale).astype(jnp.bfloat16)
    d_v_cross = key_grads(pb_cross, d_o_cross).astype(jnp.bfloat16)
    g_cross_query = weight_grad(h_cross, d_q_cross)
    g_cross_key = weight_grad(encoded, d_k_cross)
    g_cross_value = weight_grad(encoded, d_v_cross)
    enc_state_grad = project_back(d_k_cross, cross_key) + project_back(d_v_cross, cross_value)
    d_h_cross = project_back(d_q_cross, cross_query)
    norm_value, norm_back = jax.vjp(scaled_norm, after_self, gain_cross)
    d_part, g_gain_cross = norm_back(d_h_cross)
    grad_one = grad_two + d_part
    branch_one = grad_one.astype(jnp.bfloat16)
    g_self_out = weight_grad(o_self, branch_one)
    d_o_self = project_back(branch_one, self_output).astype(jnp.bfloat16)
    ds_self = score_grads(p_self, pair_products(d_o_self, v_self))
    d_q_self = (apply_probs(ds_self, k_self) * scale).astype(jnp.bfloat16)
    d_k_self = (key_grads(ds_self, q_self) * scale).astype(jnp.bfloat16)
    d_v_self = key_grads(pb_self, d_o_self).astype(jnp.bfloat16)
    g_self_query = weight_grad(h_self, d_q_self)
    g_self_key = weight_grad(h_self, d_k_self)
    g_self_value = weight_grad(h_self, d_v_self)
    d_h_self = (
        project_back(d_q_self, self_query)
        + project_back(d_k_self, self_key)
        + project_back(d_v_self, self_value)
    )
    norm_value, norm_back = jax.vjp(scaled_norm, inputs, gain_self)
    d_part, g_gain_self = norm_back(d_h_self)
    dec_input_grad = grad_one + d_part
    grads = reduce_grads(
        [
            [g_narrow],
            [g_expand],
            [g_cross_query, g_cross_key, g_cross_value, g_cross_out],
            [g_self_query, g_self_key, g_self_value, g_self_out],
        ],
        members,
        groups,
    )
    (total_narrow,) = grads[0]
    (total_expand,) = grads[1]
    gains = lax.psum(jnp.stack([g_gain_self, g_gain_cross, g_gain_mlp]), ("tm", "clip"))
    part = D // members
    gains = lax.dynamic_slice_in_dim(gains, lax.axis_index("tm") * part, part, 1)
    cross_query_t, cross_key_t, cross_value_t, cross_out_t = grads[2]
    self_query_t, self_key_t, self_value_t, self_out_t = grads[3]
    totals = (
        self_query_t, self_key_t, self_value_t, self_out_t,
        cross_query_t, cross_key_t, cross_value_t, cross_out_t,
        total_expand, total_narrow, gains[0], gains[1], gains[2],
    )
    return (
        encoded[None],
        dec_output[None],
        dec_input_grad[None],
        enc_state_grad[None],
        totals[0],
        totals[1],
        totals[2],
        totals[3],
        totals[4],
        totals[5],
        totals[6],
        totals[7],
        totals[8],
        totals[9],
        totals[10],
        totals[11],
        totals[12],
    )


def solution(mesh):
    placed = (
        P("tm", "clip", None, None),
        P(),
        P(),
        P(),
        P(),
        P(),
        P(),
        P("clip", "tm", None, None),
        P("clip", "tm"),
        P(),
        P(),
        P(),
        P(),
        P(),
        P(),
        P(),
        P(),
        P(),
        P(),
        P(),
        P(),
        P(),
        P("clip", "tm", None, None),
    )
    return jax.shard_map(
        functools.partial(body, mesh.shape["tm"], mesh.shape["clip"]),
        mesh=mesh,
        in_specs=placed,
        out_specs=(
            P("clip", "tm", None, None),
            P("clip", "tm", None, None),
            P("clip", "tm", None, None),
            P("clip", "tm", None, None),
            P("tm", None),
            P("tm", None),
            P("tm", None),
            P("tm", None),
            P("tm", None),
            P("tm", None),
            P("tm", None),
            P("tm", None),
            P("tm", None),
            P("tm", None),
            P("tm"),
            P("tm"),
            P("tm"),
        ),
        check_vma=False,
    )
```

```python
import functools
import math

import jax
import jax.numpy as jnp
from jax import lax
from jax.experimental import pallas as pl
from jax.experimental.pallas import tpu as pltpu
from jax.sharding import PartitionSpec as P

D = 768
HEADS = 12
HD = 64


def layer_norm(values):
    centre = jnp.mean(values, axis=-1, keepdims=True)
    shifted = values - centre
    spread = jnp.mean(shifted * shifted, axis=-1, keepdims=True)
    return shifted * lax.rsqrt(spread + 1e-05)


def scaled_norm(values, norm_gain):
    return layer_norm(values) * norm_gain


def gelu_exact(values):
    return jax.nn.gelu(values, approximate=False)


def project(activations, weight):
    return jnp.einsum("ctd,de->cte", activations, weight, preferred_element_type=jnp.float32)


def project_back(gradient, weight):
    return jnp.einsum("cte,de->ctd", gradient, weight, preferred_element_type=jnp.float32)


def weight_grad(activations, gradient):
    return jnp.einsum("ctd,cte->de", activations, gradient, preferred_element_type=jnp.float32)


def split_heads(values):
    return values.reshape(values.shape[0], values.shape[1], HEADS, HD)


def merge_heads(values):
    return values.reshape(values.shape[0], values.shape[1], HEADS * HD)


def pair_products(left, right):
    return jnp.einsum(
        "cqhd,ckhd->chqk", split_heads(left), split_heads(right), preferred_element_type=jnp.float32
    )


def apply_probs(probs, values):
    return merge_heads(
        jnp.einsum(
            "chqk,ckhd->cqhd", probs, split_heads(values), preferred_element_type=jnp.float32
        )
    )


def key_grads(probs, values):
    return merge_heads(
        jnp.einsum(
            "chqk,cqhd->ckhd", probs, split_heads(values), preferred_element_type=jnp.float32
        )
    )


def normalize(scores):
    highest = jnp.max(scores, axis=-1, keepdims=True)
    raised = jnp.exp(scores - highest)
    return raised / jnp.sum(raised, axis=-1, keepdims=True)


def score_grads(probs, products):
    weighted = jnp.sum(probs * products, axis=-1, keepdims=True)
    return (probs * (products - weighted)).astype(jnp.bfloat16)


def sinusoids(length, features):
    halfway = features // 2
    factor = math.log(10000.0) / (halfway - 1)
    inverse = jnp.exp(-factor * jnp.arange(halfway, dtype=jnp.float32))
    moments = jnp.arange(length, dtype=jnp.int32).astype(jnp.float32)
    angles = moments[:, None] * inverse[None, :]
    return jnp.concatenate([jnp.sin(angles), jnp.cos(angles)], axis=1)


def encode(mel_clips, conv_first, conv_second, enc_projection, enc_output, enc_expand, enc_narrow):
    frames = mel_clips.shape[1]
    length = frames // 2
    padded = jnp.pad(mel_clips, ((0, 0), (1, 1), (0, 0)))
    first_conv = sum(
        (project(padded[:, offset : offset + frames], conv_first[offset]) for offset in range(3))
    )
    stem_rows = gelu_exact(first_conv).astype(jnp.bfloat16)
    padded = jnp.pad(stem_rows, ((0, 0), (1, 1), (0, 0)))
    second = sum(
        (
            project(padded[:, offset : offset + frames : 2], conv_second[offset])
            for offset in range(3)
        )
    )
    state = gelu_exact(second) + sinusoids(length, D)[None]
    joint = project(layer_norm(state).astype(jnp.bfloat16), enc_projection)
    queries = joint[..., :D].astype(jnp.bfloat16)
    key_part = joint[..., D : 2 * D].astype(jnp.bfloat16)
    value_part = joint[..., 2 * D :].astype(jnp.bfloat16)
    scores = pair_products(queries, key_part) * HD ** (-0.5)
    highest = jnp.max(scores, axis=-1, keepdims=True)
    raised = jnp.exp(scores - highest)
    totals = jnp.transpose(jnp.sum(raised, axis=-1), (0, 2, 1))
    mixed = jnp.einsum(
        "chqk,ckhd->cqhd",
        raised.astype(jnp.bfloat16),
        split_heads(value_part),
        preferred_element_type=jnp.float32,
    )
    mixed = merge_heads(mixed / totals[..., None]).astype(jnp.bfloat16)
    state = state + project(mixed, enc_output)
    widened = gelu_exact(project(layer_norm(state).astype(jnp.bfloat16), enc_expand)).astype(
        jnp.bfloat16
    )
    state = state + project(widened, enc_narrow)
    return layer_norm(state).astype(jnp.bfloat16)


def trade(values, axis, size, bit):
    return lax.ppermute(values, axis, [(i, i ^ bit) for i in range(size)])


def add_rounded(left, right):
    return (left.astype(jnp.float32) + right.astype(jnp.float32)).astype(jnp.bfloat16)


def halve(values, dim, axis, size, bit):
    mine = (lax.axis_index(axis) // bit) % 2
    kept = lax.dynamic_index_in_dim(values, mine, dim, keepdims=False)
    sent = lax.dynamic_index_in_dim(values, 1 - mine, dim, keepdims=False)
    return add_rounded(kept, trade(sent, axis, size, bit))


def bits_of(size):
    return [1 << k for k in range(size.bit_length() - 1)]


def members_first(values, members, groups):
    for bit in bits_of(members):
        values = halve(values, len(values.shape) - 3, "tm", members, bit)
    for bit in bits_of(groups):
        values = add_rounded(values, trade(values, "clip", groups, bit))
    return values.astype(jnp.float32)


def groups_first(values, members, groups):
    values = halve(values, len(values.shape) - 3, "tm", members, 1)
    lead = values.shape[:-2]
    rows, columns = values.shape[-2:]
    for bit in bits_of(groups):
        values = values.reshape(lead + (2, values.shape[-2] // 2, columns))
        values = halve(values, len(lead), "clip", groups, bit)
    for bit in bits_of(members)[1:]:
        values = halve(values, len(values.shape) - 3, "tm", members, bit)
    for bit in bits_of(groups)[::-1]:
        mine = (lax.axis_index("clip") // bit) % 2
        other = trade(values, "clip", groups, bit)
        values = jnp.where(
            mine == 0, jnp.concatenate([values, other]), jnp.concatenate([other, values])
        )
    return values.astype(jnp.float32)


def sum_plain(matrices, gains, members, groups):
    split = (2,) * (members.bit_length() - 1)
    totals = []
    for place, matrix in enumerate(matrices):
        blocks = matrix.reshape(split + (matrix.shape[0] // members, matrix.shape[1]))
        totals.append((members_first, groups_first)[place % 2](blocks, members, groups))
    return tuple(totals), lax.psum(gains, ("tm", "clip"))


MESH = pl.DeviceIdType.MESH
PART = 48
UNITS = 16
UNIT_ORDER = (12, 8, 13, 9, 14, 10, 15, 11, 7, 4, 5, 6, 3, 0, 1, 2)


def add_halves(left, right):
    return (left.astype(jnp.float32) + right.astype(jnp.float32)).astype(jnp.bfloat16)


def sum_kernel(*refs):
    matrices, gain_in = refs[:10], refs[10]
    out, gain_out = refs[11:13]
    (own, got0, a1, a2, a3, a4, b1, b2, b3, b4, b5, gain_sum, gain_got) = refs[13:26]
    own_sem, send_sem, recv_sem, gain_send, gain_recv = refs[26:]
    tm, clip = lax.axis_index("tm"), lax.axis_index("clip")
    core, along_x, low_z, high_z = tm % 2, (tm // 2) % 2, (tm // 4) % 2, tm // 8
    core_peer, x_peer, low_peer, high_peer = (
        (tm + 1 - 2 * core, clip),
        (tm + 2 - 4 * along_x, clip),
        (tm + 4 - 8 * low_z, clip),
        (tm + 8 - 16 * high_z, clip),
    )
    clip_peer = (tm, 1 - clip)
    peers = (core_peer, x_peer, low_peer, high_peer, clip_peer)
    barrier = pltpu.get_barrier_semaphore()
    for peer in peers:
        pl.semaphore_signal(barrier, inc=1, device_id=peer, device_id_type=MESH)
    pl.semaphore_wait(barrier, len(peers))

    def source(unit, side):
        if unit < 8:
            return matrices[unit].at[:, :, :, side]
        if unit < 12:
            return matrices[8].at[:, :, :, side, :, pl.ds((unit - 8) * D, D)]
        return matrices[9].at[:, :, :, side, unit - 12]

    started = []

    def send(src, dst, stage, unit, peer):
        copy = pltpu.make_async_remote_copy(
            src_ref=src,
            dst_ref=dst,
            send_sem=send_sem.at[stage, unit],
            recv_sem=recv_sem.at[stage, unit],
            device_id=peer,
            device_id_type=MESH,
        )
        copy.start()
        started.append(copy)
        return copy

    copies = {}
    own_columns = pl.ds(pl.multiple_of(clip * (D // 2), D // 2), D // 2)
    other_columns = pl.ds(pl.multiple_of((1 - clip) * (D // 2), D // 2), D // 2)

    def begin(place):
        unit = UNIT_ORDER[place]
        keep = pltpu.make_async_copy(source(unit, core), own.at[place], own_sem.at[place])
        keep.start()
        copies[0, place] = send(source(unit, 1 - core), got0.at[place], 0, place, core_peer)
        copies["own", place] = keep

    def step(stage, place):
        pair = place // 2
        if place % 2 == 0 and stage > 5 or stage > 6:
            return
        copies[stage - 1, place].wait_recv()
        if stage == 1:
            copies["own", place].wait()

            @pl.loop(0, 8)
            def _(block):
                i, j, k = block // 4, (block // 2) % 2, block % 2
                got0[place, i, j, k] = add_halves(got0[place, i, j, k], own[place, i, j, k])

        if place % 2 == 0:
            if stage == 1:
                copies[1, place] = send(
                    got0.at[place, :, :, 1 - along_x], a1.at[pair], 1, place, x_peer
                )
            elif stage == 2:

                @pl.loop(0, 4)
                def _(block):
                    i, j = block // 2, block % 2
                    a1[pair, i, j] = add_halves(a1[pair, i, j], got0[place, i, j, along_x])

                copies[2, place] = send(a1.at[pair, :, 1 - low_z], a2.at[pair], 2, place, low_peer)
            elif stage == 3:

                @pl.loop(0, 2)
                def _(i):
                    a2[pair, i] = add_halves(a2[pair, i], a1[pair, i, low_z])

                copies[3, place] = send(a2.at[pair, 1 - high_z], a3.at[pair], 3, place, high_peer)
            elif stage == 4:
                a3[pair] = add_halves(a3[pair], a2[pair, high_z])
                copies[4, place] = send(a3.at[pair], a4.at[pair], 4, place, clip_peer)
            elif stage == 5:
                out[UNIT_ORDER[place]] = a3[pair].astype(jnp.float32) + a4[pair].astype(jnp.float32)
            return
        if stage == 1:
            copies[1, place] = send(
                got0.at[place, :, :, :, :, other_columns], b1.at[pair], 1, place, clip_peer
            )
        elif stage == 2:

            @pl.loop(0, 8)
            def _(block):
                i, j, k = block // 4, (block // 2) % 2, block % 2
                b1[pair, i, j, k] = add_halves(
                    b1[pair, i, j, k], got0[place, i, j, k, :, own_columns]
                )

            copies[2, place] = send(b1.at[pair, :, :, 1 - along_x], b2.at[pair], 2, place, x_peer)
        elif stage == 3:

            @pl.loop(0, 4)
            def _(block):
                i, j = block // 2, block % 2
                b2[pair, i, j] = add_halves(b2[pair, i, j], b1[pair, i, j, along_x])

            copies[3, place] = send(b2.at[pair, :, 1 - low_z], b3.at[pair], 3, place, low_peer)
        elif stage == 4:

            @pl.loop(0, 2)
            def _(i):
                b3[pair, i] = add_halves(b3[pair, i], b2[pair, i, low_z])

            copies[4, place] = send(b3.at[pair, 1 - high_z], b4.at[pair], 4, place, high_peer)
        elif stage == 5:
            b4[pair] = add_halves(b4[pair], b3[pair, high_z])
            copies[5, place] = send(b4.at[pair], b5.at[pair], 5, place, clip_peer)
        elif stage == 6:
            out[UNIT_ORDER[place], :, own_columns] = b4[pair].astype(jnp.float32)
            out[UNIT_ORDER[place], :, other_columns] = b5[pair].astype(jnp.float32)

    gain_copies = {}

    def gain_step(number):
        if number == 0:
            gain_sum[0] = gain_in[...]
        else:
            gain_copies[number - 1].wait_recv()
            gain_sum[number] = gain_sum[number - 1] + gain_got[number - 1]
        if number == len(peers):
            gain_out[...] = gain_sum[number]
            return
        copy = pltpu.make_async_remote_copy(
            src_ref=gain_sum.at[number],
            dst_ref=gain_got.at[number],
            send_sem=gain_send.at[number],
            recv_sem=gain_recv.at[number],
            device_id=peers[number],
            device_id_type=MESH,
        )
        copy.start()
        started.append(copy)
        gain_copies[number] = copy

    pairs = UNITS // 2
    ahead = 2
    for place in range(UNITS):
        begin(place)
    for tick in range(-ahead, pairs + 5):
        if 0 <= tick <= len(peers):
            gain_step(tick)
        for stage in range(1, 7):
            pair = tick + ahead if stage == 1 else tick + 2 - stage
            if 0 <= pair < pairs:
                step(stage, 2 * pair + 1)
                step(stage, 2 * pair)
    for copy in started:
        copy.wait_send()


def sum_gradients(matrices, gains, members, groups):
    if (members, groups) != (16, 2):
        return sum_plain(matrices, gains, members, groups)
    shaped = [
        matrix.reshape((2, 2, 2, 2, PART, matrix.shape[1])) for matrix in matrices[:9]
    ] + [matrices[9].reshape((2, 2, 2, 2, 4, PART, D))]
    low, half = jnp.bfloat16, UNITS // 2
    wide, thin = (PART, D), (PART, D // 2)
    everywhere = pl.BlockSpec(memory_space=pl.ANY)
    inside = pl.BlockSpec(memory_space=pltpu.VMEM)
    summed, gains = pl.pallas_call(
        sum_kernel,
        out_shape=(
            jax.ShapeDtypeStruct((UNITS,) + wide, jnp.float32),
            jax.ShapeDtypeStruct(gains.shape, jnp.float32),
        ),
        in_specs=[everywhere] * 10 + [inside],
        out_specs=(inside, inside),
        scratch_shapes=[
            pltpu.VMEM((UNITS, 2, 2, 2) + wide, low),
            pltpu.VMEM((UNITS, 2, 2, 2) + wide, low),
            pltpu.VMEM((half, 2, 2) + wide, low),
            pltpu.VMEM((half, 2) + wide, low),
            pltpu.VMEM((half,) + wide, low),
            pltpu.VMEM((half,) + wide, low),
            pltpu.VMEM((half, 2, 2, 2) + thin, low),
            pltpu.VMEM((half, 2, 2) + thin, low),
            pltpu.VMEM((half, 2) + thin, low),
            pltpu.VMEM((half,) + thin, low),
            pltpu.VMEM((half,) + thin, low),
            pltpu.VMEM((6,) + gains.shape, jnp.float32),
            pltpu.VMEM((5,) + gains.shape, jnp.float32),
            pltpu.SemaphoreType.DMA((UNITS,)),
            pltpu.SemaphoreType.DMA((6, UNITS)),
            pltpu.SemaphoreType.DMA((6, UNITS)),
            pltpu.SemaphoreType.DMA((5,)),
            pltpu.SemaphoreType.DMA((5,)),
        ],
        compiler_params=pltpu.CompilerParams(
            collective_id=0, has_side_effects=True, vmem_limit_bytes=48 * 2**20
        ),
    )(*shaped, gains)
    expand = jnp.concatenate([summed[8 + k] for k in range(4)], axis=1)
    narrow = summed[12:].reshape(4 * PART, D)
    return tuple(summed[k] for k in range(8)) + (expand, narrow), gains


def body(
    members,
    groups,
    mel_frames,
    conv_first,
    conv_second,
    enc_projection,
    enc_output,
    enc_expand,
    enc_narrow,
    dec_input,
    lengths,
    self_query,
    self_key,
    self_value,
    self_output,
    cross_query,
    cross_key,
    cross_value,
    cross_output,
    mlp_expand,
    mlp_narrow,
    gain_self,
    gain_cross,
    gain_mlp,
    cotangent,
):
    arrived = lax.all_to_all(mel_frames, "tm", split_axis=2, concat_axis=0, tiled=True)
    mel_clips = jnp.transpose(arrived[:, 0], (1, 0, 2))
    encoded = encode(
        mel_clips, conv_first, conv_second, enc_projection, enc_output, enc_expand, enc_narrow
    )
    scale = HD ** (-0.5)
    inputs = dec_input[0].astype(jnp.float32)
    clip_lengths = lengths[0]
    places = jnp.arange(inputs.shape[1], dtype=jnp.int32)
    live_rows = places[None, :] < clip_lengths[:, None]
    h_self = scaled_norm(inputs, gain_self).astype(jnp.bfloat16)
    q_self = project(h_self, self_query).astype(jnp.bfloat16)
    k_self = project(h_self, self_key).astype(jnp.bfloat16)
    v_self = project(h_self, self_value).astype(jnp.bfloat16)
    allowed = (places[None, None, :] <= places[None, :, None]) & (
        places[None, None, :] < clip_lengths[:, None, None]
    )
    p_self = normalize(jnp.where(allowed[:, None], pair_products(q_self, k_self) * scale, -1e30))
    pb_self = p_self.astype(jnp.bfloat16)
    o_self = apply_probs(pb_self, v_self).astype(jnp.bfloat16)
    after_self = inputs + project(o_self, self_output)
    h_cross = scaled_norm(after_self, gain_cross).astype(jnp.bfloat16)
    q_cross = project(h_cross, cross_query).astype(jnp.bfloat16)
    k_cross = project(encoded, cross_key).astype(jnp.bfloat16)
    v_cross = project(encoded, cross_value).astype(jnp.bfloat16)
    p_cross = normalize(pair_products(q_cross, k_cross) * scale)
    pb_cross = p_cross.astype(jnp.bfloat16)
    o_cross = apply_probs(pb_cross, v_cross).astype(jnp.bfloat16)
    after_cross = after_self + project(o_cross, cross_output)
    h_mlp = scaled_norm(after_cross, gain_mlp).astype(jnp.bfloat16)
    hidden = project(h_mlp, mlp_expand)
    activated = gelu_exact(hidden).astype(jnp.bfloat16)
    after_mlp = after_cross + project(activated, mlp_narrow)
    dec_output = jnp.where(live_rows[..., None], after_mlp, 0.0).astype(jnp.bfloat16)
    grad_three = jnp.where(live_rows[..., None], cotangent[0].astype(jnp.float32), 0.0)
    branch_three = grad_three.astype(jnp.bfloat16)
    g_narrow = weight_grad(activated, branch_three)
    d_active = project_back(branch_three, mlp_narrow)
    gelu_value, gelu_back = jax.vjp(gelu_exact, hidden)
    d_hidden = gelu_back(d_active)[0].astype(jnp.bfloat16)
    g_expand = weight_grad(h_mlp, d_hidden)
    d_h_mlp = project_back(d_hidden, mlp_expand)
    norm_value, norm_back = jax.vjp(scaled_norm, after_cross, gain_mlp)
    d_part, g_gain_mlp = norm_back(d_h_mlp)
    grad_two = grad_three + d_part
    branch_two = grad_two.astype(jnp.bfloat16)
    g_cross_out = weight_grad(o_cross, branch_two)
    d_o_cross = project_back(branch_two, cross_output).astype(jnp.bfloat16)
    ds_cross = score_grads(p_cross, pair_products(d_o_cross, v_cross))
    d_q_cross = (apply_probs(ds_cross, k_cross) * scale).astype(jnp.bfloat16)
    d_k_cross = (key_grads(ds_cross, q_cross) * scale).astype(jnp.bfloat16)
    d_v_cross = key_grads(pb_cross, d_o_cross).astype(jnp.bfloat16)
    g_cross_query = weight_grad(h_cross, d_q_cross)
    g_cross_key = weight_grad(encoded, d_k_cross)
    g_cross_value = weight_grad(encoded, d_v_cross)
    enc_state_grad = project_back(d_k_cross, cross_key) + project_back(d_v_cross, cross_value)
    d_h_cross = project_back(d_q_cross, cross_query)
    norm_value, norm_back = jax.vjp(scaled_norm, after_self, gain_cross)
    d_part, g_gain_cross = norm_back(d_h_cross)
    grad_one = grad_two + d_part
    branch_one = grad_one.astype(jnp.bfloat16)
    g_self_out = weight_grad(o_self, branch_one)
    d_o_self = project_back(branch_one, self_output).astype(jnp.bfloat16)
    ds_self = score_grads(p_self, pair_products(d_o_self, v_self))
    d_q_self = (apply_probs(ds_self, k_self) * scale).astype(jnp.bfloat16)
    d_k_self = (key_grads(ds_self, q_self) * scale).astype(jnp.bfloat16)
    d_v_self = key_grads(pb_self, d_o_self).astype(jnp.bfloat16)
    g_self_query = weight_grad(h_self, d_q_self)
    g_self_key = weight_grad(h_self, d_k_self)
    g_self_value = weight_grad(h_self, d_v_self)
    d_h_self = (
        project_back(d_q_self, self_query)
        + project_back(d_k_self, self_key)
        + project_back(d_v_self, self_value)
    )
    norm_value, norm_back = jax.vjp(scaled_norm, inputs, gain_self)
    d_part, g_gain_self = norm_back(d_h_self)
    dec_input_grad = grad_one + d_part
    matrices = [
        g_self_query, g_self_key, g_self_value, g_self_out,
        g_cross_query, g_cross_key, g_cross_value, g_cross_out,
        g_expand, g_narrow,
    ]
    matrices = [matrix.astype(jnp.bfloat16) for matrix in matrices]
    gains = jnp.concatenate(
        [g_gain_self[None], g_gain_cross[None], g_gain_mlp[None], jnp.zeros((5, D), jnp.float32)]
    )
    totals, gains = sum_gradients(matrices, gains, members, groups)
    part = D // members
    gains = lax.dynamic_slice_in_dim(gains, lax.axis_index("tm") * part, part, 1)
    totals = totals + (gains[0], gains[1], gains[2])
    return (
        encoded[None],
        dec_output[None],
        dec_input_grad[None],
        enc_state_grad[None],
        totals[0],
        totals[1],
        totals[2],
        totals[3],
        totals[4],
        totals[5],
        totals[6],
        totals[7],
        totals[8],
        totals[9],
        totals[10],
        totals[11],
        totals[12],
    )


def solution(mesh):
    placed = (
        P("tm", "clip", None, None),
        P(),
        P(),
        P(),
        P(),
        P(),
        P(),
        P("clip", "tm", None, None),
        P("clip", "tm"),
        P(),
        P(),
        P(),
        P(),
        P(),
        P(),
        P(),
        P(),
        P(),
        P(),
        P(),
        P(),
        P(),
        P("clip", "tm", None, None),
    )
    return jax.shard_map(
        functools.partial(body, mesh.shape["tm"], mesh.shape["clip"]),
        mesh=mesh,
        in_specs=placed,
        out_specs=(
            P("clip", "tm", None, None),
            P("clip", "tm", None, None),
            P("clip", "tm", None, None),
            P("clip", "tm", None, None),
            P("tm", None),
            P("tm", None),
            P("tm", None),
            P("tm", None),
            P("tm", None),
            P("tm", None),
            P("tm", None),
            P("tm", None),
            P("tm", None),
            P("tm", None),
            P("tm"),
            P("tm"),
            P("tm"),
        ),
        check_vma=False,
    )
```

```python
import functools
import math

import jax
import jax.numpy as jnp
import numpy as np
from jax import lax
from jax.experimental import pallas as pl
from jax.experimental.pallas import tpu as pltpu
from jax.sharding import PartitionSpec as P

D = 768
HEADS = 12
HD = 64
PAIRS = HEADS // 2
LANES = 2 * HD
SCALE = HD ** (-0.5)
LOW = jnp.bfloat16
WIDE = jnp.float32
EVERYWHERE = pl.BlockSpec(memory_space=pl.ANY)
INSIDE = pl.BlockSpec(memory_space=pltpu.VMEM)


def shape_of(shape, kind=LOW):
    return jax.ShapeDtypeStruct(shape, kind)


def parameters(megabytes=58):
    return pltpu.CompilerParams(vmem_limit_bytes=megabytes * 2**20)


def center(values):
    shifted = values - jnp.mean(values, axis=-1, keepdims=True)
    spread = jnp.mean(shifted * shifted, axis=-1, keepdims=True)
    root = lax.rsqrt(spread + 1e-05)
    return shifted * root, root


def center_back(gradient, values, gain):
    normed, root = center(values)
    inner = gradient * gain
    first = jnp.mean(inner, axis=-1, keepdims=True)
    second = jnp.mean(inner * normed, axis=-1, keepdims=True)
    gain_part = jnp.sum(gradient * normed, axis=0, keepdims=True)
    return root * (inner - first - normed * second), gain_part


def gelu(values):
    return values * (0.5 + 0.5 * lax.erf(values * 2**-0.5))


def gelu_both(values):
    area = 0.5 + 0.5 * lax.erf(values * 2**-0.5)
    slope = area + values * ((2 * math.pi) ** -0.5 * jnp.exp(-0.5 * values * values))
    return values * area, slope


def dot(left, right):
    return jnp.dot(left, right, preferred_element_type=WIDE)


def dot_back(left, right):
    return lax.dot_general(left, right, (((1,), (1,)), ((), ())), preferred_element_type=WIDE)


def dot_rows(left, right):
    return lax.dot_general(left, right, (((0,), (0,)), ((), ())), preferred_element_type=WIDE)


def strips(total, width):
    return [(at, min(width, total - at)) for at in range(0, total, width)]


class Fetch:
    def __init__(self, sources, targets, semaphores):
        self.copies = [
            pltpu.make_async_copy(source, target, semaphores.at[place])
            for place, (source, target) in enumerate(zip(sources, targets))
        ]
        for copy in self.copies:
            copy.start()

    def wait(self, place):
        self.copies[place].wait()


def pair_lanes(pair):
    return pl.ds(pl.multiple_of(pair * LANES, LANES), LANES)


def head_rows(pair, side):
    return pl.ds(pl.multiple_of(pair * LANES + side * HD, HD), HD)


def attend(q_ref, k_ref, vt_ref, bias_ref, ot_ref, inverse_ref, raised_ref):
    @pl.loop(0, PAIRS)
    def _(pair):
        queries, keys = q_ref[:, pair_lanes(pair)], k_ref[:, pair_lanes(pair)]
        for side in range(2):
            cut = slice(side * HD, (side + 1) * HD)
            scores = dot_back(keys[:, cut], queries[:, cut])
            if bias_ref is not None:
                scores = scores + bias_ref[...]
            raised = jnp.exp(scores - jnp.max(scores, axis=0, keepdims=True))
            inverse = 1.0 / jnp.sum(raised, axis=0, keepdims=True)
            raised = raised.astype(LOW)
            mixed = dot(vt_ref[head_rows(pair, side), :], raised)
            ot_ref[head_rows(pair, side), :] = (mixed * inverse).astype(LOW)
            if raised_ref is not None:
                raised_ref[2 * pair + side] = raised
                total = jnp.sum(raised.astype(WIDE), axis=0, keepdims=True)
                rank = lax.broadcasted_iota(jnp.int32, inverse_ref.shape[1:], 0)
                inverse_ref[2 * pair + side] = jnp.where(rank == 0, inverse, 1.0 / total)


def attend_back(
    q_ref, kt_ref, v_ref, raised_ref, inverse_ref, dot_ref, dov_ref, dqt_ref, dk_ref, dv_ref
):
    @pl.loop(0, PAIRS)
    def _(pair):
        lanes = pair_lanes(pair)
        queries, values, grads = q_ref[:, lanes], v_ref[:, lanes], dov_ref[:, lanes]
        key_sides, value_sides = [], []
        for side in range(2):
            rows = head_rows(pair, side)
            cut = slice(side * HD, (side + 1) * HD)
            back = dot_ref[rows, :]
            raised = raised_ref[2 * pair + side]
            weights = raised.astype(WIDE)
            weighted = weights * dot(values[:, cut], back)
            delta = jnp.sum(weighted, axis=0, keepdims=True) * inverse_ref[2 * pair + side, 1:2, :]
            score_grad = (weighted - weights * delta).astype(LOW)
            dqt_ref[rows, :] = (dot(kt_ref[rows, :], score_grad) * SCALE).astype(LOW)
            key_sides.append(dot(score_grad, queries[:, cut]))
            value_sides.append(dot(raised, grads[:, cut]))
        dk_ref[:, lanes] = jnp.concatenate(key_sides, axis=1).astype(LOW)
        dv_ref[:, lanes] = jnp.concatenate(value_sides, axis=1).astype(LOW)


def encoder_kernel(
    mel_ref, position_ref, first_h, second_h, joint_h, output_h, expand_h, narrow_h,
    out_ref, out_t_ref,
    first_w, second_w, joint_w, output_w, expand_w, narrow_w,
    even, odd, state, hidden, q, k, vt, mixed_t, semaphores,
):
    length = out_ref.shape[0]
    fetch = Fetch(
        (first_h, second_h, joint_h, output_h, expand_h, narrow_h),
        (first_w, second_w, joint_w, output_w, expand_w, narrow_w),
        semaphores,
    )
    taps = [mel_ref[pl.ds(offset, length, stride=2), :].astype(LOW) for offset in range(4)]
    fetch.wait(0)
    for at, width in strips(D, 256):
        cols = pl.ds(at, width)
        for start, target in ((0, even), (1, odd)):
            total = sum(dot(taps[start + o], first_w[o, :, cols]) for o in range(3))
            target[:, cols] = gelu(total).astype(LOW)
    fetch.wait(1)
    ranks = lax.broadcasted_iota(jnp.int32, (length, 256), 0)
    for at, width in strips(D, 256):
        cols = pl.ds(at, width)
        before = pltpu.roll(dot(odd[...], second_w[0, :, cols]), 1, 0)
        total = dot(even[...], second_w[1, :, cols]) + dot(odd[...], second_w[2, :, cols])
        total = total + jnp.where(ranks == 0, 0.0, before)
        state[:, cols] = gelu(total) + position_ref[:, cols]
    hidden[...] = center(state[...])[0].astype(LOW)
    fetch.wait(2)
    for at, width in strips(D, 256):
        cols = pl.ds(at, width)
        q[:, cols] = (dot(hidden[...], joint_w[:, cols]).astype(LOW) * SCALE).astype(LOW)
        k[:, cols] = dot(hidden[...], joint_w[:, pl.ds(D + at, width)]).astype(LOW)
        vt[cols, :] = dot(hidden[...], joint_w[:, pl.ds(2 * D + at, width)]).astype(LOW).T
    attend(q, k, vt, None, mixed_t, None, None)
    fetch.wait(3)
    mixed = mixed_t[...].T
    for at, width in strips(D, 256):
        cols = pl.ds(at, width)
        state[:, cols] += dot(mixed, output_w[:, cols])
    hidden[...] = center(state[...])[0].astype(LOW)
    fetch.wait(4)
    fetch.wait(5)

    @pl.loop(0, expand_w.shape[1] // 512)
    def _(strip):
        cols = pl.ds(pl.multiple_of(strip * 512, 512), 512)
        widened = gelu(dot(hidden[...], expand_w[:, cols])).astype(LOW)
        state[...] += dot(widened, narrow_w[cols, :])

    encoded = center(state[...])[0].astype(LOW)
    out_ref[...] = encoded
    out_t_ref[...] = encoded.T


def encode(mel_clips, conv_first, conv_second, enc_projection, enc_output, enc_expand, enc_narrow):
    frames = mel_clips.shape[0]
    length = frames // 2
    mel = jnp.pad(mel_clips.astype(WIDE), ((1, 7), (0, 0)))
    weights = (conv_first, conv_second, enc_projection, enc_output, enc_expand, enc_narrow)
    return pl.pallas_call(
        encoder_kernel,
        out_shape=(shape_of((length, D)), shape_of((D, length))),
        in_specs=[INSIDE] * 2 + [EVERYWHERE] * 6,
        out_specs=(INSIDE, INSIDE),
        scratch_shapes=[pltpu.VMEM(weight.shape, LOW) for weight in weights]
        + [
            pltpu.VMEM((length, D), LOW),
            pltpu.VMEM((length, D), LOW),
            pltpu.VMEM((length, D), WIDE),
            pltpu.VMEM((length, D), LOW),
            pltpu.VMEM((length, D), LOW),
            pltpu.VMEM((length, D), LOW),
            pltpu.VMEM((D, length), LOW),
            pltpu.VMEM((D, length), LOW),
            pltpu.SemaphoreType.DMA((6,)),
        ],
        compiler_params=parameters(),
    )(mel, sinusoids(length, D), *weights)


def sinusoids(length, features):
    halfway = features // 2
    inverse = np.exp(-math.log(10000.0) / (halfway - 1) * np.arange(halfway)).astype(np.float32)
    angles = np.arange(length, dtype=np.float32)[:, None] * inverse[None, :]
    angles = angles.astype(np.float64)
    return jnp.asarray(np.concatenate([np.sin(angles), np.cos(angles)], axis=1).astype(np.float32))


def self_kernel(
    length_ref, x_ref, gain_ref, query_h, key_h, value_h, output_h,
    x1_ref, ht_ref, q_ref, kt_ref, v_ref, raised_ref, inverse_ref, ot_ref,
    query_w, key_w, value_w, output_w, hidden, k, vt, bias, semaphores,
):
    fetch = Fetch(
        (query_h, key_h, value_h, output_h), (query_w, key_w, value_w, output_w), semaphores
    )
    rows = x_ref.shape[0]
    hidden[...] = (center(x_ref[...].astype(WIDE))[0] * gain_ref[...]).astype(LOW)
    keys = lax.broadcasted_iota(jnp.int32, (rows, rows), 0)
    queries = lax.broadcasted_iota(jnp.int32, (rows, rows), 1)
    allowed = (keys <= queries) & (keys < length_ref[0])
    bias[...] = jnp.where(allowed, 0.0, -1e30)
    fetch.wait(0)
    fetch.wait(1)
    fetch.wait(2)
    for at, width in strips(D, 256):
        cols = pl.ds(at, width)
        q_ref[:, cols] = (dot(hidden[...], query_w[:, cols]).astype(LOW) * SCALE).astype(LOW)
        part = dot(hidden[...], key_w[:, cols]).astype(LOW)
        k[:, cols] = part
        kt_ref[cols, :] = part.T
        part = dot(hidden[...], value_w[:, cols]).astype(LOW)
        v_ref[:, cols] = part
        vt[cols, :] = part.T
    ht_ref[...] = hidden[...].T
    attend(q_ref, k, vt, bias, ot_ref, inverse_ref, raised_ref)
    fetch.wait(3)
    mixed = ot_ref[...].T
    for at, width in strips(D, 256):
        cols = pl.ds(at, width)
        x1_ref[:, cols] = x_ref[:, cols].astype(WIDE) + dot(mixed, output_w[:, cols])


def self_forward(lengths, inputs, gain, weights):
    rows = inputs.shape[0]
    plain, turned = (rows, D), (D, rows)
    return pl.pallas_call(
        self_kernel,
        out_shape=(
            shape_of(plain, WIDE), shape_of(turned), shape_of(plain), shape_of(turned),
            shape_of(plain), shape_of((HEADS, rows, rows)), shape_of((HEADS, 8, rows), WIDE),
            shape_of(turned),
        ),
        in_specs=[pl.BlockSpec(memory_space=pltpu.SMEM), INSIDE, INSIDE] + [EVERYWHERE] * 4,
        out_specs=(INSIDE,) * 8,
        scratch_shapes=[pltpu.VMEM((D, D), LOW)] * 4
        + [
            pltpu.VMEM(plain, LOW),
            pltpu.VMEM(plain, LOW),
            pltpu.VMEM(turned, LOW),
            pltpu.VMEM((rows, rows), WIDE),
            pltpu.SemaphoreType.DMA((4,)),
        ],
        compiler_params=parameters(),
    )(lengths, inputs, gain, *weights)


def cross_kernel(
    length_ref, x1_ref, encoded_ref, cotangent_ref, gain_cross_ref, gain_mlp_ref,
    query_h, key_h, value_h, output_h, expand_h, narrow_h,
    out_ref, g2_ref, gain_grad_ref, ht_ref, q_ref, kt_ref, v_ref, raised_ref, inverse_ref, ot_ref,
    expand_grad_ref, narrow_grad_ref,
    query_w, key_w, value_w, output_w, expand_w, narrow_w, hidden, hidden_t, k, vt, x2, x3, b3,
    back, semaphores,
):
    fetch = Fetch(
        (query_h, key_h, value_h, output_h, expand_h, narrow_h),
        (query_w, key_w, value_w, output_w, expand_w, narrow_w),
        semaphores,
    )
    rows = x1_ref.shape[0]
    hidden[...] = (center(x1_ref[...])[0] * gain_cross_ref[...]).astype(LOW)
    ht_ref[...] = hidden[...].T
    fetch.wait(0)
    fetch.wait(1)
    fetch.wait(2)
    for at, width in strips(D, 256):
        cols = pl.ds(at, width)
        q_ref[:, cols] = (dot(hidden[...], query_w[:, cols]).astype(LOW) * SCALE).astype(LOW)
        part = dot(encoded_ref[...], key_w[:, cols]).astype(LOW)
        k[:, cols] = part
        kt_ref[cols, :] = part.T
        part = dot(encoded_ref[...], value_w[:, cols]).astype(LOW)
        v_ref[:, cols] = part
        vt[cols, :] = part.T
    attend(q_ref, k, vt, None, ot_ref, inverse_ref, raised_ref)
    fetch.wait(3)
    mixed = ot_ref[...].T
    for at, width in strips(D, 256):
        cols = pl.ds(at, width)
        x2[:, cols] = x1_ref[:, cols] + dot(mixed, output_w[:, cols])
    hidden[...] = (center(x2[...])[0] * gain_mlp_ref[...]).astype(LOW)
    hidden_t[...] = hidden[...].T
    x3[...] = x2[...]
    live = lax.broadcasted_iota(jnp.int32, (rows, D), 0) < length_ref[0]
    b3[...] = jnp.where(live, cotangent_ref[...].astype(WIDE), 0.0).astype(LOW)
    back[...] = jnp.zeros_like(back)
    fetch.wait(4)
    fetch.wait(5)

    @pl.loop(0, expand_w.shape[1] // 512)
    def _(strip):
        cols = pl.ds(pl.multiple_of(strip * 512, 512), 512)
        active, slope = gelu_both(dot(hidden[...], expand_w[:, cols]))
        active = active.astype(LOW)
        grad = (slope * dot_back(b3[...], narrow_w[cols, :])).astype(LOW)
        x3[...] += dot(active, narrow_w[cols, :])
        narrow_grad_ref[cols, :] = dot_rows(active, b3[...]).astype(LOW)
        expand_grad_ref[:, cols] = dot(hidden_t[...], grad).astype(LOW)
        back[...] += dot_back(grad, expand_w[:, cols])

    out_ref[...] = jnp.where(live, x3[...], 0.0).astype(LOW)
    part, gain_part = center_back(back[...], x2[...], gain_mlp_ref[...])
    gain_grad_ref[...] = gain_part
    g2_ref[...] = b3[...].astype(WIDE) + part


def cross_forward(lengths, x1, encoded, cotangent, gain_cross, gain_mlp, weights):
    rows, frames = x1.shape[0], encoded.shape[0]
    wide = weights[4].shape[1]
    plain, turned = (rows, D), (D, rows)
    return pl.pallas_call(
        cross_kernel,
        out_shape=(
            shape_of(plain), shape_of(plain, WIDE), shape_of((1, D), WIDE), shape_of(turned),
            shape_of(plain), shape_of((D, frames)), shape_of((frames, D)),
            shape_of((HEADS, frames, rows)), shape_of((HEADS, 8, rows), WIDE), shape_of(turned),
            shape_of((D, wide)), shape_of((wide, D)),
        ),
        in_specs=[pl.BlockSpec(memory_space=pltpu.SMEM)] + [INSIDE] * 5 + [EVERYWHERE] * 6,
        out_specs=(INSIDE,) * 12,
        scratch_shapes=[pltpu.VMEM(weight.shape, LOW) for weight in weights]
        + [
            pltpu.VMEM(plain, LOW),
            pltpu.VMEM(turned, LOW),
            pltpu.VMEM((frames, D), LOW),
            pltpu.VMEM((D, frames), LOW),
            pltpu.VMEM(plain, WIDE),
            pltpu.VMEM(plain, WIDE),
            pltpu.VMEM(plain, LOW),
            pltpu.VMEM(plain, WIDE),
            pltpu.SemaphoreType.DMA((6,)),
        ],
        compiler_params=parameters(),
    )(lengths, x1, encoded, cotangent, gain_cross, gain_mlp, *weights)


def spread_grads(out_grad, output_w, inverse_ref, dov, dot_t):
    for at, width in strips(D, 256):
        part = dot_back(out_grad, output_w[at : at + width, :]).astype(LOW).T
        sides = [
            part[head * HD : (head + 1) * HD, :].astype(WIDE) * inverse_ref[at // HD + head, 0:1, :]
            for head in range(width // HD)
        ]
        part = jnp.concatenate(sides, axis=0).astype(LOW)
        dot_t[at : at + width, :] = part
        dov[:, at : at + width] = part.T


def cross_back_kernel(
    g2_ref, x1_ref, gain_ref, ht_ref, q_ref, kt_ref, v_ref, raised_ref, inverse_ref, ot_ref,
    encoded_t_ref, query_h, key_h, value_h, output_h,
    g1_ref, gain_grad_ref, state_grad_ref, query_g, key_g, value_g, output_g,
    query_w, key_w, value_w, output_w, dov, dot_t, dqt, dk, dv, semaphores,
):
    fetch = Fetch(
        (output_h, query_h, key_h, value_h), (output_w, query_w, key_w, value_w), semaphores
    )
    b2 = g2_ref[...].astype(LOW)
    fetch.wait(0)
    spread_grads(b2, output_w, inverse_ref, dov, dot_t)
    for at, width in strips(D, 256):
        output_g[:, at : at + width] = dot(ot_ref[...], b2[:, at : at + width]).astype(LOW)
    attend_back(q_ref, kt_ref, v_ref, raised_ref, inverse_ref, dot_t, dov, dqt, dk, dv)
    dq = dqt[...].T
    for place in range(1, 4):
        fetch.wait(place)
    for at, width in strips(D, 256):
        cols = slice(at, at + width)
        query_g[:, cols] = dot(ht_ref[...], dq[:, cols]).astype(LOW)
        key_g[:, cols] = dot(encoded_t_ref[...], dk[:, cols]).astype(LOW)
        value_g[:, cols] = dot(encoded_t_ref[...], dv[:, cols]).astype(LOW)
        state_grad_ref[:, cols] = dot_back(dk[...], key_w[cols, :]) + dot_back(
            dv[...], value_w[cols, :]
        )
    part, gain_part = center_back(dot_back(dq, query_w[...]), x1_ref[...], gain_ref[...])
    gain_grad_ref[...] = gain_part
    g1_ref[...] = g2_ref[...] + part


def cross_backward(operands, weights):
    rows, frames = operands[0].shape[0], operands[10].shape[1]
    plain, turned, square = (rows, D), (D, rows), shape_of((D, D))
    return pl.pallas_call(
        cross_back_kernel,
        out_shape=(
            shape_of(plain, WIDE), shape_of((1, D), WIDE), shape_of((frames, D), WIDE),
            square, square, square, square,
        ),
        in_specs=[INSIDE] * 11 + [EVERYWHERE] * 4,
        out_specs=(INSIDE,) * 7,
        scratch_shapes=[pltpu.VMEM((D, D), LOW)] * 4
        + [
            pltpu.VMEM(plain, LOW),
            pltpu.VMEM(turned, LOW),
            pltpu.VMEM(turned, LOW),
            pltpu.VMEM((frames, D), LOW),
            pltpu.VMEM((frames, D), LOW),
            pltpu.SemaphoreType.DMA((4,)),
        ],
        compiler_params=parameters(),
    )(*operands, *weights)


def self_back_kernel(
    g1_ref, x_ref, gain_ref, ht_ref, q_ref, kt_ref, v_ref, raised_ref, inverse_ref, ot_ref,
    query_h, key_h, value_h, output_h,
    input_grad_ref, gain_grad_ref, query_g, key_g, value_g, output_g,
    query_w, key_w, value_w, output_w, dov, dot_t, dqt, dk, dv, semaphores,
):
    fetch = Fetch(
        (output_h, query_h, key_h, value_h), (output_w, query_w, key_w, value_w), semaphores
    )
    b1 = g1_ref[...].astype(LOW)
    fetch.wait(0)
    spread_grads(b1, output_w, inverse_ref, dov, dot_t)
    for at, width in strips(D, 256):
        output_g[:, at : at + width] = dot(ot_ref[...], b1[:, at : at + width]).astype(LOW)
    attend_back(q_ref, kt_ref, v_ref, raised_ref, inverse_ref, dot_t, dov, dqt, dk, dv)
    dq = dqt[...].T
    for place in range(1, 4):
        fetch.wait(place)
    for at, width in strips(D, 256):
        cols = slice(at, at + width)
        query_g[:, cols] = dot(ht_ref[...], dq[:, cols]).astype(LOW)
        key_g[:, cols] = dot(ht_ref[...], dk[:, cols]).astype(LOW)
        value_g[:, cols] = dot(ht_ref[...], dv[:, cols]).astype(LOW)
        input_grad_ref[:, cols] = (
            dot_back(dq, query_w[cols, :])
            + dot_back(dk[...], key_w[cols, :])
            + dot_back(dv[...], value_w[cols, :])
        )
    part, gain_part = center_back(
        input_grad_ref[...], x_ref[...].astype(WIDE), gain_ref[...]
    )
    gain_grad_ref[...] = gain_part
    input_grad_ref[...] = g1_ref[...] + part


def self_backward(operands, weights):
    rows = operands[0].shape[0]
    plain, turned, square = (rows, D), (D, rows), shape_of((D, D))
    return pl.pallas_call(
        self_back_kernel,
        out_shape=(shape_of(plain, WIDE), shape_of((1, D), WIDE), square, square, square, square),
        in_specs=[INSIDE] * 10 + [EVERYWHERE] * 4,
        out_specs=(INSIDE,) * 6,
        scratch_shapes=[pltpu.VMEM((D, D), LOW)] * 4
        + [
            pltpu.VMEM(plain, LOW),
            pltpu.VMEM(turned, LOW),
            pltpu.VMEM(turned, LOW),
            pltpu.VMEM(plain, LOW),
            pltpu.VMEM(plain, LOW),
            pltpu.SemaphoreType.DMA((4,)),
        ],
        compiler_params=parameters(),
    )(*operands, *weights)


def trade(values, axis, size, bit):
    return lax.ppermute(values, axis, [(i, i ^ bit) for i in range(size)])


def add_rounded(left, right):
    return (left.astype(jnp.float32) + right.astype(jnp.float32)).astype(jnp.bfloat16)


def halve(values, dim, axis, size, bit):
    mine = (lax.axis_index(axis) // bit) % 2
    kept = lax.dynamic_index_in_dim(values, mine, dim, keepdims=False)
    sent = lax.dynamic_index_in_dim(values, 1 - mine, dim, keepdims=False)
    return add_rounded(kept, trade(sent, axis, size, bit))


def bits_of(size):
    return [1 << k for k in range(size.bit_length() - 1)]


def members_first(values, members, groups):
    for bit in bits_of(members):
        values = halve(values, len(values.shape) - 3, "tm", members, bit)
    for bit in bits_of(groups):
        values = add_rounded(values, trade(values, "clip", groups, bit))
    return values.astype(jnp.float32)


def groups_first(values, members, groups):
    values = halve(values, len(values.shape) - 3, "tm", members, 1)
    lead = values.shape[:-2]
    rows, columns = values.shape[-2:]
    for bit in bits_of(groups):
        values = values.reshape(lead + (2, values.shape[-2] // 2, columns))
        values = halve(values, len(lead), "clip", groups, bit)
    for bit in bits_of(members)[1:]:
        values = halve(values, len(values.shape) - 3, "tm", members, bit)
    for bit in bits_of(groups)[::-1]:
        mine = (lax.axis_index("clip") // bit) % 2
        other = trade(values, "clip", groups, bit)
        values = jnp.where(
            mine == 0, jnp.concatenate([values, other]), jnp.concatenate([other, values])
        )
    return values.astype(jnp.float32)


def sum_plain(matrices, gains, members, groups):
    split = (2,) * (members.bit_length() - 1)
    totals = []
    for place, matrix in enumerate(matrices):
        blocks = matrix.reshape(split + (matrix.shape[0] // members, matrix.shape[1]))
        totals.append((members_first, groups_first)[place % 2](blocks, members, groups))
    return tuple(totals), lax.psum(gains, ("tm", "clip"))


MESH = pl.DeviceIdType.MESH
PART = 48
UNITS = 16
UNIT_ORDER = (12, 8, 13, 9, 14, 10, 15, 11, 7, 4, 5, 6, 3, 0, 1, 2)


def add_halves(left, right):
    return (left.astype(jnp.float32) + right.astype(jnp.float32)).astype(jnp.bfloat16)


def sum_kernel(*refs):
    matrices, gain_in = refs[:10], refs[10]
    out, gain_out = refs[11:13]
    (own, got0, a1, a2, a3, a4, b1, b2, b3, b4, b5, gain_sum, gain_got) = refs[13:26]
    own_sem, send_sem, recv_sem, gain_send, gain_recv = refs[26:]
    tm, clip = lax.axis_index("tm"), lax.axis_index("clip")
    core, along_x, low_z, high_z = tm % 2, (tm // 2) % 2, (tm // 4) % 2, tm // 8
    core_peer, x_peer, low_peer, high_peer = (
        (tm + 1 - 2 * core, clip),
        (tm + 2 - 4 * along_x, clip),
        (tm + 4 - 8 * low_z, clip),
        (tm + 8 - 16 * high_z, clip),
    )
    clip_peer = (tm, 1 - clip)
    peers = (core_peer, x_peer, low_peer, high_peer, clip_peer)
    barrier = pltpu.get_barrier_semaphore()
    for peer in peers:
        pl.semaphore_signal(barrier, inc=1, device_id=peer, device_id_type=MESH)
    pl.semaphore_wait(barrier, len(peers))

    def source(unit, side):
        if unit < 8:
            return matrices[unit].at[:, :, :, side]
        if unit < 12:
            return matrices[8].at[:, :, :, side, :, pl.ds((unit - 8) * D, D)]
        return matrices[9].at[:, :, :, side, unit - 12]

    started = []

    def send(src, dst, stage, unit, peer):
        copy = pltpu.make_async_remote_copy(
            src_ref=src,
            dst_ref=dst,
            send_sem=send_sem.at[stage, unit],
            recv_sem=recv_sem.at[stage, unit],
            device_id=peer,
            device_id_type=MESH,
        )
        copy.start()
        started.append(copy)
        return copy

    copies = {}
    own_columns = pl.ds(pl.multiple_of(clip * (D // 2), D // 2), D // 2)
    other_columns = pl.ds(pl.multiple_of((1 - clip) * (D // 2), D // 2), D // 2)

    def begin(place):
        unit = UNIT_ORDER[place]
        keep = pltpu.make_async_copy(source(unit, core), own.at[place], own_sem.at[place])
        keep.start()
        copies[0, place] = send(source(unit, 1 - core), got0.at[place], 0, place, core_peer)
        copies["own", place] = keep

    def step(stage, place):
        pair = place // 2
        if place % 2 == 0 and stage > 5 or stage > 6:
            return
        copies[stage - 1, place].wait_recv()
        if stage == 1:
            copies["own", place].wait()

            @pl.loop(0, 8)
            def _(block):
                i, j, k = block // 4, (block // 2) % 2, block % 2
                got0[place, i, j, k] = add_halves(got0[place, i, j, k], own[place, i, j, k])

        if place % 2 == 0:
            if stage == 1:
                copies[1, place] = send(
                    got0.at[place, :, :, 1 - along_x], a1.at[pair], 1, place, x_peer
                )
            elif stage == 2:

                @pl.loop(0, 4)
                def _(block):
                    i, j = block // 2, block % 2
                    a1[pair, i, j] = add_halves(a1[pair, i, j], got0[place, i, j, along_x])

                copies[2, place] = send(a1.at[pair, :, 1 - low_z], a2.at[pair], 2, place, low_peer)
            elif stage == 3:

                @pl.loop(0, 2)
                def _(i):
                    a2[pair, i] = add_halves(a2[pair, i], a1[pair, i, low_z])

                copies[3, place] = send(a2.at[pair, 1 - high_z], a3.at[pair], 3, place, high_peer)
            elif stage == 4:
                a3[pair] = add_halves(a3[pair], a2[pair, high_z])
                copies[4, place] = send(a3.at[pair], a4.at[pair], 4, place, clip_peer)
            elif stage == 5:
                out[UNIT_ORDER[place]] = a3[pair].astype(jnp.float32) + a4[pair].astype(jnp.float32)
            return
        if stage == 1:
            copies[1, place] = send(
                got0.at[place, :, :, :, :, other_columns], b1.at[pair], 1, place, clip_peer
            )
        elif stage == 2:

            @pl.loop(0, 8)
            def _(block):
                i, j, k = block // 4, (block // 2) % 2, block % 2
                b1[pair, i, j, k] = add_halves(
                    b1[pair, i, j, k], got0[place, i, j, k, :, own_columns]
                )

            copies[2, place] = send(b1.at[pair, :, :, 1 - along_x], b2.at[pair], 2, place, x_peer)
        elif stage == 3:

            @pl.loop(0, 4)
            def _(block):
                i, j = block // 2, block % 2
                b2[pair, i, j] = add_halves(b2[pair, i, j], b1[pair, i, j, along_x])

            copies[3, place] = send(b2.at[pair, :, 1 - low_z], b3.at[pair], 3, place, low_peer)
        elif stage == 4:

            @pl.loop(0, 2)
            def _(i):
                b3[pair, i] = add_halves(b3[pair, i], b2[pair, i, low_z])

            copies[4, place] = send(b3.at[pair, 1 - high_z], b4.at[pair], 4, place, high_peer)
        elif stage == 5:
            b4[pair] = add_halves(b4[pair], b3[pair, high_z])
            copies[5, place] = send(b4.at[pair], b5.at[pair], 5, place, clip_peer)
        elif stage == 6:
            out[UNIT_ORDER[place], :, own_columns] = b4[pair].astype(jnp.float32)
            out[UNIT_ORDER[place], :, other_columns] = b5[pair].astype(jnp.float32)

    gain_copies = {}

    def gain_step(number):
        if number == 0:
            gain_sum[0] = gain_in[...]
        else:
            gain_copies[number - 1].wait_recv()
            gain_sum[number] = gain_sum[number - 1] + gain_got[number - 1]
        if number == len(peers):
            gain_out[...] = gain_sum[number]
            return
        copy = pltpu.make_async_remote_copy(
            src_ref=gain_sum.at[number],
            dst_ref=gain_got.at[number],
            send_sem=gain_send.at[number],
            recv_sem=gain_recv.at[number],
            device_id=peers[number],
            device_id_type=MESH,
        )
        copy.start()
        started.append(copy)
        gain_copies[number] = copy

    pairs = UNITS // 2
    ahead = 2
    for place in range(UNITS):
        begin(place)
    for tick in range(-ahead, pairs + 5):
        if 0 <= tick <= len(peers):
            gain_step(tick)
        for stage in range(1, 7):
            pair = tick + ahead if stage == 1 else tick + 2 - stage
            if 0 <= pair < pairs:
                step(stage, 2 * pair + 1)
                step(stage, 2 * pair)
    for copy in started:
        copy.wait_send()


def sum_gradients(matrices, gains, members, groups):
    if (members, groups) != (16, 2):
        return sum_plain(matrices, gains, members, groups)
    shaped = [
        matrix.reshape((2, 2, 2, 2, PART, matrix.shape[1])) for matrix in matrices[:9]
    ] + [matrices[9].reshape((2, 2, 2, 2, 4, PART, D))]
    low, half = jnp.bfloat16, UNITS // 2
    wide, thin = (PART, D), (PART, D // 2)
    everywhere = pl.BlockSpec(memory_space=pl.ANY)
    inside = pl.BlockSpec(memory_space=pltpu.VMEM)
    summed, gains = pl.pallas_call(
        sum_kernel,
        out_shape=(
            jax.ShapeDtypeStruct((UNITS,) + wide, jnp.float32),
            jax.ShapeDtypeStruct(gains.shape, jnp.float32),
        ),
        in_specs=[everywhere] * 10 + [inside],
        out_specs=(inside, inside),
        scratch_shapes=[
            pltpu.VMEM((UNITS, 2, 2, 2) + wide, low),
            pltpu.VMEM((UNITS, 2, 2, 2) + wide, low),
            pltpu.VMEM((half, 2, 2) + wide, low),
            pltpu.VMEM((half, 2) + wide, low),
            pltpu.VMEM((half,) + wide, low),
            pltpu.VMEM((half,) + wide, low),
            pltpu.VMEM((half, 2, 2, 2) + thin, low),
            pltpu.VMEM((half, 2, 2) + thin, low),
            pltpu.VMEM((half, 2) + thin, low),
            pltpu.VMEM((half,) + thin, low),
            pltpu.VMEM((half,) + thin, low),
            pltpu.VMEM((6,) + gains.shape, jnp.float32),
            pltpu.VMEM((5,) + gains.shape, jnp.float32),
            pltpu.SemaphoreType.DMA((UNITS,)),
            pltpu.SemaphoreType.DMA((6, UNITS)),
            pltpu.SemaphoreType.DMA((6, UNITS)),
            pltpu.SemaphoreType.DMA((5,)),
            pltpu.SemaphoreType.DMA((5,)),
        ],
        compiler_params=pltpu.CompilerParams(
            collective_id=0, has_side_effects=True, vmem_limit_bytes=48 * 2**20
        ),
    )(*shaped, gains)
    expand = jnp.concatenate([summed[8 + k] for k in range(4)], axis=1)
    narrow = summed[12:].reshape(4 * PART, D)
    return tuple(summed[k] for k in range(8)) + (expand, narrow), gains


def body(
    members,
    groups,
    mel_frames,
    conv_first,
    conv_second,
    enc_projection,
    enc_output,
    enc_expand,
    enc_narrow,
    dec_input,
    lengths,
    self_query,
    self_key,
    self_value,
    self_output,
    cross_query,
    cross_key,
    cross_value,
    cross_output,
    mlp_expand,
    mlp_narrow,
    gain_self,
    gain_cross,
    gain_mlp,
    cotangent,
):
    arrived = lax.all_to_all(mel_frames, "tm", split_axis=2, concat_axis=0, tiled=True)
    inputs, length = dec_input[0, 0], lengths[0]
    gain_self, gain_cross, gain_mlp = gain_self[None], gain_cross[None], gain_mlp[None]
    self_weights = (self_query, self_key, self_value, self_output)
    x1, self_ht, self_q, self_kt, self_v, self_raised, self_inverse, self_ot = self_forward(
        length, inputs, gain_self, self_weights
    )
    encoded, encoded_t = encode(
        arrived[:, 0, 0], conv_first, conv_second, enc_projection, enc_output, enc_expand, enc_narrow
    )
    cross_weights = (cross_query, cross_key, cross_value, cross_output)
    (
        dec_output, g2, g_gain_mlp, cross_ht, cross_q, cross_kt, cross_v, cross_raised,
        cross_inverse, cross_ot, g_expand, g_narrow,
    ) = cross_forward(
        length, x1, encoded, cotangent[0, 0], gain_cross, gain_mlp,
        cross_weights + (mlp_expand, mlp_narrow),
    )
    (
        g1, g_gain_cross, enc_state_grad, g_cross_query, g_cross_key, g_cross_value, g_cross_out,
    ) = cross_backward(
        (
            g2, x1, gain_cross, cross_ht, cross_q, cross_kt, cross_v, cross_raised,
            cross_inverse, cross_ot, encoded_t,
        ),
        cross_weights,
    )
    (
        dec_input_grad, g_gain_self, g_self_query, g_self_key, g_self_value, g_self_out,
    ) = self_backward(
        (
            g1, inputs, gain_self, self_ht, self_q, self_kt, self_v, self_raised,
            self_inverse, self_ot,
        ),
        self_weights,
    )
    matrices = [
        g_self_query, g_self_key, g_self_value, g_self_out,
        g_cross_query, g_cross_key, g_cross_value, g_cross_out,
        g_expand, g_narrow,
    ]
    gains = jnp.concatenate(
        [g_gain_self, g_gain_cross, g_gain_mlp, jnp.zeros((5, D), jnp.float32)]
    )
    totals, gains = sum_gradients(matrices, gains, members, groups)
    part = D // members
    gains = lax.dynamic_slice_in_dim(gains, lax.axis_index("tm") * part, part, 1)
    totals = totals + (gains[0], gains[1], gains[2])
    return (
        encoded[None, None],
        dec_output[None, None],
        dec_input_grad[None, None],
        enc_state_grad[None, None],
    ) + totals


def solution(mesh):
    placed = (
        P("tm", "clip", None, None),
        P(),
        P(),
        P(),
        P(),
        P(),
        P(),
        P("clip", "tm", None, None),
        P("clip", "tm"),
        P(),
        P(),
        P(),
        P(),
        P(),
        P(),
        P(),
        P(),
        P(),
        P(),
        P(),
        P(),
        P(),
        P("clip", "tm", None, None),
    )
    return jax.shard_map(
        functools.partial(body, mesh.shape["tm"], mesh.shape["clip"]),
        mesh=mesh,
        in_specs=placed,
        out_specs=(
            P("clip", "tm", None, None),
            P("clip", "tm", None, None),
            P("clip", "tm", None, None),
            P("clip", "tm", None, None),
            P("tm", None),
            P("tm", None),
            P("tm", None),
            P("tm", None),
            P("tm", None),
            P("tm", None),
            P("tm", None),
            P("tm", None),
            P("tm", None),
            P("tm", None),
            P("tm"),
            P("tm"),
            P("tm"),
        ),
        check_vma=False,
    )
```

```python
import functools
import math
from typing import Any, NamedTuple

import jax
import jax.numpy as jnp
import numpy as np
from jax import lax
from jax.experimental import pallas as pl
from jax.experimental.pallas import tpu as pltpu
from jax.sharding import PartitionSpec as P

D = 768
HEADS = 12
HD = 64
PAIRS = HEADS // 2
LANES = 2 * HD
SCALE = HD ** (-0.5)
LOW = jnp.bfloat16
WIDE = jnp.float32
INSIDE = pl.BlockSpec(memory_space=pltpu.VMEM)
FAR = pl.BlockSpec(memory_space=pltpu.HBM)
NUMBERS = pl.BlockSpec(memory_space=pltpu.SMEM)


def shape_of(shape, kind=LOW):
    return jax.ShapeDtypeStruct(shape, kind)


def parameters(megabytes=58):
    return pltpu.CompilerParams(vmem_limit_bytes=megabytes * 2**20)


def center(values):
    shifted = values - jnp.mean(values, axis=-1, keepdims=True)
    spread = jnp.mean(shifted * shifted, axis=-1, keepdims=True)
    root = lax.rsqrt(spread + 1e-05)
    return shifted * root, root


def center_back(gradient, values, gain):
    normed, root = center(values)
    inner = gradient * gain
    first = jnp.mean(inner, axis=-1, keepdims=True)
    second = jnp.mean(inner * normed, axis=-1, keepdims=True)
    gain_part = jnp.sum(gradient * normed, axis=0, keepdims=True)
    return root * (inner - first - normed * second), gain_part


def gelu(values):
    return values * (0.5 + 0.5 * lax.erf(values * 2**-0.5))


def gelu_both(values):
    area = 0.5 + 0.5 * lax.erf(values * 2**-0.5)
    slope = area + values * ((2 * math.pi) ** -0.5 * jnp.exp(-0.5 * values * values))
    return values * area, slope


def dot(left, right):
    return jnp.dot(left, right, preferred_element_type=WIDE)


def dot_back(left, right):
    return lax.dot_general(left, right, (((1,), (1,)), ((), ())), preferred_element_type=WIDE)


def dot_rows(left, right):
    return lax.dot_general(left, right, (((0,), (0,)), ((), ())), preferred_element_type=WIDE)


def strips(total, width):
    return [(at, min(width, total - at)) for at in range(0, total, width)]


class Fetch:
    def __init__(self, sources, targets, semaphores):
        self.copies = [
            pltpu.make_async_copy(source, target, semaphores.at[place])
            for place, (source, target) in enumerate(zip(sources, targets))
        ]
        for copy in self.copies:
            copy.start()

    def wait(self, place):
        self.copies[place].wait()


def pair_lanes(pair):
    return pl.ds(pl.multiple_of(pair * LANES, LANES), LANES)


def head_rows(pair, side):
    return pl.ds(pl.multiple_of(pair * LANES + side * HD, HD), HD)


def attend(q_ref, k_ref, vt_ref, bias_ref, ot_ref, inverse_ref, raised_ref):
    @pl.loop(0, PAIRS)
    def _(pair):
        queries, keys = q_ref[:, pair_lanes(pair)], k_ref[:, pair_lanes(pair)]
        for side in range(2):
            cut = slice(side * HD, (side + 1) * HD)
            scores = dot_back(keys[:, cut], queries[:, cut])
            if bias_ref is not None:
                scores = scores + bias_ref[...]
            raised = jnp.exp(scores - jnp.max(scores, axis=0, keepdims=True))
            inverse = 1.0 / jnp.sum(raised, axis=0, keepdims=True)
            raised = raised.astype(LOW)
            mixed = dot(vt_ref[head_rows(pair, side), :], raised)
            ot_ref[head_rows(pair, side), :] = (mixed * inverse).astype(LOW)
            if raised_ref is not None:
                raised_ref[2 * pair + side] = raised
                total = jnp.sum(raised.astype(WIDE), axis=0, keepdims=True)
                rank = lax.broadcasted_iota(jnp.int32, inverse_ref.shape[1:], 0)
                inverse_ref[2 * pair + side] = jnp.where(rank == 0, inverse, 1.0 / total)


def attend_pair(
    pair, q_ref, kt_ref, v_ref, raised_ref, inverse_ref, dot_ref, dov_ref, dqt_ref, dk_ref, dv_ref
):
    lanes = pair_lanes(pair)
    queries, values, grads = q_ref[:, lanes], v_ref[:, lanes], dov_ref[:, lanes]
    key_sides, value_sides = [], []
    for side in range(2):
        rows = head_rows(pair, side)
        cut = slice(side * HD, (side + 1) * HD)
        raised = raised_ref[side]
        weights = raised.astype(WIDE)
        weighted = weights * dot(values[:, cut], dot_ref[rows, :])
        delta = jnp.sum(weighted, axis=0, keepdims=True) * inverse_ref[2 * pair + side, 1:2, :]
        score_grad = (weighted - weights * delta).astype(LOW)
        dqt_ref[rows, :] = (dot(kt_ref[rows, :], score_grad) * SCALE).astype(LOW)
        key_sides.append(dot(score_grad, queries[:, cut]))
        value_sides.append(dot(raised, grads[:, cut]))
    dk_ref[:, lanes] = jnp.concatenate(key_sides, axis=1).astype(LOW)
    dv_ref[:, lanes] = jnp.concatenate(value_sides, axis=1).astype(LOW)


def attend_back(q_ref, kt_ref, v_ref, raised_ref, *rest):
    @pl.loop(0, PAIRS)
    def _(pair):
        attend_pair(pair, q_ref, kt_ref, v_ref, raised_ref.at[pl.ds(2 * pair, 2)], *rest)


def encoder_kernel(
    mel_ref, position_ref, first_h, second_h, joint_h, output_h, expand_h, narrow_h,
    out_ref, out_t_ref,
    first_w, second_w, joint_w, output_w, expand_w, narrow_w,
    even, odd, state, hidden, q, k, vt, mixed_t, semaphores,
):
    length = out_ref.shape[0]
    fetch = Fetch(
        (first_h, second_h, joint_h, output_h, expand_h, narrow_h),
        (first_w, second_w, joint_w, output_w, expand_w, narrow_w),
        semaphores,
    )
    taps = [mel_ref[pl.ds(offset, length, stride=2), :].astype(LOW) for offset in range(4)]
    fetch.wait(0)
    for at, width in strips(D, 256):
        cols = pl.ds(at, width)
        for start, target in ((0, even), (1, odd)):
            total = sum(dot(taps[start + o], first_w[o, :, cols]) for o in range(3))
            target[:, cols] = gelu(total).astype(LOW)
    fetch.wait(1)
    ranks = lax.broadcasted_iota(jnp.int32, (length, 256), 0)
    for at, width in strips(D, 256):
        cols = pl.ds(at, width)
        before = pltpu.roll(dot(odd[...], second_w[0, :, cols]), 1, 0)
        total = dot(even[...], second_w[1, :, cols]) + dot(odd[...], second_w[2, :, cols])
        total = total + jnp.where(ranks == 0, 0.0, before)
        state[:, cols] = gelu(total) + position_ref[:, cols]
    hidden[...] = center(state[...])[0].astype(LOW)
    fetch.wait(2)
    for at, width in strips(D, 256):
        cols = pl.ds(at, width)
        q[:, cols] = (dot(hidden[...], joint_w[:, cols]).astype(LOW) * SCALE).astype(LOW)
        k[:, cols] = dot(hidden[...], joint_w[:, pl.ds(D + at, width)]).astype(LOW)
        vt[cols, :] = dot(hidden[...], joint_w[:, pl.ds(2 * D + at, width)]).astype(LOW).T
    attend(q, k, vt, None, mixed_t, None, None)
    fetch.wait(3)
    mixed = mixed_t[...].T
    for at, width in strips(D, 256):
        cols = pl.ds(at, width)
        state[:, cols] += dot(mixed, output_w[:, cols])
    hidden[...] = center(state[...])[0].astype(LOW)
    fetch.wait(4)
    fetch.wait(5)

    @pl.loop(0, expand_w.shape[1] // 512)
    def _(strip):
        cols = pl.ds(pl.multiple_of(strip * 512, 512), 512)
        widened = gelu(dot(hidden[...], expand_w[:, cols])).astype(LOW)
        state[...] += dot(widened, narrow_w[cols, :])

    encoded = center(state[...])[0].astype(LOW)
    out_ref[...] = encoded
    out_t_ref[...] = encoded.T


def encode(mel_clips, conv_first, conv_second, enc_projection, enc_output, enc_expand, enc_narrow):
    frames = mel_clips.shape[0]
    length = frames // 2
    mel = jnp.pad(mel_clips.astype(WIDE), ((1, 7), (0, 0)))
    weights = (conv_first, conv_second, enc_projection, enc_output, enc_expand, enc_narrow)
    return pl.pallas_call(
        encoder_kernel,
        out_shape=(shape_of((length, D)), shape_of((D, length))),
        in_specs=[INSIDE] * 2 + [FAR] * 6,
        out_specs=(INSIDE, INSIDE),
        scratch_shapes=[pltpu.VMEM(weight.shape, LOW) for weight in weights]
        + [
            pltpu.VMEM((length, D), LOW),
            pltpu.VMEM((length, D), LOW),
            pltpu.VMEM((length, D), WIDE),
            pltpu.VMEM((length, D), LOW),
            pltpu.VMEM((length, D), LOW),
            pltpu.VMEM((length, D), LOW),
            pltpu.VMEM((D, length), LOW),
            pltpu.VMEM((D, length), LOW),
            pltpu.SemaphoreType.DMA((6,)),
        ],
        compiler_params=parameters(),
    )(mel, sinusoids(length, D), *weights)


def sinusoids(length, features):
    halfway = features // 2
    inverse = np.exp(-math.log(10000.0) / (halfway - 1) * np.arange(halfway)).astype(np.float32)
    angles = np.arange(length, dtype=np.float32)[:, None] * inverse[None, :]
    angles = angles.astype(np.float64)
    return jnp.asarray(np.concatenate([np.sin(angles), np.cos(angles)], axis=1).astype(np.float32))


def self_kernel(
    length_ref, x_ref, gain_ref, output_h, query_h, key_h, value_h,
    x1_ref, ht_ref, q_ref, kt_ref, v_ref, raised_ref, inverse_ref, ot_ref,
    output_w, query_w, key_w, value_w, hidden, k, vt, bias, semaphores,
):
    fetch = Fetch(
        (query_h, key_h, value_h, output_h), (query_w, key_w, value_w, output_w), semaphores
    )
    rows = x_ref.shape[0]
    hidden[...] = (center(x_ref[...].astype(WIDE))[0] * gain_ref[...]).astype(LOW)
    keys = lax.broadcasted_iota(jnp.int32, (rows, rows), 0)
    queries = lax.broadcasted_iota(jnp.int32, (rows, rows), 1)
    allowed = (keys <= queries) & (keys < length_ref[0])
    bias[...] = jnp.where(allowed, 0.0, -1e30)
    fetch.wait(0)
    fetch.wait(1)
    fetch.wait(2)
    for at, width in strips(D, 256):
        cols = pl.ds(at, width)
        q_ref[:, cols] = (dot(hidden[...], query_w[:, cols]).astype(LOW) * SCALE).astype(LOW)
        part = dot(hidden[...], key_w[:, cols]).astype(LOW)
        k[:, cols] = part
        kt_ref[cols, :] = part.T
        part = dot(hidden[...], value_w[:, cols]).astype(LOW)
        v_ref[:, cols] = part
        vt[cols, :] = part.T
    ht_ref[...] = hidden[...].T
    attend(q_ref, k, vt, bias, ot_ref, inverse_ref, raised_ref)
    fetch.wait(3)
    mixed = ot_ref[...].T
    for at, width in strips(D, 256):
        cols = pl.ds(at, width)
        x1_ref[:, cols] = x_ref[:, cols].astype(WIDE) + dot(mixed, output_w[:, cols])


def self_forward(lengths, inputs, gain, weights):
    rows = inputs.shape[0]
    plain, turned = (rows, D), (D, rows)
    x1, *layer = pl.pallas_call(
        self_kernel,
        out_shape=(
            shape_of(plain, WIDE), shape_of(turned), shape_of(plain), shape_of(turned),
            shape_of(plain), shape_of((HEADS, rows, rows)), shape_of((HEADS, 8, rows), WIDE),
            shape_of(turned),
        ),
        in_specs=[NUMBERS, INSIDE, INSIDE] + [FAR] * 4,
        out_specs=(INSIDE,) * 8,
        scratch_shapes=[pltpu.VMEM((D, D), LOW)] * 4
        + [
            pltpu.VMEM(plain, LOW),
            pltpu.VMEM(plain, LOW),
            pltpu.VMEM(turned, LOW),
            pltpu.VMEM((rows, rows), WIDE),
            pltpu.SemaphoreType.DMA((4,)),
        ],
        compiler_params=parameters(),
    )(lengths, inputs, gain, *weights)
    return x1, Layer(*layer)


class Layer(NamedTuple):
    ht: Any
    q: Any
    kt: Any
    v: Any
    raised: Any
    inverse: Any
    ot: Any


class Weights(NamedTuple):
    output: Any
    query: Any
    key: Any
    value: Any


def cross_kernel(
    length_ref, x1_ref, encoded_ref, cotangent_ref, gain_cross_ref, gain_mlp_ref,
    output_h, query_h, key_h, value_h,
    x2_ref, hidden_ref, hidden_t_ref, b3_ref,
    ht_ref, q_ref, kt_ref, v_ref, raised_ref, inverse_ref, ot_ref,
    output_w, query_w, key_w, value_w, hidden, k, vt, semaphores,
):
    fetch = Fetch(
        (query_h, key_h, value_h, output_h), (query_w, key_w, value_w, output_w), semaphores
    )
    rows = x1_ref.shape[0]
    hidden[...] = (center(x1_ref[...])[0] * gain_cross_ref[...]).astype(LOW)
    ht_ref[...] = hidden[...].T
    live = lax.broadcasted_iota(jnp.int32, (rows, D), 0) < length_ref[0]
    b3_ref[...] = jnp.where(live, cotangent_ref[...].astype(WIDE), 0.0).astype(LOW)
    fetch.wait(0)
    fetch.wait(1)
    fetch.wait(2)
    for at, width in strips(D, 256):
        cols = pl.ds(at, width)
        q_ref[:, cols] = (dot(hidden[...], query_w[:, cols]).astype(LOW) * SCALE).astype(LOW)
        part = dot(encoded_ref[...], key_w[:, cols]).astype(LOW)
        k[:, cols] = part
        kt_ref[cols, :] = part.T
        part = dot(encoded_ref[...], value_w[:, cols]).astype(LOW)
        v_ref[:, cols] = part
        vt[cols, :] = part.T
    attend(q_ref, k, vt, None, ot_ref, inverse_ref, raised_ref)
    fetch.wait(3)
    mixed = ot_ref[...].T
    for at, width in strips(D, 256):
        cols = pl.ds(at, width)
        x2_ref[:, cols] = x1_ref[:, cols] + dot(mixed, output_w[:, cols])
    hidden = (center(x2_ref[...])[0] * gain_mlp_ref[...]).astype(LOW)
    hidden_ref[...] = hidden
    hidden_t_ref[...] = hidden.T


def cross_forward(lengths, x1, encoded, cotangent, gain_cross, gain_mlp, weights):
    rows, frames = x1.shape[0], encoded.shape[0]
    plain, turned = (rows, D), (D, rows)
    x2, hidden, hidden_t, b3, *layer = pl.pallas_call(
        cross_kernel,
        out_shape=(
            shape_of(plain, WIDE), shape_of(plain), shape_of(turned), shape_of(plain),
            shape_of(turned), shape_of(plain), shape_of((D, frames)), shape_of((frames, D)),
            shape_of((HEADS, frames, rows)), shape_of((HEADS, 8, rows), WIDE), shape_of(turned),
        ),
        in_specs=[NUMBERS] + [INSIDE] * 5 + [FAR] * 4,
        out_specs=(INSIDE,) * 11,
        scratch_shapes=[pltpu.VMEM(weight.shape, LOW) for weight in weights]
        + [
            pltpu.VMEM(plain, LOW),
            pltpu.VMEM((frames, D), LOW),
            pltpu.VMEM((D, frames), LOW),
            pltpu.SemaphoreType.DMA((4,)),
        ],
        compiler_params=parameters(),
    )(lengths, x1, encoded, cotangent, gain_cross, gain_mlp, *weights)
    return x2, hidden, hidden_t, b3, Layer(*layer)


def feed_kernel(
    length_ref, x2_ref, hidden, hidden_t, b3, gain_ref, expand_h, narrow_h,
    out_ref, g2_ref, gain_grad_ref, expand_grad_ref, narrow_grad_ref,
    expand_w, narrow_w, x3, back, semaphores,
):
    fetch = Fetch((expand_h, narrow_h), (expand_w, narrow_w), semaphores)
    x3[...] = x2_ref[...]
    back[...] = jnp.zeros_like(back)
    fetch.wait(0)
    fetch.wait(1)

    @pl.loop(0, expand_w.shape[1] // 512)
    def _(strip):
        cols = pl.ds(pl.multiple_of(strip * 512, 512), 512)
        active, slope = gelu_both(dot(hidden[...], expand_w[:, cols]))
        active = active.astype(LOW)
        grad = (slope * dot_back(b3[...], narrow_w[cols, :])).astype(LOW)
        x3[...] += dot(active, narrow_w[cols, :])
        narrow_grad_ref[cols, :] = dot_rows(active, b3[...]).astype(LOW)
        expand_grad_ref[:, cols] = dot(hidden_t[...], grad).astype(LOW)
        back[...] += dot_back(grad, expand_w[:, cols])

    live = lax.broadcasted_iota(jnp.int32, x3.shape, 0) < length_ref[0]
    out_ref[...] = jnp.where(live, x3[...], 0.0).astype(LOW)
    part, gain_part = center_back(back[...], x2_ref[...], gain_ref[...])
    gain_grad_ref[...] = gain_part
    g2_ref[...] = b3[...].astype(WIDE) + part


def feed_both(lengths, x2, hidden, hidden_t, b3, gain_mlp, expand, narrow):
    plain = x2.shape
    return pl.pallas_call(
        feed_kernel,
        out_shape=(
            shape_of(plain), shape_of(plain, WIDE), shape_of((1, D), WIDE),
            shape_of(expand.shape), shape_of(narrow.shape),
        ),
        in_specs=[NUMBERS] + [INSIDE] * 5 + [FAR] * 2,
        out_specs=(INSIDE,) * 5,
        scratch_shapes=[
            pltpu.VMEM(expand.shape, LOW),
            pltpu.VMEM(narrow.shape, LOW),
            pltpu.VMEM(plain, WIDE),
            pltpu.VMEM(plain, WIDE),
            pltpu.SemaphoreType.DMA((2,)),
        ],
        compiler_params=parameters(),
    )(lengths, x2, hidden, hidden_t, b3, gain_mlp, expand, narrow)


def spread_grads(out_grad, output_w, inverse_ref, dov, dot_t):
    for at, width in strips(D, 256):
        part = dot_back(out_grad, output_w[at : at + width, :]).astype(LOW).T
        sides = [
            part[head * HD : (head + 1) * HD, :].astype(WIDE) * inverse_ref[at // HD + head, 0:1, :]
            for head in range(width // HD)
        ]
        part = jnp.concatenate(sides, axis=0).astype(LOW)
        dot_t[at : at + width, :] = part
        dov[:, at : at + width] = part.T


def cross_back_kernel(
    g2_ref, x1_ref, gain_ref, ht_ref, q_ref, kt_ref, v_ref, raised_ref, inverse_ref, ot_ref,
    encoded_t_ref, output_h, query_h, key_h, value_h,
    g1_ref, gain_grad_ref, state_grad_ref, query_g, key_g, value_g, output_g,
    output_w, query_w, key_w, value_w, dov, dot_t, dqt, dk, dv, semaphores,
):
    fetch = Fetch(
        (output_h, query_h, key_h, value_h), (output_w, query_w, key_w, value_w), semaphores
    )
    b2 = g2_ref[...].astype(LOW)
    fetch.wait(0)
    spread_grads(b2, output_w, inverse_ref, dov, dot_t)
    for at, width in strips(D, 256):
        output_g[:, at : at + width] = dot(ot_ref[...], b2[:, at : at + width]).astype(LOW)
    attend_back(q_ref, kt_ref, v_ref, raised_ref, inverse_ref, dot_t, dov, dqt, dk, dv)
    dq = dqt[...].T
    for place in range(1, 4):
        fetch.wait(place)
    for at, width in strips(D, 256):
        cols = slice(at, at + width)
        query_g[:, cols] = dot(ht_ref[...], dq[:, cols]).astype(LOW)
        key_g[:, cols] = dot(encoded_t_ref[...], dk[:, cols]).astype(LOW)
        value_g[:, cols] = dot(encoded_t_ref[...], dv[:, cols]).astype(LOW)
        state_grad_ref[:, cols] = dot_back(dk[...], key_w[cols, :]) + dot_back(
            dv[...], value_w[cols, :]
        )
    part, gain_part = center_back(dot_back(dq, query_w[...]), x1_ref[...], gain_ref[...])
    gain_grad_ref[...] = gain_part
    g1_ref[...] = g2_ref[...] + part


def cross_backward(operands, weights):
    rows, frames = operands[0].shape[0], operands[10].shape[1]
    plain, turned, square = (rows, D), (D, rows), shape_of((D, D))
    return pl.pallas_call(
        cross_back_kernel,
        out_shape=(
            shape_of(plain, WIDE), shape_of((1, D), WIDE), shape_of((frames, D), WIDE),
            square, square, square, square,
        ),
        in_specs=[INSIDE] * 11 + [FAR] * 4,
        out_specs=(INSIDE,) * 7,
        scratch_shapes=[pltpu.VMEM((D, D), LOW)] * 4
        + [
            pltpu.VMEM(plain, LOW),
            pltpu.VMEM(turned, LOW),
            pltpu.VMEM(turned, LOW),
            pltpu.VMEM((frames, D), LOW),
            pltpu.VMEM((frames, D), LOW),
            pltpu.SemaphoreType.DMA((4,)),
        ],
        compiler_params=parameters(),
    )(*operands, *weights)


def self_back_kernel(
    g1_ref, x_ref, gain_ref, ht_ref, q_ref, kt_ref, v_ref, raised_ref, inverse_ref, ot_ref,
    output_h, query_h, key_h, value_h,
    input_grad_ref, gain_grad_ref, query_g, key_g, value_g, output_g,
    output_w, query_w, key_w, value_w, dov, dot_t, dqt, dk, dv, semaphores,
):
    fetch = Fetch(
        (output_h, query_h, key_h, value_h), (output_w, query_w, key_w, value_w), semaphores
    )
    b1 = g1_ref[...].astype(LOW)
    fetch.wait(0)
    spread_grads(b1, output_w, inverse_ref, dov, dot_t)
    for at, width in strips(D, 256):
        output_g[:, at : at + width] = dot(ot_ref[...], b1[:, at : at + width]).astype(LOW)
    attend_back(q_ref, kt_ref, v_ref, raised_ref, inverse_ref, dot_t, dov, dqt, dk, dv)
    dq = dqt[...].T
    for place in range(1, 4):
        fetch.wait(place)
    for at, width in strips(D, 256):
        cols = slice(at, at + width)
        query_g[:, cols] = dot(ht_ref[...], dq[:, cols]).astype(LOW)
        key_g[:, cols] = dot(ht_ref[...], dk[:, cols]).astype(LOW)
        value_g[:, cols] = dot(ht_ref[...], dv[:, cols]).astype(LOW)
        input_grad_ref[:, cols] = (
            dot_back(dq, query_w[cols, :])
            + dot_back(dk[...], key_w[cols, :])
            + dot_back(dv[...], value_w[cols, :])
        )
    part, gain_part = center_back(
        input_grad_ref[...], x_ref[...].astype(WIDE), gain_ref[...]
    )
    gain_grad_ref[...] = gain_part
    input_grad_ref[...] = g1_ref[...] + part


def self_backward(operands, weights):
    rows = operands[0].shape[0]
    plain, turned, square = (rows, D), (D, rows), shape_of((D, D))
    return pl.pallas_call(
        self_back_kernel,
        out_shape=(shape_of(plain, WIDE), shape_of((1, D), WIDE), square, square, square, square),
        in_specs=[INSIDE] * 10 + [FAR] * 4,
        out_specs=(INSIDE,) * 6,
        scratch_shapes=[pltpu.VMEM((D, D), LOW)] * 4
        + [
            pltpu.VMEM(plain, LOW),
            pltpu.VMEM(turned, LOW),
            pltpu.VMEM(turned, LOW),
            pltpu.VMEM(plain, LOW),
            pltpu.VMEM(plain, LOW),
            pltpu.SemaphoreType.DMA((4,)),
        ],
        compiler_params=parameters(),
    )(*operands, *weights)


def trade(values, axis, size, bit):
    return lax.ppermute(values, axis, [(i, i ^ bit) for i in range(size)])


def add_rounded(left, right):
    return (left.astype(jnp.float32) + right.astype(jnp.float32)).astype(jnp.bfloat16)


def halve(values, dim, axis, size, bit):
    mine = (lax.axis_index(axis) // bit) % 2
    kept = lax.dynamic_index_in_dim(values, mine, dim, keepdims=False)
    sent = lax.dynamic_index_in_dim(values, 1 - mine, dim, keepdims=False)
    return add_rounded(kept, trade(sent, axis, size, bit))


def bits_of(size):
    return [1 << k for k in range(size.bit_length() - 1)]


def members_first(values, members, groups):
    for bit in bits_of(members):
        values = halve(values, len(values.shape) - 3, "tm", members, bit)
    for bit in bits_of(groups):
        values = add_rounded(values, trade(values, "clip", groups, bit))
    return values.astype(jnp.float32)


def groups_first(values, members, groups):
    values = halve(values, len(values.shape) - 3, "tm", members, 1)
    lead = values.shape[:-2]
    rows, columns = values.shape[-2:]
    for bit in bits_of(groups):
        values = values.reshape(lead + (2, values.shape[-2] // 2, columns))
        values = halve(values, len(lead), "clip", groups, bit)
    for bit in bits_of(members)[1:]:
        values = halve(values, len(values.shape) - 3, "tm", members, bit)
    for bit in bits_of(groups)[::-1]:
        mine = (lax.axis_index("clip") // bit) % 2
        other = trade(values, "clip", groups, bit)
        values = jnp.where(
            mine == 0, jnp.concatenate([values, other]), jnp.concatenate([other, values])
        )
    return values.astype(jnp.float32)


def sum_plain(matrices, gains, members, groups):
    split = (2,) * (members.bit_length() - 1)
    totals = []
    for place, matrix in enumerate(matrices):
        blocks = matrix.reshape(split + (matrix.shape[0] // members, matrix.shape[1]))
        totals.append((members_first, groups_first)[place % 2](blocks, members, groups))
    return tuple(totals), lax.psum(gains, ("tm", "clip"))


MESH = pl.DeviceIdType.MESH
PART = 48
UNITS = 16
UNIT_ORDER = (8, 9, 10, 11, 12, 13, 14, 15, 7, 4, 5, 6, 3, 0, 1, 2)
LETTERS = "ABBCAACBCBBBABBA"
STEPS = (
    1000, 0, 1001, 1, 8, 1002, 9, 16, 1003, 2, 17, 24, 32, 40, 1004, 48,
    1005, 10, 25, 3, 33, 41, 49, 56, 1006, 64, 1007, 11, 18, 57, 65, 26,
    1008, 1009, 4, 1010, 34, 42, 50, 5, 12, 58, 72, 80, 88, 1011, 1012, 19,
    73, 81, 89, 1013, 96, 1014, 59, 66, 97, 1015, 27, 74, 1016, 1017, 20, 35,
    82, 51, 28, 98, 104, 112, 120, 1018, 13, 75, 90, 105, 43, 29, 113, 14,
    60, 83, 121, 52, 67, 99, 91, 21, 76, 106, 84, 122, 92, 36, 44, 114,
    61, 53, 68, 107, 22, 123, 77, 37, 85, 115, 45, 93, 108, 62, 100, 69,
    78, 116, 86, 124, 94, 109, 101, 125, 117, 110, 118,
)


def add_halves(left, right):
    return (left.astype(WIDE) + right.astype(WIDE)).astype(LOW)


class Sums:
    def __init__(self, made, emit, s):
        self.made, self.emit = made, emit
        self.got0, self.a, self.b = s.got0, (s.a1, s.a2, s.a3, s.a4), (s.b1, s.b2, s.b3, s.b4, s.b5)
        self.send_sem, self.recv_sem = s.send_sem, s.recv_sem
        self.gain_send, self.gain_recv = s.gain_send, s.gain_recv
        self.gain_sum, self.gain_got = s.gain_sum, s.gain_got
        tm, clip = lax.axis_index("tm"), lax.axis_index("clip")
        self.core, self.x, self.low, self.high = tm % 2, (tm // 2) % 2, (tm // 4) % 2, tm // 8
        self.core_peer = (tm + 1 - 2 * self.core, clip)
        self.x_peer = (tm + 2 - 4 * self.x, clip)
        self.low_peer = (tm + 4 - 8 * self.low, clip)
        self.high_peer = (tm + 8 - 16 * self.high, clip)
        self.clip_peer = (tm, 1 - clip)
        self.peers = (self.core_peer, self.x_peer, self.low_peer, self.high_peer, self.clip_peer)
        half = D // 2
        self.mine = pl.ds(pl.multiple_of(clip * half, half), half)
        self.other = pl.ds(pl.multiple_of((1 - clip) * half, half), half)
        self.copies, self.gain_copies, self.places = {}, {}, {}
        self.started, self.left = [], set()
        self.slots = {
            place: sum((LETTERS[k] == "B") == (LETTERS[place] == "B") for k in range(place))
            for place in range(UNITS)
        }

    def meet(self):
        barrier = pltpu.get_barrier_semaphore()
        for peer in self.peers:
            pl.semaphore_signal(barrier, inc=1, device_id=peer, device_id_type=MESH)
        pl.semaphore_wait(barrier, len(self.peers))

    def send(self, src, dst, stage, place, peer):
        copy = pltpu.make_async_remote_copy(
            src_ref=src,
            dst_ref=dst,
            send_sem=self.send_sem.at[stage, place],
            recv_sem=self.recv_sem.at[stage, place],
            device_id=peer,
            device_id_type=MESH,
        )
        copy.start()
        self.places[stage, place] = len(self.started)
        self.started.append(copy)
        self.copies[stage, place] = copy

    def step(self, stage, place):
        if stage == 0:
            buffer, number = self.made(place)
            source = buffer.at[:, :, :, 1 - self.core, number]
            self.send(source, self.got0.at[place], 0, place, self.core_peer)
            return
        self.copies[stage - 1, place].wait_recv()
        if stage == 1:
            self.add_cores(place)
        step = dict(A=self.step_a, B=self.step_b, C=self.step_c)[LETTERS[place]]
        step(stage, place, self.slots[place])

    def add_cores(self, place):
        got0 = self.got0
        buffer, number = self.made(place)

        @pl.loop(0, 8)
        def _(block):
            i, j, k = block // 4, (block // 2) % 2, block % 2
            mine = buffer[i, j, k, self.core, number]
            got0[place, i, j, k] = add_halves(got0[place, i, j, k], mine)

    def step_a(self, stage, place, slot):
        got0, (a1, a2, a3, a4) = self.got0, self.a
        if stage == 1:
            source = got0.at[place, :, :, 1 - self.x]
            self.send(source, a1.at[slot], 1, place, self.x_peer)
        elif stage == 2:

            @pl.loop(0, 4)
            def _(block):
                i, j = block // 2, block % 2
                a1[slot, i, j] = add_halves(a1[slot, i, j], got0[place, i, j, self.x])

            self.send(a1.at[slot, :, 1 - self.low], a2.at[slot], 2, place, self.low_peer)
        elif stage == 3:

            @pl.loop(0, 2)
            def _(i):
                a2[slot, i] = add_halves(a2[slot, i], a1[slot, i, self.low])

            self.send(a2.at[slot, 1 - self.high], a3.at[slot], 3, place, self.high_peer)
        else:
            self.last_two(stage, place, slot, self.high)

    def step_c(self, stage, place, slot):
        got0, (a1, a2, a3, a4) = self.got0, self.a
        if stage == 1:
            source = got0.at[place, :, 1 - self.low]
            self.send(source, a1.at[slot], 1, place, self.low_peer)
        elif stage == 2:

            @pl.loop(0, 4)
            def _(block):
                i, j = block // 2, block % 2
                a1[slot, i, j] = add_halves(a1[slot, i, j], got0[place, i, self.low, j])

            self.send(a1.at[slot, 1 - self.high], a2.at[slot], 2, place, self.high_peer)
        elif stage == 3:

            @pl.loop(0, 2)
            def _(i):
                a2[slot, i] = add_halves(a2[slot, i], a1[slot, self.high, i])

            self.send(a2.at[slot, 1 - self.x], a3.at[slot], 3, place, self.x_peer)
        else:
            self.last_two(stage, place, slot, self.x)

    def last_two(self, stage, place, slot, side):
        a1, a2, a3, a4 = self.a
        if stage == 4:
            a3[slot] = add_halves(a3[slot], a2[slot, side])
            self.send(a3.at[slot], a4.at[slot], 4, place, self.clip_peer)
        else:
            total = a3[slot].astype(WIDE) + a4[slot].astype(WIDE)
            self.emit(UNIT_ORDER[place], slice(0, D), total)

    def step_b(self, stage, place, slot):
        got0, (b1, b2, b3, b4, b5) = self.got0, self.b
        if stage == 1:
            source = got0.at[place, :, :, :, :, self.other]
            self.send(source, b1.at[slot], 1, place, self.clip_peer)
        elif stage == 2:

            @pl.loop(0, 8)
            def _(block):
                i, j, k = block // 4, (block // 2) % 2, block % 2
                b1[slot, i, j, k] = add_halves(
                    b1[slot, i, j, k], got0[place, i, j, k, :, self.mine]
                )

            self.send(b1.at[slot, :, :, 1 - self.x], b2.at[slot], 2, place, self.x_peer)
        elif stage == 3:

            @pl.loop(0, 4)
            def _(block):
                i, j = block // 2, block % 2
                b2[slot, i, j] = add_halves(b2[slot, i, j], b1[slot, i, j, self.x])

            self.send(b2.at[slot, :, 1 - self.low], b3.at[slot], 3, place, self.low_peer)
        elif stage == 4:

            @pl.loop(0, 2)
            def _(i):
                b3[slot, i] = add_halves(b3[slot, i], b2[slot, i, self.low])

            self.send(b3.at[slot, 1 - self.high], b4.at[slot], 4, place, self.high_peer)
        elif stage == 5:
            b4[slot] = add_halves(b4[slot], b3[slot, self.high])
            self.send(b4.at[slot], b5.at[slot], 5, place, self.clip_peer)
        else:
            self.emit(UNIT_ORDER[place], self.mine, b4[slot].astype(WIDE))
            self.emit(UNIT_ORDER[place], self.other, b5[slot].astype(WIDE))

    def gain_step(self, number):
        if number > 0:
            self.gain_copies[number - 1].wait_recv()
            self.gain_sum[number] = self.gain_sum[number - 1] + self.gain_got[number - 1]
        if number < len(self.peers):
            copy = pltpu.make_async_remote_copy(
                src_ref=self.gain_sum.at[number],
                dst_ref=self.gain_got.at[number],
                send_sem=self.gain_send.at[number],
                recv_sem=self.gain_recv.at[number],
                device_id=self.peers[number],
                device_id_type=MESH,
            )
            copy.start()
            self.started.append(copy)
            self.gain_copies[number] = copy

    def leave(self, place):
        self.copies[0, place].wait_send()
        self.left.add(self.places[0, place])

    def finish(self):
        for number, copy in enumerate(self.started):
            if number not in self.left:
                copy.wait_send()


class BackIn(NamedTuple):
    length: Any
    x2: Any
    hidden: Any
    hidden_t: Any
    b3: Any
    x1: Any
    x: Any
    encoded_t: Any
    gain_mlp: Any
    gain_cross: Any
    gain_self: Any
    expand_w: Any
    narrow_w: Any
    cross: Layer
    own: Layer
    cross_w: Weights
    own_w: Weights


class BackOut(NamedTuple):
    output: Any
    input_grad: Any
    state_grad: Any
    summed: Any
    gains: Any


class Room(NamedTuple):
    x1: Any
    encoded_t: Any
    cross: Layer
    own: Layer
    weight: Any
    raised: Any
    g: Any
    x3: Any
    low: Any
    dov: Any
    dot_t: Any
    dqt: Any
    dk: Any
    dv: Any
    kept: Any
    narrow: Any
    total: Any
    got0: Any
    a1: Any
    a2: Any
    a3: Any
    a4: Any
    b1: Any
    b2: Any
    b3: Any
    b4: Any
    b5: Any
    gain_sum: Any
    gain_got: Any
    fetch_sem: Any
    raised_sem: Any
    out_sem: Any
    send_sem: Any
    recv_sem: Any
    gain_send: Any
    gain_recv: Any


class Once:
    def __init__(self, copy):
        self.copy, self.pending = copy, True
        copy.start()

    def ready(self):
        if self.pending:
            self.copy.wait()
        self.pending = False


def back_kernel(tree, *refs):
    given, out, s = jax.tree.unflatten(tree, refs)
    count = [0]

    def fetch(source, target):
        copy = pltpu.make_async_copy(source, target, s.fetch_sem.at[count[0]])
        count[0] += 1
        return Once(copy)

    def fetch_layer(source, target):
        return {
            field: fetch(getattr(source, field), getattr(target, field))
            for field in Layer._fields
            if getattr(target, field) is not None
        }

    def raised_copy(layer, pair):
        source = layer.raised.at[pl.ds(2 * pair, 2)]
        slot = pair % 2
        return pltpu.make_async_copy(
            source, s.raised.at[slot, :, pl.ds(0, source.shape[1])], s.raised_sem.at[slot]
        )

    def made(place):
        if 4 <= place < 8 or place >= 12:
            return s.narrow, place % 4
        return s.kept, place % 4 + 4 * (place >= 8)

    def keep(place, at, width, values):
        buffer, number = made(place)
        buffer[:, :, :, :, number, :, at : at + width] = values.astype(LOW).reshape(
            2, 2, 2, 2, PART, width
        )

    def emit(unit, cols, total):
        s.total[unit, :, cols] = total

    sums = Sums(made, emit, s)
    live = {}
    waits = {}

    def feed(strip):
        def run():
            first, second = s.weight[2 * (strip % 2)], s.weight[2 * (strip % 2) + 1]
            if strip == 0:
                for name in ("hidden", "hidden_t", "b3", "x2"):
                    waits[name].ready()
            for at, width in strips(D, 2 * 4 * PART):
                cols = slice(at, at + width)
                if at == 0:
                    waits["first", strip].ready()
                active, slope = gelu_both(dot(s.dk[...], first[:, cols]))
                active = active.astype(LOW)
                if at == 0:
                    waits["second", strip].ready()
                grad = (slope * dot_back(s.low[...], second[cols, :])).astype(LOW)
                keep(strip, at, width, dot(s.dot_t[...], grad))
                s.narrow[strip // 2, strip % 2, at // width] = (
                    dot_rows(active, s.low[...]).astype(LOW).reshape(2, 4, PART, D)
                )
                forward, backward = dot(active, second[cols, :]), dot_back(grad, first[:, cols])
                if strip == 0 and at == 0:
                    s.x3[...] = s.x1[...] + forward
                    s.g[...] = backward
                else:
                    s.x3[...] += forward
                    s.g[...] += backward
            if strip < 2:
                fetch_feed(strip + 2)

        return run

    def fetch_feed(strip):
        cols = pl.ds(strip * D, D)
        waits["first", strip] = fetch(given.expand_w.at[:, cols], s.weight[2 * (strip % 2)])
        waits["second", strip] = fetch(given.narrow_w.at[cols, :], s.weight[2 * (strip % 2) + 1])

    def feed_end():
        for place, name in enumerate(Weights._fields):
            waits["cross", name] = fetch(getattr(given.cross_w, name), s.weight[place])
        live = lax.broadcasted_iota(jnp.int32, s.x3.shape, 0) < given.length[0]
        s.dv[...] = jnp.where(live, s.x3[...], 0.0).astype(LOW)
        waits["output"] = Once(pltpu.make_async_copy(s.dv, out.output, s.out_sem.at[0]))
        part, gain_part = center_back(s.g[...], s.x1[...], given.gain_mlp[...])
        s.gain_sum[0, 2:3, :] = gain_part
        s.g[...] = s.low[...].astype(WIDE) + part
        waits["x1"] = fetch(given.x1, s.x1)

    def spread(layer, room, name):
        def run():
            waits[name, "output"].ready()
            waits[name]["inverse"].ready()
            s.low[...] = s.g[...].astype(LOW)
            spread_grads(s.low[...], s.weight[0], room.inverse, s.dov, s.dot_t)
            if name == "cross":
                waits["own", "output"] = fetch(given.own_w.output, s.weight[0])

        return run

    def output_grad(room, name, place):
        def run():
            waits[name]["ot"].ready()
            if name == "own":
                for unit in range(4, 8):
                    sums.leave(unit)
            for at, width in strips(D, 256):
                keep(place, at, width, dot(room.ot[...], s.low[:, at : at + width]))

        return run

    def attention(layer, room, name, first):
        def run():
            for field in ("q", "kt", "v"):
                waits[name][field].ready()
            waits["output"].ready()
            inner = layer.raised.shape[1]

            @pl.loop(first, first + 2)
            def _(pair):
                raised_copy(layer, pair).wait()
                slot = pair % 2
                attend_pair(
                    pair,
                    room.q,
                    room.kt,
                    room.v,
                    s.raised.at[slot, :, pl.ds(0, inner)],
                    room.inverse,
                    s.dot_t,
                    s.dov,
                    s.dqt,
                    s.dk.at[pl.ds(0, inner)],
                    s.dv.at[pl.ds(0, inner)],
                )
                if first < PAIRS - 2:
                    raised_copy(layer, pair + 2).start()
                elif name == "cross":
                    raised_copy(given.own, slot).start()

        return run

    def cross_grads():
        waits["cross"]["ht"].ready()
        waits["encoded_t"].ready()
        frames = s.encoded_t.shape[1]
        s.low[...] = s.dqt[...].T
        for at, width in strips(D, 256):
            cols = slice(at, at + width)
            keep(9, at, width, dot(s.cross.ht[...], s.low[:, cols]))
            keep(10, at, width, dot(s.encoded_t[...], s.dk[0:frames, cols]))
            keep(11, at, width, dot(s.encoded_t[...], s.dv[0:frames, cols]))

    def cross_inputs():
        for name in ("query", "key", "value"):
            waits["cross", name].ready()
        waits["x1"].ready()
        frames = s.encoded_t.shape[1]
        for at, width in strips(D, 256):
            cols = slice(at, at + width)
            s.x3[0:frames, cols] = dot_back(s.dk[0:frames, :], s.weight[2][cols, :]) + dot_back(
                s.dv[0:frames, :], s.weight[3][cols, :]
            )
        state = s.x3.at[pl.ds(0, frames)]
        waits["state"] = Once(pltpu.make_async_copy(state, out.state_grad, s.out_sem.at[1]))
        part, gain_part = center_back(
            dot_back(s.low[...], s.weight[1][...]), s.x1[...], given.gain_cross[...]
        )
        s.gain_sum[0, 1:2, :] = gain_part
        s.g[...] += part
        for place, name in enumerate(Weights._fields):
            if place:
                waits["own", name] = fetch(getattr(given.own_w, name), s.weight[place])

    def self_grads():
        waits["own"]["ht"].ready()
        waits["x"] = fetch(given.x, s.dov)
        s.low[...] = s.dqt[...].T
        for at, width in strips(D, 256):
            cols = slice(at, at + width)
            keep(13, at, width, dot(s.own.ht[...], s.low[:, cols]))
            keep(14, at, width, dot(s.own.ht[...], s.dk[:, cols]))
            keep(15, at, width, dot(s.own.ht[...], s.dv[:, cols]))

    def self_inputs():
        for name in ("query", "key", "value"):
            waits["own", name].ready()
        waits["x"].ready()
        for at, width in strips(D, 256):
            cols = slice(at, at + width)
            s.x1[:, cols] = (
                dot_back(s.low[...], s.weight[1][cols, :])
                + dot_back(s.dk[...], s.weight[2][cols, :])
                + dot_back(s.dv[...], s.weight[3][cols, :])
            )
        part, gain_part = center_back(s.x1[...], s.dov[...].astype(WIDE), given.gain_self[...])
        s.gain_sum[0, 0:1, :] = gain_part
        s.g[...] += part
        waits["input"] = Once(pltpu.make_async_copy(s.g, out.input_grad, s.out_sem.at[2]))

    pieces = (
        [feed(strip) for strip in range(4)]
        + [feed_end, spread(given.cross, s.cross, "cross"), output_grad(s.cross, "cross", 8)]
        + [attention(given.cross, s.cross, "cross", first) for first in (0, 2, 4)]
        + [cross_grads, cross_inputs]
        + [spread(given.own, s.own, "own"), output_grad(s.own, "own", 12)]
        + [attention(given.own, s.own, "own", first) for first in (0, 2, 4)]
        + [self_grads, self_inputs]
    )
    waits["hidden"] = fetch(given.hidden, s.dk)
    fetch_feed(0)
    waits["b3"] = fetch(given.b3, s.low)
    waits["hidden_t"] = fetch(given.hidden_t, s.dot_t)
    waits["x2"] = fetch(given.x2, s.x1)
    fetch_feed(1)
    waits["cross"] = fetch_layer(given.cross, s.cross)
    raised_copy(given.cross, 0).start()
    raised_copy(given.cross, 1).start()
    waits["encoded_t"] = fetch(given.encoded_t, s.encoded_t)
    waits["own"] = fetch_layer(given.own, s.own)
    s.gain_sum[0] = jnp.zeros(s.gain_sum.shape[1:], WIDE)
    met, done, gain_number = False, 0, 0
    for number, code in enumerate(STEPS):
        if code < 1000:
            if not met:
                sums.meet()
                met = True
            sums.step(code % 8, code // 8)
        else:
            pieces[code - 1000]()
            done += 1
        if done == len(pieces) and gain_number < 6 and number % 4 == 0:
            sums.gain_step(gain_number)
            gain_number += 1
    for number in range(gain_number, 6):
        sums.gain_step(number)
    out.gains[...] = s.gain_sum[5]
    result = pltpu.make_async_copy(s.total, out.summed, s.out_sem.at[3])
    result.start()
    sums.finish()
    waits["state"].ready()
    waits["input"].ready()
    result.wait()


def room_for(given):
    rows, frames = given.x.shape[0], given.encoded_t.shape[1]
    split = (2, 2, 2, 2)
    thin = LETTERS.count("B")
    thick = UNITS - thin
    half = D // 2

    def low(*shape):
        return pltpu.VMEM(shape, LOW)

    def wide(*shape):
        return pltpu.VMEM(shape, WIDE)

    def like(array):
        return pltpu.VMEM(array.shape, array.dtype)

    def layer(source):
        return jax.tree.map(like, source)._replace(raised=None)

    plain, turned = (rows, D), (D, rows)
    dma = pltpu.SemaphoreType.DMA
    return Room(
        x1=like(given.x1), encoded_t=like(given.encoded_t),
        cross=layer(given.cross), own=layer(given.own),
        weight=[low(D, D)] * 4, raised=low(2, 2, rows, rows),
        g=wide(*plain), x3=wide(*plain), low=low(*plain), dov=low(*plain), dot_t=low(*turned),
        dqt=low(*turned), dk=low(*plain), dv=low(*plain),
        kept=low(*split, 8, PART, D), narrow=low(*split, 4, PART, D),
        total=wide(UNITS, PART, D), got0=low(UNITS, 2, 2, 2, PART, D),
        a1=low(thick, 2, 2, PART, D), a2=low(thick, 2, PART, D), a3=low(thick, PART, D),
        a4=low(thick, PART, D), b1=low(thin, 2, 2, 2, PART, half), b2=low(thin, 2, 2, PART, half),
        b3=low(thin, 2, PART, half), b4=low(thin, PART, half), b5=low(thin, PART, half),
        gain_sum=wide(6, 8, D), gain_got=wide(5, 8, D),
        fetch_sem=dma((40,)), raised_sem=dma((2,)), out_sem=dma((4,)),
        send_sem=dma((6, UNITS)), recv_sem=dma((6, UNITS)), gain_send=dma((5,)),
        gain_recv=dma((5,)),
    )


def backward_and_sum(given):
    rows, frames = given.x.shape[0], given.encoded_t.shape[1]
    outs = BackOut(
        output=shape_of((rows, D)), input_grad=shape_of((rows, D), WIDE),
        state_grad=shape_of((frames, D), WIDE), summed=shape_of((UNITS, PART, D), WIDE),
        gains=shape_of((8, D), WIDE),
    )
    room = room_for(given)
    places = jax.tree.map(lambda _: FAR, given)._replace(
        length=NUMBERS, gain_mlp=INSIDE, gain_cross=INSIDE, gain_self=INSIDE
    )
    results = pl.pallas_call(
        functools.partial(back_kernel, jax.tree.structure((given, outs, room))),
        out_shape=tuple(outs),
        in_specs=jax.tree.leaves(places),
        out_specs=(FAR,) * 4 + (INSIDE,),
        scratch_shapes=jax.tree.leaves(room),
        compiler_params=pltpu.CompilerParams(
            collective_id=0, has_side_effects=True, vmem_limit_bytes=63 * 2**20
        ),
    )(*jax.tree.leaves(given))
    return BackOut(*results)


def finish_kernel(output, input_grad, state_grad, summed, *refs):
    outs, (rows_low, rows_wide, frames_wide, blocks, taken, given) = refs[:13], refs[13:]
    parts = [
        (summed.at[pl.ds(0, 8)], blocks.at[pl.ds(0, 8)]),
        (summed.at[pl.ds(8, 8)], blocks.at[pl.ds(8, 8)]),
        (input_grad, rows_wide),
        (state_grad, frames_wide),
        (output, rows_low),
    ]
    results = [
        [(blocks.at[unit], outs[3 + unit]) for unit in range(8)],
        [(blocks.at[pl.ds(12, 4)], outs[12])]
        + [(blocks.at[8 + k], outs[11].at[:, pl.ds(k * D, D)]) for k in range(4)],
        [(rows_wide, outs[1])],
        [(frames_wide, outs[2])],
        [(rows_low, outs[0])],
    ]
    arriving = [
        pltpu.make_async_copy(*pair, taken.at[place]) for place, pair in enumerate(parts)
    ]
    for copy in arriving:
        copy.start()
    leaving = []
    for copy, pairs in zip(arriving, results):
        copy.wait()
        for pair in pairs:
            leaving.append(pltpu.make_async_copy(*pair, given.at[len(leaving)]))
            leaving[-1].start()
    for copy in leaving:
        copy.wait()


def finish(made):
    outs = [shape_of(made[k].shape, made[k].dtype) for k in range(3)]
    outs += [shape_of((PART, D), WIDE)] * 8
    outs += [shape_of((PART, 4 * D), WIDE), shape_of((4, PART, D), WIDE)]
    *results, narrow = pl.pallas_call(
        finish_kernel,
        out_shape=tuple(outs),
        in_specs=[FAR] * 4,
        out_specs=(FAR,) * len(outs),
        scratch_shapes=[pltpu.VMEM(array.shape, array.dtype) for array in made[:4]]
        + [pltpu.SemaphoreType.DMA((5,)), pltpu.SemaphoreType.DMA((16,))],
        compiler_params=parameters(62),
    )(*made[:4])
    return *results, narrow.reshape(4 * PART, D)


def body(
    members,
    groups,
    mel_frames,
    conv_first,
    conv_second,
    enc_projection,
    enc_output,
    enc_expand,
    enc_narrow,
    dec_input,
    lengths,
    self_query,
    self_key,
    self_value,
    self_output,
    cross_query,
    cross_key,
    cross_value,
    cross_output,
    mlp_expand,
    mlp_narrow,
    gain_self,
    gain_cross,
    gain_mlp,
    cotangent,
):
    arrived = lax.all_to_all(mel_frames, "tm", split_axis=2, concat_axis=0, tiled=True)
    inputs, length = dec_input[0, 0], lengths[0]
    own_w = Weights(self_output, self_query, self_key, self_value)
    x1, own = self_forward(length, inputs, gain_self, own_w)
    encoded, encoded_t = encode(
        arrived[:, 0, 0], conv_first, conv_second, enc_projection, enc_output, enc_expand, enc_narrow
    )
    cross_w = Weights(cross_output, cross_query, cross_key, cross_value)
    x2, hidden, hidden_t, b3, cross = cross_forward(
        length, x1, encoded, cotangent[0, 0], gain_cross, gain_mlp, cross_w
    )
    if (members, groups) == (16, 2):
        made = backward_and_sum(
            BackIn(
                length, x2, hidden, hidden_t, b3, x1, inputs, encoded_t,
                gain_mlp, gain_cross, gain_self, mlp_expand, mlp_narrow,
                cross, own, cross_w, own_w,
            )
        )
        dec_output, dec_input_grad, enc_state_grad, *totals = finish(made)
        gains = made.gains
    else:
        dec_output, g2, g_gain_mlp, g_expand, g_narrow = feed_both(
            length, x2, hidden, hidden_t, b3, gain_mlp, mlp_expand, mlp_narrow
        )
        g1, g_gain_cross, enc_state_grad, *cross_grads = cross_backward(
            (g2, x1, gain_cross) + tuple(cross) + (encoded_t,), cross_w
        )
        dec_input_grad, g_gain_self, *self_grads = self_backward(
            (g1, inputs, gain_self) + tuple(own), own_w
        )
        gains = jnp.concatenate([g_gain_self, g_gain_cross, g_gain_mlp, jnp.zeros((5, D), WIDE)])
        totals, gains = sum_plain(
            self_grads + cross_grads + [g_expand, g_narrow], gains, members, groups
        )
    part = D // members
    gains = lax.dynamic_slice_in_dim(gains, lax.axis_index("tm") * part, part, 1)
    return (
        encoded[None, None],
        dec_output[None, None],
        dec_input_grad[None, None],
        enc_state_grad[None, None],
        *totals,
        gains[0],
        gains[1],
        gains[2],
    )


def solution(mesh):
    placed = (
        P("tm", "clip", None, None),
        P(),
        P(),
        P(),
        P(),
        P(),
        P(),
        P("clip", "tm", None, None),
        P("clip", "tm"),
        P(),
        P(),
        P(),
        P(),
        P(),
        P(),
        P(),
        P(),
        P(),
        P(),
        P(),
        P(),
        P(),
        P("clip", "tm", None, None),
    )
    return jax.shard_map(
        functools.partial(body, mesh.shape["tm"], mesh.shape["clip"]),
        mesh=mesh,
        in_specs=placed,
        out_specs=(
            P("clip", "tm", None, None),
            P("clip", "tm", None, None),
            P("clip", "tm", None, None),
            P("clip", "tm", None, None),
            P("tm", None),
            P("tm", None),
            P("tm", None),
            P("tm", None),
            P("tm", None),
            P("tm", None),
            P("tm", None),
            P("tm", None),
            P("tm", None),
            P("tm", None),
            P("tm"),
            P("tm"),
            P("tm"),
        ),
        check_vma=False,
    )
```

```python
import functools
import math
from typing import Any, NamedTuple

import jax
import jax.numpy as jnp
import numpy as np
from jax import lax
from jax.experimental import pallas as pl
from jax.experimental.pallas import tpu as pltpu
from jax.sharding import PartitionSpec as P

D = 768
HEADS = 12
HD = 64
PAIRS = HEADS // 2
LANES = 2 * HD
SCALE = HD ** (-0.5)
LOW = jnp.bfloat16
WIDE = jnp.float32
INSIDE = pl.BlockSpec(memory_space=pltpu.VMEM)
FAR = pl.BlockSpec(memory_space=pltpu.HBM)
MESH = pl.DeviceIdType.MESH
NUMBERS = pl.BlockSpec(memory_space=pltpu.SMEM)


def shape_of(shape, kind=LOW):
    return jax.ShapeDtypeStruct(shape, kind)


def parameters(megabytes=58):
    return pltpu.CompilerParams(vmem_limit_bytes=megabytes * 2**20)


def center(values):
    shifted = values - jnp.mean(values, axis=-1, keepdims=True)
    spread = jnp.mean(shifted * shifted, axis=-1, keepdims=True)
    root = lax.rsqrt(spread + 1e-05)
    return shifted * root, root


def center_back(gradient, values, gain):
    normed, root = center(values)
    inner = gradient * gain
    first = jnp.mean(inner, axis=-1, keepdims=True)
    second = jnp.mean(inner * normed, axis=-1, keepdims=True)
    gain_part = jnp.sum(gradient * normed, axis=0, keepdims=True)
    return root * (inner - first - normed * second), gain_part


def gelu(values):
    return values * (0.5 + 0.5 * lax.erf(values * 2**-0.5))


def gelu_both(values):
    area = 0.5 + 0.5 * lax.erf(values * 2**-0.5)
    slope = area + values * ((2 * math.pi) ** -0.5 * jnp.exp(-0.5 * values * values))
    return values * area, slope


def dot(left, right):
    return jnp.dot(left, right, preferred_element_type=WIDE)


def dot_back(left, right):
    return lax.dot_general(left, right, (((1,), (1,)), ((), ())), preferred_element_type=WIDE)


def dot_rows(left, right):
    return lax.dot_general(left, right, (((0,), (0,)), ((), ())), preferred_element_type=WIDE)


def strips(total, width):
    return [(at, min(width, total - at)) for at in range(0, total, width)]


class Fetch:
    def __init__(self, sources, targets, semaphores):
        self.copies = [
            pltpu.make_async_copy(source, target, semaphores.at[place])
            for place, (source, target) in enumerate(zip(sources, targets))
        ]
        for copy in self.copies:
            copy.start()

    def wait(self, place):
        self.copies[place].wait()


def pair_lanes(pair):
    return pl.ds(pl.multiple_of(pair * LANES, LANES), LANES)


def head_rows(pair, side):
    return pl.ds(pl.multiple_of(pair * LANES + side * HD, HD), HD)


def attend(q_ref, k_ref, vt_ref, bias_ref, ot_ref, inverse_ref=None, raised_ref=None, leave=None):
    ones = jnp.ones((16, vt_ref.shape[1]), LOW)

    @pl.loop(0, PAIRS)
    def _(pair):
        queries, keys = q_ref[:, pair_lanes(pair)], k_ref[:, pair_lanes(pair)]
        for side in range(2):
            cut = slice(side * HD, (side + 1) * HD)
            scores = dot_back(keys[:, cut], queries[:, cut])
            if bias_ref is not None:
                scores = scores + bias_ref[...]
            raised = jnp.exp(scores - jnp.max(scores, axis=0, keepdims=True)).astype(LOW)
            rows = head_rows(pair, side)
            mixed = dot(jnp.concatenate([vt_ref[rows, :], ones], axis=0), raised)
            inverse = 1.0 / mixed[HD : HD + 1]
            ot_ref[rows, :] = mixed[:HD] * inverse
            if raised_ref is not None:
                raised_ref[2 * pair + side] = raised
                inverse_ref[2 * pair + side] = jnp.broadcast_to(inverse, inverse_ref.shape[1:])
        if leave is not None:
            leave(pair)


def attend_pair(
    pair, q_ref, kt_ref, v_ref, raised_ref, delta_ref, dot_ref, dov_ref, dqt_ref, dk_ref, dv_ref
):
    lanes = pair_lanes(pair)
    queries, values, grads = q_ref[:, lanes], v_ref[:, lanes], dov_ref[:, lanes]
    key_sides, value_sides = [], []
    for side in range(2):
        rows = head_rows(pair, side)
        cut = slice(side * HD, (side + 1) * HD)
        raised = raised_ref[side]
        products = dot(values[:, cut], dot_ref[rows, :]) - delta_ref[2 * pair + side, 0:1, :]
        score_grad = (raised.astype(WIDE) * products).astype(LOW)
        dqt_ref[rows, :] = (dot(kt_ref[rows, :], score_grad) * SCALE).astype(LOW)
        key_sides.append(dot(score_grad, queries[:, cut]))
        value_sides.append(dot(raised, grads[:, cut]))
    dk_ref[:, lanes] = jnp.concatenate(key_sides, axis=1).astype(LOW)
    dv_ref[:, lanes] = jnp.concatenate(value_sides, axis=1).astype(LOW)


def attend_back(q_ref, kt_ref, v_ref, raised_ref, *rest):
    @pl.loop(0, PAIRS)
    def _(pair):
        attend_pair(pair, q_ref, kt_ref, v_ref, raised_ref.at[pl.ds(2 * pair, 2)], *rest)


def encoder_kernel(
    mel_ref, position_ref, first_h, second_h, joint_h, output_h, expand_h, narrow_h,
    out_ref, out_t_ref,
    first_w, second_w, joint_w, output_w, expand_w, narrow_w,
    even, odd, state, hidden, q, k, vt, mixed_t, semaphores,
):
    length = out_ref.shape[0]
    fetch = Fetch(
        (first_h, second_h, joint_h, output_h, expand_h, narrow_h),
        (first_w, second_w, joint_w, output_w, expand_w, narrow_w),
        semaphores,
    )
    taps = [mel_ref[pl.ds(7 + tap, length, stride=2), :].astype(LOW) for tap in range(4)]
    fetch.wait(0)
    for at, width in strips(D, 256):
        cols = pl.ds(at, width)
        for start, target in ((0, even), (1, odd)):
            total = sum(dot(taps[start + o], first_w[o, :, cols]) for o in range(3))
            target[:, cols] = gelu(total).astype(LOW)
    fetch.wait(1)
    ranks = lax.broadcasted_iota(jnp.int32, (length, 256), 0)
    for at, width in strips(D, 256):
        cols = pl.ds(at, width)
        before = pltpu.roll(dot(odd[...], second_w[0, :, cols]), 1, 0)
        total = dot(even[...], second_w[1, :, cols]) + dot(odd[...], second_w[2, :, cols])
        total = total + jnp.where(ranks == 0, 0.0, before)
        state[:, cols] = gelu(total) + position_ref[:, cols]
    hidden[...] = center(state[...])[0].astype(LOW)
    fetch.wait(2)
    for at, width in strips(D, 256):
        cols = pl.ds(at, width)
        q[:, cols] = (dot(hidden[...], joint_w[:, cols]).astype(LOW) * SCALE).astype(LOW)
        k[:, cols] = dot(hidden[...], joint_w[:, pl.ds(D + at, width)]).astype(LOW)
        vt[cols, :] = dot(hidden[...], joint_w[:, pl.ds(2 * D + at, width)]).astype(LOW).T
    attend(q, k, vt, None, mixed_t)
    fetch.wait(3)
    mixed = mixed_t[...].astype(LOW).T
    for at, width in strips(D, 256):
        cols = pl.ds(at, width)
        state[:, cols] += dot(mixed, output_w[:, cols])
    hidden[...] = center(state[...])[0].astype(LOW)
    fetch.wait(4)
    fetch.wait(5)

    @pl.loop(0, expand_w.shape[1] // 512)
    def _(strip):
        cols = pl.ds(pl.multiple_of(strip * 512, 512), 512)
        widened = gelu(dot(hidden[...], expand_w[:, cols])).astype(LOW)
        state[...] += dot(widened, narrow_w[cols, :])

    encoded = center(state[...])[0].astype(LOW)
    out_ref[...] = encoded
    out_t_ref[...] = encoded.T


def encode(mel, conv_first, conv_second, enc_projection, enc_output, enc_expand, enc_narrow):
    length = (mel.shape[0] - 16) // 2
    weights = (conv_first, conv_second, enc_projection, enc_output, enc_expand, enc_narrow)
    return pl.pallas_call(
        encoder_kernel,
        out_shape=(shape_of((length, D)), shape_of((D, length))),
        in_specs=[INSIDE] * 2 + [FAR] * 6,
        out_specs=(INSIDE, INSIDE),
        scratch_shapes=[pltpu.VMEM(weight.shape, LOW) for weight in weights]
        + [
            pltpu.VMEM((length, D), LOW),
            pltpu.VMEM((length, D), LOW),
            pltpu.VMEM((length, D), WIDE),
            pltpu.VMEM((length, D), LOW),
            pltpu.VMEM((length, D), LOW),
            pltpu.VMEM((length, D), LOW),
            pltpu.VMEM((D, length), LOW),
            pltpu.VMEM((D, length), WIDE),
            pltpu.SemaphoreType.DMA((6,)),
        ],
        compiler_params=parameters(),
    )(mel, sinusoids(length, D), *weights)


def sinusoids(length, features):
    halfway = features // 2
    inverse = np.exp(-math.log(10000.0) / (halfway - 1) * np.arange(halfway)).astype(np.float32)
    angles = np.arange(length, dtype=np.float32)[:, None] * inverse[None, :]
    angles = angles.astype(np.float64)
    return jnp.asarray(np.concatenate([np.sin(angles), np.cos(angles)], axis=1).astype(np.float32))


class Layer(NamedTuple):
    ht: Any
    q: Any
    kt: Any
    v: Any
    raised: Any
    inverse: Any
    ot: Any


class Weights(NamedTuple):
    output: Any
    query: Any
    key: Any
    value: Any


class Leave:
    def __init__(self, held, targets, semaphores):
        self.pairs, self.semaphores, self.started = list(zip(held, targets)), semaphores, []

    def __call__(self, *places):
        for place in places:
            copy = pltpu.make_async_copy(*self.pairs[place], self.semaphores.at[place])
            copy.start()
            self.started.append(copy)

    def scores(self, place, first):
        def copy(pair):
            held, target = self.pairs[place]
            heads = pl.ds(2 * pair, 2)
            return pltpu.make_async_copy(
                held.at[heads], target.at[heads], self.semaphores.at[first + pair]
            )

        self.started += [copy(pair) for pair in range(PAIRS)]
        return lambda pair: copy(pair).start()

    def finish(self):
        for copy in self.started:
            copy.wait()


def self_kernel(
    members, length_ref, x_ref, gain_ref, mel_h, output_h, query_h, key_h, value_h, *refs
):
    outs, held = refs[:9], refs[9:18]
    output_w, query_w, key_w, value_w, hidden, k, vt, bias = refs[18:26]
    semaphores, out_sem, own_sem, send_sem, recv_sem = refs[26:]
    x1, ht, q, kt, v, raised, inverse, ot, mel = held
    leave = Leave(held, outs, out_sem)
    tm, clip = lax.axis_index("tm"), lax.axis_index("clip")
    barrier = pltpu.get_barrier_semaphore()

    @pl.loop(1, members)
    def _(step):
        peer = (lax.rem(tm + step, members), clip)
        pl.semaphore_signal(barrier, inc=1, device_id=peer, device_id_type=MESH)

    fetch = Fetch(
        (query_h, key_h, value_h, output_h), (query_w, key_w, value_w, output_w), semaphores
    )
    rows = x_ref.shape[0]
    hidden[...] = (center(x_ref[...].astype(WIDE))[0] * gain_ref[...]).astype(LOW)
    keys = lax.broadcasted_iota(jnp.int32, (rows, rows), 0)
    queries = lax.broadcasted_iota(jnp.int32, (rows, rows), 1)
    allowed = (keys <= queries) & (keys < length_ref[0])
    bias[...] = jnp.where(allowed, 0.0, -1e30)
    fetch.wait(0)
    fetch.wait(1)
    fetch.wait(2)
    for at, width in strips(D, 256):
        cols = pl.ds(at, width)
        q[:, cols] = (dot(hidden[...], query_w[:, cols]).astype(LOW) * SCALE).astype(LOW)
        part = dot(hidden[...], key_w[:, cols]).astype(LOW)
        k[:, cols] = part
        kt[cols, :] = part.T
        part = dot(hidden[...], value_w[:, cols]).astype(LOW)
        v[:, cols] = part
        vt[cols, :] = part.T
    ht[...] = hidden[...].T
    leave(1, 2, 3, 4)
    pl.semaphore_wait(barrier, members - 1)
    frames = mel_h.shape[1]
    place = pl.ds(pl.multiple_of(8 + tm * frames, 8), frames)

    def pass_on(step):
        peer = lax.rem(tm + step, members)
        return pltpu.make_async_remote_copy(
            src_ref=mel_h.at[peer],
            dst_ref=mel.at[place],
            send_sem=send_sem.at[step],
            recv_sem=recv_sem.at[step],
            device_id=(peer, clip),
            device_id_type=MESH,
        )

    @pl.loop(1, members)
    def _(step):
        pass_on(step).start()

    stay = pltpu.make_async_copy(mel_h.at[tm], mel.at[place], own_sem)
    stay.start()
    mel[0:8, :] = jnp.zeros((8, mel.shape[1]), WIDE)
    mel[mel.shape[0] - 8 :, :] = jnp.zeros((8, mel.shape[1]), WIDE)
    attend(q, k, vt, bias, ot, inverse, raised, leave.scores(5, 9))
    leave(6, 7)
    fetch.wait(3)
    mixed = ot[...].astype(LOW).T
    for at, width in strips(D, 256):
        cols = pl.ds(at, width)
        x1[:, cols] = x_ref[:, cols].astype(WIDE) + dot(mixed, output_w[:, cols])
    leave(0)

    @pl.loop(1, members)
    def _(step):
        pass_on(step).wait()

    stay.wait()
    leave(8)
    leave.finish()


def held_like(shapes):
    return [pltpu.VMEM(shape.shape, shape.dtype) for shape in shapes]


def self_forward(lengths, inputs, gain, mel_frames, members, weights):
    rows = inputs.shape[0]
    mel = jnp.transpose(mel_frames.astype(WIDE), (1, 0, 2))
    arrived = (members * mel.shape[1] + 16, mel.shape[2])
    plain, turned = (rows, D), (D, rows)
    outs = (
        shape_of(plain, WIDE), shape_of(turned), shape_of(plain), shape_of(turned),
        shape_of(plain), shape_of((HEADS, rows, rows)), shape_of((HEADS, 8, rows), WIDE),
        shape_of(turned, WIDE), shape_of(arrived, WIDE),
    )
    x1, *layer, arrived = pl.pallas_call(
        functools.partial(self_kernel, members),
        out_shape=outs,
        in_specs=[NUMBERS, INSIDE, INSIDE] + [FAR] * 5,
        out_specs=(FAR,) * 9,
        scratch_shapes=held_like(outs)
        + [pltpu.VMEM((D, D), LOW)] * 4
        + [
            pltpu.VMEM(plain, LOW),
            pltpu.VMEM(plain, LOW),
            pltpu.VMEM(turned, LOW),
            pltpu.VMEM((rows, rows), WIDE),
            pltpu.SemaphoreType.DMA((4,)),
            pltpu.SemaphoreType.DMA((9 + PAIRS,)),
            pltpu.SemaphoreType.DMA(()),
            pltpu.SemaphoreType.DMA((members,)),
            pltpu.SemaphoreType.DMA((members,)),
        ],
        compiler_params=pltpu.CompilerParams(
            collective_id=1, has_side_effects=True, vmem_limit_bytes=58 * 2**20
        ),
    )(lengths, inputs, gain, mel, *weights)
    return x1, Layer(*layer), arrived


def cross_kernel(
    length_ref, x1_ref, encoded_ref, cotangent_ref, gain_cross_ref, gain_mlp_ref,
    output_h, query_h, key_h, value_h, *refs
):
    outs, held = refs[:11], refs[11:22]
    output_w, query_w, key_w, value_w, k, vt, semaphores, out_sem = refs[22:]
    x2, hidden, hidden_t, b3, ht, q, kt, v, raised, inverse, ot = held
    leave = Leave(held, outs, out_sem)
    fetch = Fetch(
        (query_h, key_h, value_h, output_h), (query_w, key_w, value_w, output_w), semaphores
    )
    rows = x1_ref.shape[0]
    hidden[...] = (center(x1_ref[...])[0] * gain_cross_ref[...]).astype(LOW)
    fetch.wait(0)
    fetch.wait(1)
    fetch.wait(2)
    for at, width in strips(D, 256):
        cols = pl.ds(at, width)
        q[:, cols] = (dot(hidden[...], query_w[:, cols]).astype(LOW) * SCALE).astype(LOW)
        part = dot(encoded_ref[...], key_w[:, cols]).astype(LOW)
        k[:, cols] = part
        kt[cols, :] = part.T
        part = dot(encoded_ref[...], value_w[:, cols]).astype(LOW)
        v[:, cols] = part
        vt[cols, :] = part.T
    ht[...] = hidden[...].T
    live = lax.broadcasted_iota(jnp.int32, (rows, D), 0) < length_ref[0]
    b3[...] = jnp.where(live, cotangent_ref[...].astype(WIDE), 0.0).astype(LOW)
    leave(3, 4, 5, 6, 7)
    attend(q, k, vt, None, ot, inverse, raised, leave.scores(8, 11))
    leave(9, 10)
    fetch.wait(3)
    mixed = ot[...].astype(LOW).T
    for at, width in strips(D, 256):
        cols = pl.ds(at, width)
        x2[:, cols] = x1_ref[:, cols] + dot(mixed, output_w[:, cols])
    leave(0)
    hidden[...] = (center(x2[...])[0] * gain_mlp_ref[...]).astype(LOW)
    leave(1)
    hidden_t[...] = hidden[...].T
    leave(2)
    leave.finish()


def cross_forward(lengths, x1, encoded, cotangent, gain_cross, gain_mlp, weights):
    rows, frames = x1.shape[0], encoded.shape[0]
    plain, turned = (rows, D), (D, rows)
    outs = (
        shape_of(plain, WIDE), shape_of(plain), shape_of(turned), shape_of(plain),
        shape_of(turned), shape_of(plain), shape_of((D, frames)), shape_of((frames, D)),
        shape_of((HEADS, frames, rows)), shape_of((HEADS, 8, rows), WIDE),
        shape_of(turned, WIDE),
    )
    x2, hidden, hidden_t, b3, *layer = pl.pallas_call(
        cross_kernel,
        out_shape=outs,
        in_specs=[NUMBERS] + [INSIDE] * 5 + [FAR] * 4,
        out_specs=(FAR,) * 11,
        scratch_shapes=held_like(outs)
        + [pltpu.VMEM(weight.shape, LOW) for weight in weights]
        + [
            pltpu.VMEM((frames, D), LOW),
            pltpu.VMEM((D, frames), LOW),
            pltpu.SemaphoreType.DMA((4,)),
            pltpu.SemaphoreType.DMA((11 + PAIRS,)),
        ],
        compiler_params=parameters(),
    )(lengths, x1, encoded, cotangent, gain_cross, gain_mlp, *weights)
    return x2, hidden, hidden_t, b3, Layer(*layer)


def feed_kernel(
    length_ref, x2_ref, hidden, hidden_t, b3, gain_ref, expand_h, narrow_h,
    out_ref, g2_ref, gain_grad_ref, expand_grad_ref, narrow_grad_ref,
    expand_w, narrow_w, x3, back, semaphores,
):
    fetch = Fetch((expand_h, narrow_h), (expand_w, narrow_w), semaphores)
    x3[...] = x2_ref[...]
    back[...] = jnp.zeros_like(back)
    fetch.wait(0)
    fetch.wait(1)

    @pl.loop(0, expand_w.shape[1] // 512)
    def _(strip):
        cols = pl.ds(pl.multiple_of(strip * 512, 512), 512)
        active, slope = gelu_both(dot(hidden[...], expand_w[:, cols]))
        active = active.astype(LOW)
        grad = (slope * dot_back(b3[...], narrow_w[cols, :])).astype(LOW)
        x3[...] += dot(active, narrow_w[cols, :])
        narrow_grad_ref[cols, :] = dot_rows(active, b3[...]).astype(LOW)
        expand_grad_ref[:, cols] = dot(hidden_t[...], grad).astype(LOW)
        back[...] += dot_back(grad, expand_w[:, cols])

    live = lax.broadcasted_iota(jnp.int32, x3.shape, 0) < length_ref[0]
    out_ref[...] = jnp.where(live, x3[...], 0.0).astype(LOW)
    part, gain_part = center_back(back[...], x2_ref[...], gain_ref[...])
    gain_grad_ref[...] = gain_part
    g2_ref[...] = b3[...].astype(WIDE) + part


def feed_both(lengths, x2, hidden, hidden_t, b3, gain_mlp, expand, narrow):
    plain = x2.shape
    return pl.pallas_call(
        feed_kernel,
        out_shape=(
            shape_of(plain), shape_of(plain, WIDE), shape_of((1, D), WIDE),
            shape_of(expand.shape), shape_of(narrow.shape),
        ),
        in_specs=[NUMBERS] + [INSIDE] * 5 + [FAR] * 2,
        out_specs=(INSIDE,) * 5,
        scratch_shapes=[
            pltpu.VMEM(expand.shape, LOW),
            pltpu.VMEM(narrow.shape, LOW),
            pltpu.VMEM(plain, WIDE),
            pltpu.VMEM(plain, WIDE),
            pltpu.SemaphoreType.DMA((2,)),
        ],
        compiler_params=parameters(),
    )(lengths, x2, hidden, hidden_t, b3, gain_mlp, expand, narrow)


def spread_grads(out_grad, output_w, inverse_ref, ot_ref, delta_ref, dov, dot_t):
    for at, width in strips(D, 256):
        part = dot_back(out_grad, output_w[at : at + width, :]).astype(LOW).T
        sides = []
        for number in range(width // HD):
            head = at // HD + number
            side = part[number * HD : (number + 1) * HD, :].astype(WIDE)
            side = (side * inverse_ref[head, 0:1, :]).astype(LOW)
            mixed = ot_ref[head * HD : (head + 1) * HD, :]
            delta = jnp.sum(mixed * side.astype(WIDE), axis=0, keepdims=True)
            delta_ref[head] = jnp.broadcast_to(delta, delta_ref.shape[1:])
            sides.append(side)
        part = jnp.concatenate(sides, axis=0)
        dot_t[at : at + width, :] = part
        dov[:, at : at + width] = part.T


def cross_back_kernel(
    g2_ref, x1_ref, gain_ref, ht_ref, q_ref, kt_ref, v_ref, raised_ref, inverse_ref, ot_ref,
    encoded_t_ref, output_h, query_h, key_h, value_h,
    g1_ref, gain_grad_ref, state_grad_ref, query_g, key_g, value_g, output_g,
    output_w, query_w, key_w, value_w, dov, dot_t, dqt, dk, dv, delta, semaphores,
):
    fetch = Fetch(
        (output_h, query_h, key_h, value_h), (output_w, query_w, key_w, value_w), semaphores
    )
    b2 = g2_ref[...].astype(LOW)
    fetch.wait(0)
    spread_grads(b2, output_w, inverse_ref, ot_ref, delta, dov, dot_t)
    mixed = ot_ref[...].astype(LOW)
    for at, width in strips(D, 256):
        output_g[:, at : at + width] = dot(mixed, b2[:, at : at + width]).astype(LOW)
    attend_back(q_ref, kt_ref, v_ref, raised_ref, delta, dot_t, dov, dqt, dk, dv)
    dq = dqt[...].T
    for place in range(1, 4):
        fetch.wait(place)
    for at, width in strips(D, 256):
        cols = slice(at, at + width)
        query_g[:, cols] = dot(ht_ref[...], dq[:, cols]).astype(LOW)
        key_g[:, cols] = dot(encoded_t_ref[...], dk[:, cols]).astype(LOW)
        value_g[:, cols] = dot(encoded_t_ref[...], dv[:, cols]).astype(LOW)
        state_grad_ref[:, cols] = dot_back(dk[...], key_w[cols, :]) + dot_back(
            dv[...], value_w[cols, :]
        )
    part, gain_part = center_back(dot_back(dq, query_w[...]), x1_ref[...], gain_ref[...])
    gain_grad_ref[...] = gain_part
    g1_ref[...] = g2_ref[...] + part


def cross_backward(operands, weights):
    rows, frames = operands[0].shape[0], operands[10].shape[1]
    plain, turned, square = (rows, D), (D, rows), shape_of((D, D))
    return pl.pallas_call(
        cross_back_kernel,
        out_shape=(
            shape_of(plain, WIDE), shape_of((1, D), WIDE), shape_of((frames, D), WIDE),
            square, square, square, square,
        ),
        in_specs=[INSIDE] * 11 + [FAR] * 4,
        out_specs=(INSIDE,) * 7,
        scratch_shapes=[pltpu.VMEM((D, D), LOW)] * 4
        + [
            pltpu.VMEM(plain, LOW),
            pltpu.VMEM(turned, LOW),
            pltpu.VMEM(turned, LOW),
            pltpu.VMEM((frames, D), LOW),
            pltpu.VMEM((frames, D), LOW),
            pltpu.VMEM((HEADS, 8, rows), WIDE),
            pltpu.SemaphoreType.DMA((4,)),
        ],
        compiler_params=parameters(),
    )(*operands, *weights)


def self_back_kernel(
    g1_ref, x_ref, gain_ref, ht_ref, q_ref, kt_ref, v_ref, raised_ref, inverse_ref, ot_ref,
    output_h, query_h, key_h, value_h,
    input_grad_ref, gain_grad_ref, query_g, key_g, value_g, output_g,
    output_w, query_w, key_w, value_w, dov, dot_t, dqt, dk, dv, delta, semaphores,
):
    fetch = Fetch(
        (output_h, query_h, key_h, value_h), (output_w, query_w, key_w, value_w), semaphores
    )
    b1 = g1_ref[...].astype(LOW)
    fetch.wait(0)
    spread_grads(b1, output_w, inverse_ref, ot_ref, delta, dov, dot_t)
    mixed = ot_ref[...].astype(LOW)
    for at, width in strips(D, 256):
        output_g[:, at : at + width] = dot(mixed, b1[:, at : at + width]).astype(LOW)
    attend_back(q_ref, kt_ref, v_ref, raised_ref, delta, dot_t, dov, dqt, dk, dv)
    dq = dqt[...].T
    for place in range(1, 4):
        fetch.wait(place)
    for at, width in strips(D, 256):
        cols = slice(at, at + width)
        query_g[:, cols] = dot(ht_ref[...], dq[:, cols]).astype(LOW)
        key_g[:, cols] = dot(ht_ref[...], dk[:, cols]).astype(LOW)
        value_g[:, cols] = dot(ht_ref[...], dv[:, cols]).astype(LOW)
        input_grad_ref[:, cols] = (
            dot_back(dq, query_w[cols, :])
            + dot_back(dk[...], key_w[cols, :])
            + dot_back(dv[...], value_w[cols, :])
        )
    part, gain_part = center_back(
        input_grad_ref[...], x_ref[...].astype(WIDE), gain_ref[...]
    )
    gain_grad_ref[...] = gain_part
    input_grad_ref[...] = g1_ref[...] + part


def self_backward(operands, weights):
    rows = operands[0].shape[0]
    plain, turned, square = (rows, D), (D, rows), shape_of((D, D))
    return pl.pallas_call(
        self_back_kernel,
        out_shape=(shape_of(plain, WIDE), shape_of((1, D), WIDE), square, square, square, square),
        in_specs=[INSIDE] * 10 + [FAR] * 4,
        out_specs=(INSIDE,) * 6,
        scratch_shapes=[pltpu.VMEM((D, D), LOW)] * 4
        + [
            pltpu.VMEM(plain, LOW),
            pltpu.VMEM(turned, LOW),
            pltpu.VMEM(turned, LOW),
            pltpu.VMEM(plain, LOW),
            pltpu.VMEM(plain, LOW),
            pltpu.VMEM((HEADS, 8, rows), WIDE),
            pltpu.SemaphoreType.DMA((4,)),
        ],
        compiler_params=parameters(),
    )(*operands, *weights)


def trade(values, axis, size, bit):
    return lax.ppermute(values, axis, [(i, i ^ bit) for i in range(size)])


def add_rounded(left, right):
    return (left.astype(jnp.float32) + right.astype(jnp.float32)).astype(jnp.bfloat16)


def halve(values, dim, axis, size, bit):
    mine = (lax.axis_index(axis) // bit) % 2
    kept = lax.dynamic_index_in_dim(values, mine, dim, keepdims=False)
    sent = lax.dynamic_index_in_dim(values, 1 - mine, dim, keepdims=False)
    return add_rounded(kept, trade(sent, axis, size, bit))


def bits_of(size):
    return [1 << k for k in range(size.bit_length() - 1)]


def members_first(values, members, groups):
    for bit in bits_of(members):
        values = halve(values, len(values.shape) - 3, "tm", members, bit)
    for bit in bits_of(groups):
        values = add_rounded(values, trade(values, "clip", groups, bit))
    return values.astype(jnp.float32)


def groups_first(values, members, groups):
    values = halve(values, len(values.shape) - 3, "tm", members, 1)
    lead = values.shape[:-2]
    rows, columns = values.shape[-2:]
    for bit in bits_of(groups):
        values = values.reshape(lead + (2, values.shape[-2] // 2, columns))
        values = halve(values, len(lead), "clip", groups, bit)
    for bit in bits_of(members)[1:]:
        values = halve(values, len(values.shape) - 3, "tm", members, bit)
    for bit in bits_of(groups)[::-1]:
        mine = (lax.axis_index("clip") // bit) % 2
        other = trade(values, "clip", groups, bit)
        values = jnp.where(
            mine == 0, jnp.concatenate([values, other]), jnp.concatenate([other, values])
        )
    return values.astype(jnp.float32)


def sum_plain(matrices, gains, members, groups):
    split = (2,) * (members.bit_length() - 1)
    totals = []
    for place, matrix in enumerate(matrices):
        blocks = matrix.reshape(split + (matrix.shape[0] // members, matrix.shape[1]))
        totals.append((members_first, groups_first)[place % 2](blocks, members, groups))
    return tuple(totals), lax.psum(gains, ("tm", "clip"))


PART = 48
UNITS = 16
UNIT_ORDER = (8, 9, 10, 11, 12, 13, 14, 15, 7, 4, 5, 6, 3, 0, 1, 2)
LETTERS = "ABBBCABCAABBABBB"
STEPS = (
    1000, 1001, 0, 1002, 1003, 1, 8, 1004, 1005, 16, 9, 1006, 1007, 17, 56, 32,
    2, 40, 1008, 24, 1009, 57, 10, 33, 48, 1010, 64, 3, 41, 1011, 25, 49,
    65, 11, 1012, 72, 18, 1013, 58, 73, 1014, 80, 1015, 42, 26, 81, 1016, 88,
    1017, 34, 1018, 66, 4, 89, 12, 50, 1019, 96, 1020, 19, 97, 43, 59, 1021,
    104, 82, 1022, 74, 105, 5, 1023, 67, 112, 35, 27, 1024, 20, 113, 90, 13,
    51, 1025, 120, 1026, 75, 128, 44, 121, 106, 98, 28, 60, 68, 129, 52, 21,
    83, 114, 36, 14, 76, 99, 45, 91, 29, 84, 53, 107, 130, 92, 122, 100,
    115, 61, 108, 85, 131, 69, 22, 123, 116, 93, 37, 77, 109, 30, 54, 132,
    124, 101, 86, 117, 94, 110, 133, 125, 118, 126,
)


def add_halves(left, right):
    return left + right


class Sums:
    def __init__(self, made, emit, s):
        self.made, self.emit = made, emit
        self.got0, self.a, self.b = s.got0, (s.a1, s.a2, s.a3, s.a4), (s.b1, s.b2, s.b3, s.b4, s.b5)
        self.send_sem, self.recv_sem = s.send_sem, s.recv_sem
        self.gain_send, self.gain_recv = s.gain_send, s.gain_recv
        self.gain_sum, self.gain_got = s.gain_sum, s.gain_got
        tm, clip = lax.axis_index("tm"), lax.axis_index("clip")
        self.core, self.x, self.low, self.high = tm % 2, (tm // 2) % 2, (tm // 4) % 2, tm // 8
        self.core_peer = (tm + 1 - 2 * self.core, clip)
        self.x_peer = (tm + 2 - 4 * self.x, clip)
        self.low_peer = (tm + 4 - 8 * self.low, clip)
        self.high_peer = (tm + 8 - 16 * self.high, clip)
        self.clip_peer = (tm, 1 - clip)
        self.peers = (self.core_peer, self.x_peer, self.low_peer, self.high_peer, self.clip_peer)
        half = D // 2
        self.mine = pl.ds(pl.multiple_of(clip * half, half), half)
        self.other = pl.ds(pl.multiple_of((1 - clip) * half, half), half)
        self.copies, self.gain_copies, self.places = {}, {}, {}
        self.started, self.left = [], set()
        self.slots = {
            place: sum((LETTERS[k] == "B") == (LETTERS[place] == "B") for k in range(place))
            for place in range(UNITS)
        }

    def meet(self):
        barrier = pltpu.get_barrier_semaphore()
        for peer in self.peers:
            pl.semaphore_signal(barrier, inc=1, device_id=peer, device_id_type=MESH)
        pl.semaphore_wait(barrier, len(self.peers))

    def send(self, src, dst, stage, place, peer):
        copy = pltpu.make_async_remote_copy(
            src_ref=src,
            dst_ref=dst,
            send_sem=self.send_sem.at[stage, place],
            recv_sem=self.recv_sem.at[stage, place],
            device_id=peer,
            device_id_type=MESH,
        )
        copy.start()
        self.places[stage, place] = len(self.started)
        self.started.append(copy)
        self.copies[stage, place] = copy

    def step(self, stage, place):
        if stage == 0:
            buffer, number = self.made(place)
            source = buffer.at[:, :, :, 1 - self.core, number]
            self.send(source, self.got0.at[place], 0, place, self.core_peer)
            return
        self.copies[stage - 1, place].wait_recv()
        if stage == 1:
            self.add_cores(place)
        step = dict(A=self.step_a, B=self.step_b, C=self.step_c)[LETTERS[place]]
        step(stage, place, self.slots[place])

    def add_cores(self, place):
        got0 = self.got0
        buffer, number = self.made(place)

        @pl.loop(0, 8)
        def _(block):
            i, j, k = block // 4, (block // 2) % 2, block % 2
            mine = buffer[i, j, k, self.core, number]
            got0[place, i, j, k] = add_halves(got0[place, i, j, k], mine)

    def step_a(self, stage, place, slot):
        got0, (a1, a2, a3, a4) = self.got0, self.a
        if stage == 1:
            source = got0.at[place, :, :, 1 - self.x]
            self.send(source, a1.at[slot], 1, place, self.x_peer)
        elif stage == 2:

            @pl.loop(0, 4)
            def _(block):
                i, j = block // 2, block % 2
                a1[slot, i, j] = add_halves(a1[slot, i, j], got0[place, i, j, self.x])

            self.send(a1.at[slot, :, 1 - self.low], a2.at[slot], 2, place, self.low_peer)
        elif stage == 3:

            @pl.loop(0, 2)
            def _(i):
                a2[slot, i] = add_halves(a2[slot, i], a1[slot, i, self.low])

            self.send(a2.at[slot, 1 - self.high], a3.at[slot], 3, place, self.high_peer)
        else:
            self.last_two(stage, place, slot, self.high)

    def step_c(self, stage, place, slot):
        got0, (a1, a2, a3, a4) = self.got0, self.a
        if stage == 1:
            source = got0.at[place, :, 1 - self.low]
            self.send(source, a1.at[slot], 1, place, self.low_peer)
        elif stage == 2:

            @pl.loop(0, 4)
            def _(block):
                i, j = block // 2, block % 2
                a1[slot, i, j] = add_halves(a1[slot, i, j], got0[place, i, self.low, j])

            self.send(a1.at[slot, 1 - self.high], a2.at[slot], 2, place, self.high_peer)
        elif stage == 3:

            @pl.loop(0, 2)
            def _(i):
                a2[slot, i] = add_halves(a2[slot, i], a1[slot, self.high, i])

            self.send(a2.at[slot, 1 - self.x], a3.at[slot], 3, place, self.x_peer)
        else:
            self.last_two(stage, place, slot, self.x)

    def last_two(self, stage, place, slot, side):
        a1, a2, a3, a4 = self.a
        if stage == 4:
            a3[slot] = add_halves(a3[slot], a2[slot, side])
            self.send(a3.at[slot], a4.at[slot], 4, place, self.clip_peer)
        else:
            total = a3[slot].astype(WIDE) + a4[slot].astype(WIDE)
            self.emit(UNIT_ORDER[place], slice(0, D), total)

    def step_b(self, stage, place, slot):
        got0, (b1, b2, b3, b4, b5) = self.got0, self.b
        if stage == 1:
            source = got0.at[place, :, :, :, :, self.other]
            self.send(source, b1.at[slot], 1, place, self.clip_peer)
        elif stage == 2:

            @pl.loop(0, 8)
            def _(block):
                i, j, k = block // 4, (block // 2) % 2, block % 2
                b1[slot, i, j, k] = add_halves(
                    b1[slot, i, j, k], got0[place, i, j, k, :, self.mine]
                )

            self.send(b1.at[slot, :, :, 1 - self.x], b2.at[slot], 2, place, self.x_peer)
        elif stage == 3:

            @pl.loop(0, 4)
            def _(block):
                i, j = block // 2, block % 2
                b2[slot, i, j] = add_halves(b2[slot, i, j], b1[slot, i, j, self.x])

            self.send(b2.at[slot, :, 1 - self.low], b3.at[slot], 3, place, self.low_peer)
        elif stage == 4:

            @pl.loop(0, 2)
            def _(i):
                b3[slot, i] = add_halves(b3[slot, i], b2[slot, i, self.low])

            self.send(b3.at[slot, 1 - self.high], b4.at[slot], 4, place, self.high_peer)
        elif stage == 5:
            b4[slot] = add_halves(b4[slot], b3[slot, self.high])
            self.send(b4.at[slot], b5.at[slot], 5, place, self.clip_peer)
        else:
            self.emit(UNIT_ORDER[place], self.mine, b4[slot].astype(WIDE))
            self.emit(UNIT_ORDER[place], self.other, b5[slot].astype(WIDE))

    def gain_step(self, number):
        if number > 0:
            self.gain_copies[number - 1].wait_recv()
            self.gain_sum[number] = self.gain_sum[number - 1] + self.gain_got[number - 1]
        if number < len(self.peers):
            copy = pltpu.make_async_remote_copy(
                src_ref=self.gain_sum.at[number],
                dst_ref=self.gain_got.at[number],
                send_sem=self.gain_send.at[number],
                recv_sem=self.gain_recv.at[number],
                device_id=self.peers[number],
                device_id_type=MESH,
            )
            copy.start()
            self.started.append(copy)
            self.gain_copies[number] = copy

    def leave(self, place):
        self.copies[0, place].wait_send()
        self.left.add(self.places[0, place])

    def finish(self):
        for number, copy in enumerate(self.started):
            if number not in self.left:
                copy.wait_send()


class BackIn(NamedTuple):
    length: Any
    x2: Any
    hidden: Any
    hidden_t: Any
    b3: Any
    x1: Any
    x: Any
    encoded_t: Any
    gain_mlp: Any
    gain_cross: Any
    gain_self: Any
    expand_w: Any
    narrow_w: Any
    cross: Layer
    own: Layer
    cross_w: Weights
    own_w: Weights


class BackOut(NamedTuple):
    output: Any
    input_grad: Any
    state_grad: Any
    summed: Any
    gains: Any


class Room(NamedTuple):
    x1: Any
    encoded_t: Any
    cross: Layer
    own: Layer
    weight: Any
    raised: Any
    ot: Any
    delta: Any
    g: Any
    x3: Any
    low: Any
    dov: Any
    dot_t: Any
    dqt: Any
    dk: Any
    dv: Any
    kept: Any
    narrow: Any
    total: Any
    got0: Any
    a1: Any
    a2: Any
    a3: Any
    a4: Any
    b1: Any
    b2: Any
    b3: Any
    b4: Any
    b5: Any
    gain_sum: Any
    gain_got: Any
    fetch_sem: Any
    raised_sem: Any
    out_sem: Any
    send_sem: Any
    recv_sem: Any
    gain_send: Any
    gain_recv: Any


class Once:
    def __init__(self, copy):
        self.copy, self.pending = copy, True
        copy.start()

    def ready(self):
        if self.pending:
            self.copy.wait()
        self.pending = False


def back_kernel(tree, *refs):
    given, out, s = jax.tree.unflatten(tree, refs)
    count = [0]

    def fetch(source, target):
        copy = pltpu.make_async_copy(source, target, s.fetch_sem.at[count[0]])
        count[0] += 1
        return Once(copy)

    def fetch_layer(source, target):
        return {
            field: fetch(getattr(source, field), getattr(target, field))
            for field in Layer._fields
            if getattr(target, field) is not None
        }

    def raised_copy(layer, pair):
        source = layer.raised.at[pl.ds(2 * pair, 2)]
        slot = pair % 2
        return pltpu.make_async_copy(
            source, s.raised.at[slot, :, pl.ds(0, source.shape[1])], s.raised_sem.at[slot]
        )

    def made(place):
        if 4 <= place < 8 or place >= 12:
            return s.narrow, place % 4
        return s.kept, place % 4 + 4 * (place >= 8)

    def keep(place, at, width, values):
        buffer, number = made(place)
        buffer[:, :, :, :, number, :, at : at + width] = values.astype(LOW).reshape(
            2, 2, 2, 2, PART, width
        )

    def emit(unit, cols, total):
        s.total[unit, :, cols] = total

    sums = Sums(made, emit, s)
    live = {}
    waits = {}

    def feed(strip, half):
        def run():
            first, second = s.weight[2 * (strip % 2)], s.weight[2 * (strip % 2) + 1]
            for name in ("hidden", "hidden_t", "b3", "x2"):
                waits[name].ready()
            width = D // 2
            at = half * width
            cols = slice(at, at + width)
            waits["first", strip].ready()
            active, slope = gelu_both(dot(s.dk[...], first[:, cols]))
            active = active.astype(LOW)
            waits["second", strip].ready()
            grad = (slope * dot_back(s.low[...], second[cols, :])).astype(LOW)
            keep(strip, at, width, dot(s.dot_t[...], grad))
            s.narrow[strip // 2, strip % 2, half] = (
                dot_rows(active, s.low[...]).astype(LOW).reshape(2, 4, PART, D)
            )
            forward, backward = dot(active, second[cols, :]), dot_back(grad, first[:, cols])
            if strip == 0 and half == 0:
                s.x3[...] = s.x1[...] + forward
                s.g[...] = backward
            else:
                s.x3[...] += forward
                s.g[...] += backward
            if strip < 2 and half:
                fetch_feed(strip + 2)

        return run

    def fetch_feed(strip):
        cols = pl.ds(strip * D, D)
        waits["first", strip] = fetch(given.expand_w.at[:, cols], s.weight[2 * (strip % 2)])
        waits["second", strip] = fetch(given.narrow_w.at[cols, :], s.weight[2 * (strip % 2) + 1])

    def feed_end():
        for place, name in enumerate(Weights._fields):
            waits["cross", name] = fetch(getattr(given.cross_w, name), s.weight[place])
        live = lax.broadcasted_iota(jnp.int32, s.x3.shape, 0) < given.length[0]
        s.dv[...] = jnp.where(live, s.x3[...], 0.0).astype(LOW)
        waits["output"] = Once(pltpu.make_async_copy(s.dv, out.output, s.out_sem.at[0]))
        part, gain_part = center_back(s.g[...], s.x1[...], given.gain_mlp[...])
        s.gain_sum[0, 2:3, :] = gain_part
        s.g[...] = s.low[...].astype(WIDE) + part
        waits["x1"] = fetch(given.x1, s.x1)

    def spread(layer, room, name):
        def run():
            waits[name, "output"].ready()
            waits[name]["inverse"].ready()
            s.low[...] = s.g[...].astype(LOW)
            waits[name, "ot"].ready()
            spread_grads(s.low[...], s.weight[0], room.inverse, s.ot, s.delta, s.dov, s.dot_t)
            if name == "cross":
                waits["own", "output"] = fetch(given.own_w.output, s.weight[0])

        return run

    def output_grad(room, name, place):
        def run():
            if name == "own":
                for unit in range(4, 8):
                    sums.leave(unit)
            mixed = s.ot[...].astype(LOW)
            for at, width in strips(D, 256):
                keep(place, at, width, dot(mixed, s.low[:, at : at + width]))
            if name == "cross":
                waits["own", "ot"] = fetch(given.own.ot, s.ot)

        return run

    def attention(layer, room, name, first):
        def run():
            for field in ("q", "kt", "v"):
                waits[name][field].ready()
            waits["output"].ready()
            inner = layer.raised.shape[1]

            @pl.loop(first, first + 2)
            def _(pair):
                raised_copy(layer, pair).wait()
                slot = pair % 2
                attend_pair(
                    pair,
                    room.q,
                    room.kt,
                    room.v,
                    s.raised.at[slot, :, pl.ds(0, inner)],
                    s.delta,
                    s.dot_t,
                    s.dov,
                    s.dqt,
                    s.dk.at[pl.ds(0, inner)],
                    s.dv.at[pl.ds(0, inner)],
                )
                if first < PAIRS - 2:
                    raised_copy(layer, pair + 2).start()
                elif name == "cross":
                    raised_copy(given.own, slot).start()

        return run

    def strip_grads(first_t, second_t, inner, strip, place):
        cols = slice(256 * strip, 256 * (strip + 1))
        part = s.dqt[cols, :].T
        s.low[:, cols] = part
        keep(place, 0, 256, dot(first_t[...], part))
        keep(place, 256, 256, dot(second_t[...], s.dk[0:inner, cols]))
        keep(place, 512, 256, dot(second_t[...], s.dv[0:inner, cols]))

    def cross_grads(strip):
        def run():
            waits["cross"]["ht"].ready()
            waits["encoded_t"].ready()
            strip_grads(s.cross.ht, s.encoded_t, s.encoded_t.shape[1], strip, 9 + strip)

        return run

    def cross_inputs():
        for name in ("query", "key", "value"):
            waits["cross", name].ready()
        waits["x1"].ready()
        frames = s.encoded_t.shape[1]
        for at, width in strips(D, 256):
            cols = slice(at, at + width)
            s.x3[0:frames, cols] = dot_back(s.dk[0:frames, :], s.weight[2][cols, :]) + dot_back(
                s.dv[0:frames, :], s.weight[3][cols, :]
            )
        state = s.x3.at[pl.ds(0, frames)]
        waits["state"] = Once(pltpu.make_async_copy(state, out.state_grad, s.out_sem.at[1]))
        part, gain_part = center_back(
            dot_back(s.low[...], s.weight[1][...]), s.x1[...], given.gain_cross[...]
        )
        s.gain_sum[0, 1:2, :] = gain_part
        s.g[...] += part
        for place, name in enumerate(Weights._fields):
            if place:
                waits["own", name] = fetch(getattr(given.own_w, name), s.weight[place])

    def self_grads(strip):
        def run():
            waits["own"]["ht"].ready()
            strip_grads(s.own.ht, s.own.ht, s.own.ht.shape[1], strip, 13 + strip)
            if strip == 2:
                waits["x"] = fetch(given.x, s.dov)

        return run

    def self_inputs():
        for name in ("query", "key", "value"):
            waits["own", name].ready()
        waits["x"].ready()
        for at, width in strips(D, 256):
            cols = slice(at, at + width)
            s.x1[:, cols] = (
                dot_back(s.low[...], s.weight[1][cols, :])
                + dot_back(s.dk[...], s.weight[2][cols, :])
                + dot_back(s.dv[...], s.weight[3][cols, :])
            )
        part, gain_part = center_back(s.x1[...], s.dov[...].astype(WIDE), given.gain_self[...])
        s.gain_sum[0, 0:1, :] = gain_part
        s.g[...] += part
        waits["input"] = Once(pltpu.make_async_copy(s.g, out.input_grad, s.out_sem.at[2]))

    pieces = [feed(strip, half) for strip in range(4) for half in range(2)]
    pieces += [feed_end, spread(given.cross, s.cross, "cross"), output_grad(s.cross, "cross", 8)]
    for strip in range(3):
        pieces += [attention(given.cross, s.cross, "cross", 2 * strip), cross_grads(strip)]
    pieces += [cross_inputs, spread(given.own, s.own, "own"), output_grad(s.own, "own", 12)]
    for strip in range(3):
        pieces += [attention(given.own, s.own, "own", 2 * strip), self_grads(strip)]
    pieces.append(self_inputs)
    waits["hidden"] = fetch(given.hidden, s.dk)
    fetch_feed(0)
    waits["b3"] = fetch(given.b3, s.low)
    waits["hidden_t"] = fetch(given.hidden_t, s.dot_t)
    waits["x2"] = fetch(given.x2, s.x1)
    fetch_feed(1)
    waits["cross"] = fetch_layer(given.cross, s.cross)
    waits["cross", "ot"] = fetch(given.cross.ot, s.ot)
    raised_copy(given.cross, 0).start()
    raised_copy(given.cross, 1).start()
    waits["encoded_t"] = fetch(given.encoded_t, s.encoded_t)
    waits["own"] = fetch_layer(given.own, s.own)
    s.gain_sum[0] = jnp.zeros(s.gain_sum.shape[1:], WIDE)
    met = False
    for code in STEPS:
        if code < 1000:
            if not met:
                sums.meet()
                met = True
            if code < UNITS * 8:
                sums.step(code % 8, code // 8)
            else:
                sums.gain_step(code % 8)
        else:
            pieces[code - 1000]()
    out.gains[...] = s.gain_sum[5]
    result = pltpu.make_async_copy(s.total, out.summed, s.out_sem.at[3])
    result.start()
    sums.finish()
    waits["state"].ready()
    waits["input"].ready()
    result.wait()


def room_for(given):
    rows, frames = given.x.shape[0], given.encoded_t.shape[1]
    split = (2, 2, 2, 2)
    thin = LETTERS.count("B")
    thick = UNITS - thin
    half = D // 2

    def low(*shape):
        return pltpu.VMEM(shape, LOW)

    def wide(*shape):
        return pltpu.VMEM(shape, WIDE)

    def like(array):
        return pltpu.VMEM(array.shape, array.dtype)

    def layer(source):
        return jax.tree.map(like, source)._replace(raised=None, ot=None)

    plain, turned = (rows, D), (D, rows)
    dma = pltpu.SemaphoreType.DMA
    return Room(
        x1=like(given.x1), encoded_t=like(given.encoded_t),
        cross=layer(given.cross), own=layer(given.own),
        weight=[low(D, D)] * 4, raised=low(2, 2, rows, rows), ot=wide(*turned),
        delta=like(given.own.inverse),
        g=wide(*plain), x3=wide(*plain), low=low(*plain), dov=low(*plain), dot_t=low(*turned),
        dqt=low(*turned), dk=low(*plain), dv=low(*plain),
        kept=low(*split, 8, PART, D), narrow=low(*split, 4, PART, D),
        total=wide(UNITS, PART, D), got0=low(UNITS, 2, 2, 2, PART, D),
        a1=low(thick, 2, 2, PART, D), a2=low(thick, 2, PART, D), a3=low(thick, PART, D),
        a4=low(thick, PART, D), b1=low(thin, 2, 2, 2, PART, half), b2=low(thin, 2, 2, PART, half),
        b3=low(thin, 2, PART, half), b4=low(thin, PART, half), b5=low(thin, PART, half),
        gain_sum=wide(6, 8, D), gain_got=wide(5, 8, D),
        fetch_sem=dma((40,)), raised_sem=dma((2,)), out_sem=dma((4,)),
        send_sem=dma((6, UNITS)), recv_sem=dma((6, UNITS)), gain_send=dma((5,)),
        gain_recv=dma((5,)),
    )


def backward_and_sum(given):
    rows, frames = given.x.shape[0], given.encoded_t.shape[1]
    outs = BackOut(
        output=shape_of((rows, D)), input_grad=shape_of((rows, D), WIDE),
        state_grad=shape_of((frames, D), WIDE), summed=shape_of((UNITS, PART, D), WIDE),
        gains=shape_of((8, D), WIDE),
    )
    room = room_for(given)
    places = jax.tree.map(lambda _: FAR, given)._replace(
        length=NUMBERS, gain_mlp=INSIDE, gain_cross=INSIDE, gain_self=INSIDE
    )
    results = pl.pallas_call(
        functools.partial(back_kernel, jax.tree.structure((given, outs, room))),
        out_shape=tuple(outs),
        in_specs=jax.tree.leaves(places),
        out_specs=(FAR,) * 4 + (INSIDE,),
        scratch_shapes=jax.tree.leaves(room),
        compiler_params=pltpu.CompilerParams(
            collective_id=0, has_side_effects=True, vmem_limit_bytes=63 * 2**20
        ),
    )(*jax.tree.leaves(given))
    return BackOut(*results)


def cut(matrix, strip):
    return matrix.at[:, pl.ds(256 * strip, 256)]


def finish_kernel(output, input_grad, state_grad, summed, *refs):
    outs, (rows_low, rows_wide, frames_wide, blocks, taken, given) = refs[:13], refs[13:]
    parts = [
        (summed.at[pl.ds(0, 8)], blocks.at[pl.ds(0, 8)]),
        (summed.at[pl.ds(8, 8)], blocks.at[pl.ds(8, 8)]),
        (input_grad, rows_wide),
        (state_grad, frames_wide),
        (output, rows_low),
    ]
    results = [
        [(blocks.at[3], outs[6]), (blocks.at[7], outs[10])]
        + [
            (blocks.at[4 * layer + k, :, pl.ds(256 * m, 256)], cut(outs[3 + 4 * layer + m], k))
            for layer in range(2)
            for k in range(3)
            for m in range(3)
        ],
        [(blocks.at[pl.ds(12, 4)], outs[12])]
        + [(blocks.at[8 + k], outs[11].at[:, pl.ds(k * D, D)]) for k in range(4)],
        [(rows_wide, outs[1])],
        [(frames_wide, outs[2])],
        [(rows_low, outs[0])],
    ]
    arriving = [
        pltpu.make_async_copy(*pair, taken.at[place]) for place, pair in enumerate(parts)
    ]
    for copy in arriving:
        copy.start()
    leaving = []
    for copy, pairs in zip(arriving, results):
        copy.wait()
        for pair in pairs:
            leaving.append(pltpu.make_async_copy(*pair, given.at[len(leaving)]))
            leaving[-1].start()
    for copy in leaving:
        copy.wait()


def finish(made):
    outs = [shape_of(made[k].shape, made[k].dtype) for k in range(3)]
    outs += [shape_of((PART, D), WIDE)] * 8
    outs += [shape_of((PART, 4 * D), WIDE), shape_of((4, PART, D), WIDE)]
    *results, narrow = pl.pallas_call(
        finish_kernel,
        out_shape=tuple(outs),
        in_specs=[FAR] * 4,
        out_specs=(FAR,) * len(outs),
        scratch_shapes=[pltpu.VMEM(array.shape, array.dtype) for array in made[:4]]
        + [pltpu.SemaphoreType.DMA((5,)), pltpu.SemaphoreType.DMA((28,))],
        compiler_params=parameters(62),
    )(*made[:4])
    return *results, narrow.reshape(4 * PART, D)


def body(
    members,
    groups,
    mel_frames,
    conv_first,
    conv_second,
    enc_projection,
    enc_output,
    enc_expand,
    enc_narrow,
    dec_input,
    lengths,
    self_query,
    self_key,
    self_value,
    self_output,
    cross_query,
    cross_key,
    cross_value,
    cross_output,
    mlp_expand,
    mlp_narrow,
    gain_self,
    gain_cross,
    gain_mlp,
    cotangent,
):
    inputs, length = dec_input[0, 0], lengths[0]
    own_w = Weights(self_output, self_query, self_key, self_value)
    x1, own, mel = self_forward(length, inputs, gain_self, mel_frames[:, 0], members, own_w)
    encoded, encoded_t = encode(
        mel, conv_first, conv_second, enc_projection, enc_output, enc_expand, enc_narrow
    )
    cross_w = Weights(cross_output, cross_query, cross_key, cross_value)
    x2, hidden, hidden_t, b3, cross = cross_forward(
        length, x1, encoded, cotangent[0, 0], gain_cross, gain_mlp, cross_w
    )
    if (members, groups) == (16, 2):
        made = backward_and_sum(
            BackIn(
                length, x2, hidden, hidden_t, b3, x1, inputs, encoded_t,
                gain_mlp, gain_cross, gain_self, mlp_expand, mlp_narrow,
                cross, own, cross_w, own_w,
            )
        )
        dec_output, dec_input_grad, enc_state_grad, *totals = finish(made)
        gains = made.gains
    else:
        dec_output, g2, g_gain_mlp, g_expand, g_narrow = feed_both(
            length, x2, hidden, hidden_t, b3, gain_mlp, mlp_expand, mlp_narrow
        )
        g1, g_gain_cross, enc_state_grad, *cross_grads = cross_backward(
            (g2, x1, gain_cross) + tuple(cross) + (encoded_t,), cross_w
        )
        dec_input_grad, g_gain_self, *self_grads = self_backward(
            (g1, inputs, gain_self) + tuple(own), own_w
        )
        gains = jnp.concatenate([g_gain_self, g_gain_cross, g_gain_mlp, jnp.zeros((5, D), WIDE)])
        totals, gains = sum_plain(
            self_grads + cross_grads + [g_expand, g_narrow], gains, members, groups
        )
    part = D // members
    gains = lax.dynamic_slice_in_dim(gains, lax.axis_index("tm") * part, part, 1)
    return (
        encoded[None, None],
        dec_output[None, None],
        dec_input_grad[None, None],
        enc_state_grad[None, None],
        *totals,
        gains[0],
        gains[1],
        gains[2],
    )


def solution(mesh):
    placed = (
        P("tm", "clip", None, None),
        P(),
        P(),
        P(),
        P(),
        P(),
        P(),
        P("clip", "tm", None, None),
        P("clip", "tm"),
        P(),
        P(),
        P(),
        P(),
        P(),
        P(),
        P(),
        P(),
        P(),
        P(),
        P(),
        P(),
        P(),
        P("clip", "tm", None, None),
    )
    return jax.shard_map(
        functools.partial(body, mesh.shape["tm"], mesh.shape["clip"]),
        mesh=mesh,
        in_specs=placed,
        out_specs=(
            P("clip", "tm", None, None),
            P("clip", "tm", None, None),
            P("clip", "tm", None, None),
            P("clip", "tm", None, None),
            P("tm", None),
            P("tm", None),
            P("tm", None),
            P("tm", None),
            P("tm", None),
            P("tm", None),
            P("tm", None),
            P("tm", None),
            P("tm", None),
            P("tm", None),
            P("tm"),
            P("tm"),
            P("tm"),
        ),
        check_vma=False,
    )
```

```python
import functools
import math
from typing import Any, NamedTuple

import jax
import jax.numpy as jnp
import numpy as np
from jax import lax
from jax.experimental import pallas as pl
from jax.experimental.pallas import tpu as pltpu
from jax.sharding import PartitionSpec as P

D = 768
HEADS = 12
HD = 64
PAIRS = HEADS // 2
LANES = 2 * HD
SCALE = HD ** (-0.5)
LOW = jnp.bfloat16
WIDE = jnp.float32
INSIDE = pl.BlockSpec(memory_space=pltpu.VMEM)
FAR = pl.BlockSpec(memory_space=pltpu.HBM)
MESH = pl.DeviceIdType.MESH
NUMBERS = pl.BlockSpec(memory_space=pltpu.SMEM)


def shape_of(shape, kind=LOW):
    return jax.ShapeDtypeStruct(shape, kind)


def parameters(megabytes=58):
    return pltpu.CompilerParams(vmem_limit_bytes=megabytes * 2**20)


def center(values):
    shifted = values - jnp.mean(values, axis=-1, keepdims=True)
    spread = jnp.mean(shifted * shifted, axis=-1, keepdims=True)
    root = lax.rsqrt(spread + 1e-05)
    return shifted * root, root


def center_back(gradient, values, gain):
    normed, root = center(values)
    inner = gradient * gain
    first = jnp.mean(inner, axis=-1, keepdims=True)
    second = jnp.mean(inner * normed, axis=-1, keepdims=True)
    gain_part = jnp.sum(gradient * normed, axis=0, keepdims=True)
    return root * (inner - first - normed * second), gain_part


def gelu(values):
    return values * (0.5 + 0.5 * lax.erf(values * 2**-0.5))


def gelu_both(values):
    area = 0.5 + 0.5 * lax.erf(values * 2**-0.5)
    slope = area + values * ((2 * math.pi) ** -0.5 * jnp.exp(-0.5 * values * values))
    return values * area, slope


def dot(left, right):
    return jnp.dot(left, right, preferred_element_type=WIDE)


def dot_back(left, right):
    return lax.dot_general(left, right, (((1,), (1,)), ((), ())), preferred_element_type=WIDE)


def dot_rows(left, right):
    return lax.dot_general(left, right, (((0,), (0,)), ((), ())), preferred_element_type=WIDE)


def strips(total, width):
    return [(at, min(width, total - at)) for at in range(0, total, width)]


class Fetch:
    def __init__(self, sources, targets, semaphores):
        self.copies = [
            pltpu.make_async_copy(source, target, semaphores.at[place])
            for place, (source, target) in enumerate(zip(sources, targets))
        ]
        for copy in self.copies:
            copy.start()

    def wait(self, place):
        self.copies[place].wait()


def pair_lanes(pair):
    return pl.ds(pl.multiple_of(pair * LANES, LANES), LANES)


def head_rows(pair, side):
    return pl.ds(pl.multiple_of(pair * LANES + side * HD, HD), HD)


def attend(
    q_ref, k_ref, vt_ref, bias_ref, ot_ref, inverse_ref=None, raised_ref=None, leave=None
):
    ones = jnp.ones((16, vt_ref.shape[1]), LOW)

    @pl.loop(0, PAIRS, step=2)
    def _(first):
        heads = [(first + more, side) for more in range(2) for side in range(2)]
        cuts = [slice(side * HD, (side + 1) * HD) for _, side in heads]
        queries = [q_ref[:, pair_lanes(first + more)] for more in range(2)]
        keys = [k_ref[:, pair_lanes(first + more)] for more in range(2)]
        scores = [dot_back(keys[k // 2][:, cuts[k]], queries[k // 2][:, cuts[k]]) for k in range(4)]
        if bias_ref is not None:
            scores = [part + bias_ref[...] for part in scores]
        raised = [
            jnp.exp(part - jnp.max(part, axis=0, keepdims=True)).astype(LOW) for part in scores
        ]
        rows = [head_rows(pair, side) for pair, side in heads]
        mixed = [
            dot(jnp.concatenate([vt_ref[rows[k], :], ones], axis=0), raised[k]) for k in range(4)
        ]
        for k, (pair, side) in enumerate(heads):
            inverse = 1.0 / mixed[k][HD : HD + 1]
            ot_ref[rows[k], :] = mixed[k][:HD] * inverse
            if raised_ref is not None:
                raised_ref[2 * pair + side] = raised[k]
                inverse_ref[2 * pair + side] = jnp.broadcast_to(inverse, inverse_ref.shape[1:])
        if leave is not None:
            leave(first)
            leave(first + 1)


def attend_pair(
    pair, q_ref, kt_ref, v_ref, raised_ref, delta_ref, dot_ref, dov_ref, dqt_ref, dk_ref, dv_ref
):
    lanes = pair_lanes(pair)
    queries, values, grads = q_ref[:, lanes], v_ref[:, lanes], dov_ref[:, lanes]
    sides = range(2)
    rows = [head_rows(pair, side) for side in sides]
    cuts = [slice(side * HD, (side + 1) * HD) for side in sides]
    products = [dot(values[:, cuts[side]], dot_ref[rows[side], :]) for side in sides]
    value_sides = [dot(raised_ref[side], grads[:, cuts[side]]) for side in sides]
    score_grads = [
        (
            raised_ref[side].astype(WIDE)
            * (products[side] - delta_ref[2 * pair + side, 0:1, :])
        ).astype(LOW)
        for side in sides
    ]
    key_sides = [dot(score_grads[side], queries[:, cuts[side]]) for side in sides]
    query_sides = [dot(kt_ref[rows[side], :], score_grads[side]) for side in sides]
    for side in sides:
        dqt_ref[rows[side], :] = (query_sides[side] * SCALE).astype(LOW)
    dk_ref[:, lanes] = jnp.concatenate(key_sides, axis=1).astype(LOW)
    dv_ref[:, lanes] = jnp.concatenate(value_sides, axis=1).astype(LOW)


def attend_back(q_ref, kt_ref, v_ref, raised_ref, *rest):
    @pl.loop(0, PAIRS)
    def _(pair):
        attend_pair(pair, q_ref, kt_ref, v_ref, raised_ref.at[pl.ds(2 * pair, 2)], *rest)


def encoder_kernel(
    mel_ref, position_ref, first_h, second_h, joint_h, output_h, expand_h, narrow_h,
    out_ref, out_t_ref,
    first_w, second_w, joint_w, output_w, expand_w, narrow_w,
    even, odd, state, hidden, q, k, vt, mixed_t, semaphores,
):
    length = out_ref.shape[0]
    fetch = Fetch(
        (first_h, second_h, joint_h, output_h, expand_h, narrow_h),
        (first_w, second_w, joint_w, output_w, expand_w, narrow_w),
        semaphores,
    )
    taps = [mel_ref[pl.ds(7 + tap, length, stride=2), :].astype(LOW) for tap in range(4)]
    fetch.wait(0)
    for at, width in strips(D, 256):
        cols = pl.ds(at, width)
        for start, target in ((0, even), (1, odd)):
            total = sum(dot(taps[start + o], first_w[o, :, cols]) for o in range(3))
            target[:, cols] = gelu(total).astype(LOW)
    fetch.wait(1)
    ranks = lax.broadcasted_iota(jnp.int32, (length, 256), 0)
    for at, width in strips(D, 256):
        cols = pl.ds(at, width)
        before = pltpu.roll(dot(odd[...], second_w[0, :, cols]), 1, 0)
        total = dot(even[...], second_w[1, :, cols]) + dot(odd[...], second_w[2, :, cols])
        total = total + jnp.where(ranks == 0, 0.0, before)
        state[:, cols] = gelu(total) + position_ref[:, cols]
    hidden[...] = center(state[...])[0].astype(LOW)
    fetch.wait(2)
    for at, width in strips(D, 256):
        cols = pl.ds(at, width)
        q[:, cols] = (dot(hidden[...], joint_w[:, cols]).astype(LOW) * SCALE).astype(LOW)
        k[:, cols] = dot(hidden[...], joint_w[:, pl.ds(D + at, width)]).astype(LOW)
        vt[cols, :] = dot(hidden[...], joint_w[:, pl.ds(2 * D + at, width)]).astype(LOW).T
    attend(q, k, vt, None, mixed_t)
    fetch.wait(3)
    mixed = mixed_t[...].astype(LOW).T
    for at, width in strips(D, 256):
        cols = pl.ds(at, width)
        state[:, cols] += dot(mixed, output_w[:, cols])
    hidden[...] = center(state[...])[0].astype(LOW)
    fetch.wait(4)
    fetch.wait(5)

    @pl.loop(0, expand_w.shape[1] // 512)
    def _(strip):
        cols = pl.ds(pl.multiple_of(strip * 512, 512), 512)
        widened = gelu(dot(hidden[...], expand_w[:, cols])).astype(LOW)
        state[...] += dot(widened, narrow_w[cols, :])

    encoded = center(state[...])[0].astype(LOW)
    out_ref[...] = encoded
    out_t_ref[...] = encoded.T


def encode(mel, conv_first, conv_second, enc_projection, enc_output, enc_expand, enc_narrow):
    length = (mel.shape[0] - 16) // 2
    weights = (conv_first, conv_second, enc_projection, enc_output, enc_expand, enc_narrow)
    return pl.pallas_call(
        encoder_kernel,
        out_shape=(shape_of((length, D)), shape_of((D, length))),
        in_specs=[INSIDE] * 2 + [FAR] * 6,
        out_specs=(INSIDE, INSIDE),
        scratch_shapes=[pltpu.VMEM(weight.shape, LOW) for weight in weights]
        + [
            pltpu.VMEM((length, D), LOW),
            pltpu.VMEM((length, D), LOW),
            pltpu.VMEM((length, D), WIDE),
            pltpu.VMEM((length, D), LOW),
            pltpu.VMEM((length, D), LOW),
            pltpu.VMEM((length, D), LOW),
            pltpu.VMEM((D, length), LOW),
            pltpu.VMEM((D, length), WIDE),
            pltpu.SemaphoreType.DMA((6,)),
        ],
        compiler_params=parameters(),
    )(mel, sinusoids(length, D), *weights)


def sinusoids(length, features):
    halfway = features // 2
    inverse = np.exp(-math.log(10000.0) / (halfway - 1) * np.arange(halfway)).astype(np.float32)
    angles = np.arange(length, dtype=np.float32)[:, None] * inverse[None, :]
    angles = angles.astype(np.float64)
    return jnp.asarray(np.concatenate([np.sin(angles), np.cos(angles)], axis=1).astype(np.float32))


class Layer(NamedTuple):
    ht: Any
    q: Any
    kt: Any
    v: Any
    raised: Any
    inverse: Any
    ot: Any


class Weights(NamedTuple):
    output: Any
    query: Any
    key: Any
    value: Any


class Leave:
    def __init__(self, held, targets, semaphores):
        self.pairs, self.semaphores, self.started = list(zip(held, targets)), semaphores, []

    def __call__(self, *places):
        for place in places:
            copy = pltpu.make_async_copy(*self.pairs[place], self.semaphores.at[place])
            copy.start()
            self.started.append(copy)

    def scores(self, place, first):
        def copy(pair):
            held, target = self.pairs[place]
            heads = pl.ds(2 * pair, 2)
            return pltpu.make_async_copy(
                held.at[heads], target.at[heads], self.semaphores.at[first + pair]
            )

        self.started += [copy(pair) for pair in range(PAIRS)]
        return lambda pair: copy(pair).start()

    def finish(self):
        for copy in self.started:
            copy.wait()


def self_kernel(
    members, length_ref, x_ref, gain_ref, mel_h, output_h, query_h, key_h, value_h, *refs
):
    outs, held = refs[:9], refs[9:18]
    output_w, query_w, key_w, value_w, hidden, k, vt, bias = refs[18:26]
    semaphores, out_sem, own_sem, send_sem, recv_sem = refs[26:]
    x1, ht, q, kt, v, raised, inverse, ot, mel = held
    leave = Leave(held, outs, out_sem)
    tm, clip = lax.axis_index("tm"), lax.axis_index("clip")
    barrier = pltpu.get_barrier_semaphore()

    @pl.loop(1, members)
    def _(step):
        peer = (lax.rem(tm + step, members), clip)
        pl.semaphore_signal(barrier, inc=1, device_id=peer, device_id_type=MESH)

    fetch = Fetch(
        (query_h, key_h, value_h, output_h), (query_w, key_w, value_w, output_w), semaphores
    )
    rows = x_ref.shape[0]
    hidden[...] = (center(x_ref[...].astype(WIDE))[0] * gain_ref[...]).astype(LOW)
    keys = lax.broadcasted_iota(jnp.int32, (rows, rows), 0)
    queries = lax.broadcasted_iota(jnp.int32, (rows, rows), 1)
    allowed = (keys <= queries) & (keys < length_ref[0])
    bias[...] = jnp.where(allowed, 0.0, -1e30)
    fetch.wait(0)
    fetch.wait(1)
    fetch.wait(2)
    for at, width in strips(D, 256):
        cols = pl.ds(at, width)
        q[:, cols] = (dot(hidden[...], query_w[:, cols]).astype(LOW) * SCALE).astype(LOW)
        part = dot(hidden[...], key_w[:, cols]).astype(LOW)
        k[:, cols] = part
        kt[cols, :] = part.T
        part = dot(hidden[...], value_w[:, cols]).astype(LOW)
        v[:, cols] = part
        vt[cols, :] = part.T
    ht[...] = hidden[...].T
    leave(1, 2, 3, 4)
    pl.semaphore_wait(barrier, members - 1)
    frames = mel_h.shape[1]
    place = pl.ds(pl.multiple_of(8 + tm * frames, 8), frames)

    def pass_on(step):
        peer = lax.rem(tm + step, members)
        return pltpu.make_async_remote_copy(
            src_ref=mel_h.at[peer],
            dst_ref=mel.at[place],
            send_sem=send_sem.at[step],
            recv_sem=recv_sem.at[step],
            device_id=(peer, clip),
            device_id_type=MESH,
        )

    @pl.loop(1, members)
    def _(step):
        pass_on(step).start()

    stay = pltpu.make_async_copy(mel_h.at[tm], mel.at[place], own_sem)
    stay.start()
    mel[0:8, :] = jnp.zeros((8, mel.shape[1]), WIDE)
    mel[mel.shape[0] - 8 :, :] = jnp.zeros((8, mel.shape[1]), WIDE)
    attend(q, k, vt, bias, ot, inverse, raised, leave.scores(5, 9))
    leave(6, 7)
    fetch.wait(3)
    mixed = ot[...].astype(LOW).T
    for at, width in strips(D, 256):
        cols = pl.ds(at, width)
        x1[:, cols] = x_ref[:, cols].astype(WIDE) + dot(mixed, output_w[:, cols])
    leave(0)

    @pl.loop(1, members)
    def _(step):
        pass_on(step).wait()

    stay.wait()
    leave(8)
    leave.finish()


def held_like(shapes):
    return [pltpu.VMEM(shape.shape, shape.dtype) for shape in shapes]


def self_forward(lengths, inputs, gain, mel_frames, members, weights):
    rows = inputs.shape[0]
    mel = jnp.transpose(mel_frames.astype(WIDE), (1, 0, 2))
    arrived = (members * mel.shape[1] + 16, mel.shape[2])
    plain, turned = (rows, D), (D, rows)
    outs = (
        shape_of(plain, WIDE), shape_of(turned), shape_of(plain), shape_of(turned),
        shape_of(plain), shape_of((HEADS, rows, rows)), shape_of((HEADS, 8, rows), WIDE),
        shape_of(turned, WIDE), shape_of(arrived, WIDE),
    )
    x1, *layer, arrived = pl.pallas_call(
        functools.partial(self_kernel, members),
        out_shape=outs,
        in_specs=[NUMBERS, INSIDE, INSIDE] + [FAR] * 5,
        out_specs=(FAR,) * 9,
        scratch_shapes=held_like(outs)
        + [pltpu.VMEM((D, D), LOW)] * 4
        + [
            pltpu.VMEM(plain, LOW),
            pltpu.VMEM(plain, LOW),
            pltpu.VMEM(turned, LOW),
            pltpu.VMEM((rows, rows), WIDE),
            pltpu.SemaphoreType.DMA((4,)),
            pltpu.SemaphoreType.DMA((9 + PAIRS,)),
            pltpu.SemaphoreType.DMA(()),
            pltpu.SemaphoreType.DMA((members,)),
            pltpu.SemaphoreType.DMA((members,)),
        ],
        compiler_params=pltpu.CompilerParams(
            collective_id=1, has_side_effects=True, vmem_limit_bytes=58 * 2**20
        ),
    )(lengths, inputs, gain, mel, *weights)
    return x1, Layer(*layer), arrived


def cross_kernel(
    length_ref, x1_ref, encoded_ref, cotangent_ref, gain_cross_ref, gain_mlp_ref,
    output_h, query_h, key_h, value_h, *refs
):
    outs, held = refs[:11], refs[11:22]
    output_w, query_w, key_w, value_w, k, vt, semaphores, out_sem = refs[22:]
    x2, hidden, hidden_t, b3, ht, q, kt, v, raised, inverse, ot = held
    leave = Leave(held, outs, out_sem)
    fetch = Fetch(
        (query_h, key_h, value_h, output_h), (query_w, key_w, value_w, output_w), semaphores
    )
    rows = x1_ref.shape[0]
    hidden[...] = (center(x1_ref[...])[0] * gain_cross_ref[...]).astype(LOW)
    fetch.wait(0)
    fetch.wait(1)
    fetch.wait(2)
    for at, width in strips(D, 256):
        cols = pl.ds(at, width)
        q[:, cols] = (dot(hidden[...], query_w[:, cols]).astype(LOW) * SCALE).astype(LOW)
        part = dot(encoded_ref[...], key_w[:, cols]).astype(LOW)
        k[:, cols] = part
        kt[cols, :] = part.T
        part = dot(encoded_ref[...], value_w[:, cols]).astype(LOW)
        v[:, cols] = part
        vt[cols, :] = part.T
    ht[...] = hidden[...].T
    live = lax.broadcasted_iota(jnp.int32, (rows, D), 0) < length_ref[0]
    b3[...] = jnp.where(live, cotangent_ref[...].astype(WIDE), 0.0).astype(LOW)
    leave(3, 4, 5, 6, 7)
    attend(q, k, vt, None, ot, inverse, raised, leave.scores(8, 11))
    leave(9, 10)
    fetch.wait(3)
    mixed = ot[...].astype(LOW).T
    for at, width in strips(D, 256):
        cols = pl.ds(at, width)
        x2[:, cols] = x1_ref[:, cols] + dot(mixed, output_w[:, cols])
    leave(0)
    hidden[...] = (center(x2[...])[0] * gain_mlp_ref[...]).astype(LOW)
    leave(1)
    hidden_t[...] = hidden[...].T
    leave(2)
    leave.finish()


def cross_forward(lengths, x1, encoded, cotangent, gain_cross, gain_mlp, weights):
    rows, frames = x1.shape[0], encoded.shape[0]
    plain, turned = (rows, D), (D, rows)
    outs = (
        shape_of(plain, WIDE), shape_of(plain), shape_of(turned), shape_of(plain),
        shape_of(turned), shape_of(plain), shape_of((D, frames)), shape_of((frames, D)),
        shape_of((HEADS, frames, rows)), shape_of((HEADS, 8, rows), WIDE),
        shape_of(turned, WIDE),
    )
    x2, hidden, hidden_t, b3, *layer = pl.pallas_call(
        cross_kernel,
        out_shape=outs,
        in_specs=[NUMBERS] + [INSIDE] * 5 + [FAR] * 4,
        out_specs=(FAR,) * 11,
        scratch_shapes=held_like(outs)
        + [pltpu.VMEM(weight.shape, LOW) for weight in weights]
        + [
            pltpu.VMEM((frames, D), LOW),
            pltpu.VMEM((D, frames), LOW),
            pltpu.SemaphoreType.DMA((4,)),
            pltpu.SemaphoreType.DMA((11 + PAIRS,)),
        ],
        compiler_params=parameters(),
    )(lengths, x1, encoded, cotangent, gain_cross, gain_mlp, *weights)
    return x2, hidden, hidden_t, b3, Layer(*layer)


def feed_kernel(
    length_ref, x2_ref, hidden, hidden_t, b3, gain_ref, expand_h, narrow_h,
    out_ref, g2_ref, gain_grad_ref, expand_grad_ref, narrow_grad_ref,
    expand_w, narrow_w, x3, back, semaphores,
):
    fetch = Fetch((expand_h, narrow_h), (expand_w, narrow_w), semaphores)
    x3[...] = x2_ref[...]
    back[...] = jnp.zeros_like(back)
    fetch.wait(0)
    fetch.wait(1)

    @pl.loop(0, expand_w.shape[1] // 512)
    def _(strip):
        cols = pl.ds(pl.multiple_of(strip * 512, 512), 512)
        active, slope = gelu_both(dot(hidden[...], expand_w[:, cols]))
        active = active.astype(LOW)
        grad = (slope * dot_back(b3[...], narrow_w[cols, :])).astype(LOW)
        x3[...] += dot(active, narrow_w[cols, :])
        narrow_grad_ref[cols, :] = dot_rows(active, b3[...]).astype(LOW)
        expand_grad_ref[:, cols] = dot(hidden_t[...], grad).astype(LOW)
        back[...] += dot_back(grad, expand_w[:, cols])

    live = lax.broadcasted_iota(jnp.int32, x3.shape, 0) < length_ref[0]
    out_ref[...] = jnp.where(live, x3[...], 0.0).astype(LOW)
    part, gain_part = center_back(back[...], x2_ref[...], gain_ref[...])
    gain_grad_ref[...] = gain_part
    g2_ref[...] = b3[...].astype(WIDE) + part


def feed_both(lengths, x2, hidden, hidden_t, b3, gain_mlp, expand, narrow):
    plain = x2.shape
    return pl.pallas_call(
        feed_kernel,
        out_shape=(
            shape_of(plain), shape_of(plain, WIDE), shape_of((1, D), WIDE),
            shape_of(expand.shape), shape_of(narrow.shape),
        ),
        in_specs=[NUMBERS] + [INSIDE] * 5 + [FAR] * 2,
        out_specs=(INSIDE,) * 5,
        scratch_shapes=[
            pltpu.VMEM(expand.shape, LOW),
            pltpu.VMEM(narrow.shape, LOW),
            pltpu.VMEM(plain, WIDE),
            pltpu.VMEM(plain, WIDE),
            pltpu.SemaphoreType.DMA((2,)),
        ],
        compiler_params=parameters(),
    )(lengths, x2, hidden, hidden_t, b3, gain_mlp, expand, narrow)


def spread_grads(out_grad, output_w, inverse_ref, ot_ref, delta_ref, dov, dot_t):
    for at, width in strips(D, 256):
        part = dot_back(out_grad, output_w[at : at + width, :]).astype(LOW).T
        sides = []
        for number in range(width // HD):
            head = at // HD + number
            side = part[number * HD : (number + 1) * HD, :].astype(WIDE)
            side = (side * inverse_ref[head, 0:1, :]).astype(LOW)
            mixed = ot_ref[head * HD : (head + 1) * HD, :]
            delta = jnp.sum(mixed * side.astype(WIDE), axis=0, keepdims=True)
            delta_ref[head] = jnp.broadcast_to(delta, delta_ref.shape[1:])
            sides.append(side)
        part = jnp.concatenate(sides, axis=0)
        dot_t[at : at + width, :] = part
        dov[:, at : at + width] = part.T


def cross_back_kernel(
    g2_ref, x1_ref, gain_ref, ht_ref, q_ref, kt_ref, v_ref, raised_ref, inverse_ref, ot_ref,
    encoded_t_ref, output_h, query_h, key_h, value_h,
    g1_ref, gain_grad_ref, state_grad_ref, query_g, key_g, value_g, output_g,
    output_w, query_w, key_w, value_w, dov, dot_t, dqt, dk, dv, delta, semaphores,
):
    fetch = Fetch(
        (output_h, query_h, key_h, value_h), (output_w, query_w, key_w, value_w), semaphores
    )
    b2 = g2_ref[...].astype(LOW)
    fetch.wait(0)
    spread_grads(b2, output_w, inverse_ref, ot_ref, delta, dov, dot_t)
    mixed = ot_ref[...].astype(LOW)
    for at, width in strips(D, 256):
        output_g[:, at : at + width] = dot(mixed, b2[:, at : at + width]).astype(LOW)
    attend_back(q_ref, kt_ref, v_ref, raised_ref, delta, dot_t, dov, dqt, dk, dv)
    dq = dqt[...].T
    for place in range(1, 4):
        fetch.wait(place)
    for at, width in strips(D, 256):
        cols = slice(at, at + width)
        query_g[:, cols] = dot(ht_ref[...], dq[:, cols]).astype(LOW)
        key_g[:, cols] = dot(encoded_t_ref[...], dk[:, cols]).astype(LOW)
        value_g[:, cols] = dot(encoded_t_ref[...], dv[:, cols]).astype(LOW)
        state_grad_ref[:, cols] = dot_back(dk[...], key_w[cols, :]) + dot_back(
            dv[...], value_w[cols, :]
        )
    part, gain_part = center_back(dot_back(dq, query_w[...]), x1_ref[...], gain_ref[...])
    gain_grad_ref[...] = gain_part
    g1_ref[...] = g2_ref[...] + part


def cross_backward(operands, weights):
    rows, frames = operands[0].shape[0], operands[10].shape[1]
    plain, turned, square = (rows, D), (D, rows), shape_of((D, D))
    return pl.pallas_call(
        cross_back_kernel,
        out_shape=(
            shape_of(plain, WIDE), shape_of((1, D), WIDE), shape_of((frames, D), WIDE),
            square, square, square, square,
        ),
        in_specs=[INSIDE] * 11 + [FAR] * 4,
        out_specs=(INSIDE,) * 7,
        scratch_shapes=[pltpu.VMEM((D, D), LOW)] * 4
        + [
            pltpu.VMEM(plain, LOW),
            pltpu.VMEM(turned, LOW),
            pltpu.VMEM(turned, LOW),
            pltpu.VMEM((frames, D), LOW),
            pltpu.VMEM((frames, D), LOW),
            pltpu.VMEM((HEADS, 8, rows), WIDE),
            pltpu.SemaphoreType.DMA((4,)),
        ],
        compiler_params=parameters(),
    )(*operands, *weights)


def self_back_kernel(
    g1_ref, x_ref, gain_ref, ht_ref, q_ref, kt_ref, v_ref, raised_ref, inverse_ref, ot_ref,
    output_h, query_h, key_h, value_h,
    input_grad_ref, gain_grad_ref, query_g, key_g, value_g, output_g,
    output_w, query_w, key_w, value_w, dov, dot_t, dqt, dk, dv, delta, semaphores,
):
    fetch = Fetch(
        (output_h, query_h, key_h, value_h), (output_w, query_w, key_w, value_w), semaphores
    )
    b1 = g1_ref[...].astype(LOW)
    fetch.wait(0)
    spread_grads(b1, output_w, inverse_ref, ot_ref, delta, dov, dot_t)
    mixed = ot_ref[...].astype(LOW)
    for at, width in strips(D, 256):
        output_g[:, at : at + width] = dot(mixed, b1[:, at : at + width]).astype(LOW)
    attend_back(q_ref, kt_ref, v_ref, raised_ref, delta, dot_t, dov, dqt, dk, dv)
    dq = dqt[...].T
    for place in range(1, 4):
        fetch.wait(place)
    for at, width in strips(D, 256):
        cols = slice(at, at + width)
        query_g[:, cols] = dot(ht_ref[...], dq[:, cols]).astype(LOW)
        key_g[:, cols] = dot(ht_ref[...], dk[:, cols]).astype(LOW)
        value_g[:, cols] = dot(ht_ref[...], dv[:, cols]).astype(LOW)
        input_grad_ref[:, cols] = (
            dot_back(dq, query_w[cols, :])
            + dot_back(dk[...], key_w[cols, :])
            + dot_back(dv[...], value_w[cols, :])
        )
    part, gain_part = center_back(
        input_grad_ref[...], x_ref[...].astype(WIDE), gain_ref[...]
    )
    gain_grad_ref[...] = gain_part
    input_grad_ref[...] = g1_ref[...] + part


def self_backward(operands, weights):
    rows = operands[0].shape[0]
    plain, turned, square = (rows, D), (D, rows), shape_of((D, D))
    return pl.pallas_call(
        self_back_kernel,
        out_shape=(shape_of(plain, WIDE), shape_of((1, D), WIDE), square, square, square, square),
        in_specs=[INSIDE] * 10 + [FAR] * 4,
        out_specs=(INSIDE,) * 6,
        scratch_shapes=[pltpu.VMEM((D, D), LOW)] * 4
        + [
            pltpu.VMEM(plain, LOW),
            pltpu.VMEM(turned, LOW),
            pltpu.VMEM(turned, LOW),
            pltpu.VMEM(plain, LOW),
            pltpu.VMEM(plain, LOW),
            pltpu.VMEM((HEADS, 8, rows), WIDE),
            pltpu.SemaphoreType.DMA((4,)),
        ],
        compiler_params=parameters(),
    )(*operands, *weights)


def trade(values, axis, size, bit):
    return lax.ppermute(values, axis, [(i, i ^ bit) for i in range(size)])


def add_rounded(left, right):
    return (left.astype(jnp.float32) + right.astype(jnp.float32)).astype(jnp.bfloat16)


def halve(values, dim, axis, size, bit):
    mine = (lax.axis_index(axis) // bit) % 2
    kept = lax.dynamic_index_in_dim(values, mine, dim, keepdims=False)
    sent = lax.dynamic_index_in_dim(values, 1 - mine, dim, keepdims=False)
    return add_rounded(kept, trade(sent, axis, size, bit))


def bits_of(size):
    return [1 << k for k in range(size.bit_length() - 1)]


def members_first(values, members, groups):
    for bit in bits_of(members):
        values = halve(values, len(values.shape) - 3, "tm", members, bit)
    for bit in bits_of(groups):
        values = add_rounded(values, trade(values, "clip", groups, bit))
    return values.astype(jnp.float32)


def groups_first(values, members, groups):
    values = halve(values, len(values.shape) - 3, "tm", members, 1)
    lead = values.shape[:-2]
    rows, columns = values.shape[-2:]
    for bit in bits_of(groups):
        values = values.reshape(lead + (2, values.shape[-2] // 2, columns))
        values = halve(values, len(lead), "clip", groups, bit)
    for bit in bits_of(members)[1:]:
        values = halve(values, len(values.shape) - 3, "tm", members, bit)
    for bit in bits_of(groups)[::-1]:
        mine = (lax.axis_index("clip") // bit) % 2
        other = trade(values, "clip", groups, bit)
        values = jnp.where(
            mine == 0, jnp.concatenate([values, other]), jnp.concatenate([other, values])
        )
    return values.astype(jnp.float32)


def sum_plain(matrices, gains, members, groups):
    split = (2,) * (members.bit_length() - 1)
    totals = []
    for place, matrix in enumerate(matrices):
        blocks = matrix.reshape(split + (matrix.shape[0] // members, matrix.shape[1]))
        totals.append((members_first, groups_first)[place % 2](blocks, members, groups))
    return tuple(totals), lax.psum(gains, ("tm", "clip"))


PART = 48
UNITS = 16
UNIT_ORDER = (8, 9, 10, 11, 12, 13, 14, 15, 7, 4, 5, 6, 3, 0, 1, 2)
LETTERS = "BBCABBBACBBBAABB"
STEPS = (
    1000, 1001, 0, 1002, 1003, 1, 8, 1004, 1005, 16, 9, 1006, 1007, 2, 32, 17,
    56, 48, 1008, 24, 40, 1009, 33, 57, 1010, 64, 3, 49, 10, 1011, 25, 18,
    41, 1012, 72, 65, 1013, 4, 1014, 80, 58, 34, 1015, 73, 11, 1016, 88, 1017,
    50, 19, 1018, 66, 89, 1019, 96, 26, 1020, 42, 35, 97, 12, 59, 5, 1021,
    104, 81, 1022, 51, 105, 1023, 112, 27, 1024, 43, 36, 113, 74, 1025, 120, 1026,
    128, 98, 52, 6, 67, 90, 121, 44, 129, 82, 99, 106, 13, 20, 28, 75,
    37, 45, 114, 53, 60, 107, 91, 68, 130, 76, 100, 83, 122, 14, 92, 131,
    108, 21, 115, 84, 77, 29, 38, 46, 93, 123, 54, 132, 116, 61, 69, 124,
    85, 101, 117, 109, 78, 94, 125, 133, 86, 118, 126,
)


def add_halves(left, right):
    return left + right


class Sums:
    def __init__(self, made, emit, s):
        self.made, self.emit = made, emit
        self.got0, self.a, self.b = s.got0, (s.a1, s.a2, s.a3, s.a4), (s.b1, s.b2, s.b3, s.b4, s.b5)
        self.send_sem, self.recv_sem = s.send_sem, s.recv_sem
        self.gain_send, self.gain_recv = s.gain_send, s.gain_recv
        self.gain_sum, self.gain_got = s.gain_sum, s.gain_got
        tm, clip = lax.axis_index("tm"), lax.axis_index("clip")
        self.core, self.x, self.low, self.high = tm % 2, (tm // 2) % 2, (tm // 4) % 2, tm // 8
        self.core_peer = (tm + 1 - 2 * self.core, clip)
        self.x_peer = (tm + 2 - 4 * self.x, clip)
        self.low_peer = (tm + 4 - 8 * self.low, clip)
        self.high_peer = (tm + 8 - 16 * self.high, clip)
        self.clip_peer = (tm, 1 - clip)
        self.peers = (self.core_peer, self.x_peer, self.low_peer, self.high_peer, self.clip_peer)
        half = D // 2
        self.mine = pl.ds(pl.multiple_of(clip * half, half), half)
        self.other = pl.ds(pl.multiple_of((1 - clip) * half, half), half)
        self.copies, self.gain_copies, self.places = {}, {}, {}
        self.started, self.left = [], set()
        self.slots = {
            place: sum((LETTERS[k] == "B") == (LETTERS[place] == "B") for k in range(place))
            for place in range(UNITS)
        }

    def meet(self):
        barrier = pltpu.get_barrier_semaphore()
        for peer in self.peers:
            pl.semaphore_signal(barrier, inc=1, device_id=peer, device_id_type=MESH)
        pl.semaphore_wait(barrier, len(self.peers))

    def send(self, src, dst, stage, place, peer):
        copy = pltpu.make_async_remote_copy(
            src_ref=src,
            dst_ref=dst,
            send_sem=self.send_sem.at[stage, place],
            recv_sem=self.recv_sem.at[stage, place],
            device_id=peer,
            device_id_type=MESH,
        )
        copy.start()
        self.places[stage, place] = len(self.started)
        self.started.append(copy)
        self.copies[stage, place] = copy

    def step(self, stage, place):
        if stage == 0:
            buffer, number = self.made(place)
            source = buffer.at[:, :, :, 1 - self.core, number]
            self.send(source, self.got0.at[place], 0, place, self.core_peer)
            return
        self.copies[stage - 1, place].wait_recv()
        if stage == 1:
            self.add_cores(place)
        step = dict(A=self.step_a, B=self.step_b, C=self.step_c)[LETTERS[place]]
        step(stage, place, self.slots[place])

    def add_cores(self, place):
        got0 = self.got0
        buffer, number = self.made(place)

        @pl.loop(0, 8)
        def _(block):
            i, j, k = block // 4, (block // 2) % 2, block % 2
            mine = buffer[i, j, k, self.core, number]
            got0[place, i, j, k] = add_halves(got0[place, i, j, k], mine)

    def step_a(self, stage, place, slot):
        got0, (a1, a2, a3, a4) = self.got0, self.a
        if stage == 1:
            source = got0.at[place, :, :, 1 - self.x]
            self.send(source, a1.at[slot], 1, place, self.x_peer)
        elif stage == 2:

            @pl.loop(0, 4)
            def _(block):
                i, j = block // 2, block % 2
                a1[slot, i, j] = add_halves(a1[slot, i, j], got0[place, i, j, self.x])

            self.send(a1.at[slot, :, 1 - self.low], a2.at[slot], 2, place, self.low_peer)
        elif stage == 3:

            @pl.loop(0, 2)
            def _(i):
                a2[slot, i] = add_halves(a2[slot, i], a1[slot, i, self.low])

            self.send(a2.at[slot, 1 - self.high], a3.at[slot], 3, place, self.high_peer)
        else:
            self.last_two(stage, place, slot, self.high)

    def step_c(self, stage, place, slot):
        got0, (a1, a2, a3, a4) = self.got0, self.a
        if stage == 1:
            source = got0.at[place, :, 1 - self.low]
            self.send(source, a1.at[slot], 1, place, self.low_peer)
        elif stage == 2:

            @pl.loop(0, 4)
            def _(block):
                i, j = block // 2, block % 2
                a1[slot, i, j] = add_halves(a1[slot, i, j], got0[place, i, self.low, j])

            self.send(a1.at[slot, 1 - self.high], a2.at[slot], 2, place, self.high_peer)
        elif stage == 3:

            @pl.loop(0, 2)
            def _(i):
                a2[slot, i] = add_halves(a2[slot, i], a1[slot, self.high, i])

            self.send(a2.at[slot, 1 - self.x], a3.at[slot], 3, place, self.x_peer)
        else:
            self.last_two(stage, place, slot, self.x)

    def last_two(self, stage, place, slot, side):
        a1, a2, a3, a4 = self.a
        if stage == 4:
            a3[slot] = add_halves(a3[slot], a2[slot, side])
            self.send(a3.at[slot], a4.at[slot], 4, place, self.clip_peer)
        else:
            total = a3[slot].astype(WIDE) + a4[slot].astype(WIDE)
            self.emit(UNIT_ORDER[place], slice(0, D), total)

    def step_b(self, stage, place, slot):
        got0, (b1, b2, b3, b4, b5) = self.got0, self.b
        if stage == 1:
            source = got0.at[place, :, :, :, :, self.other]
            self.send(source, b1.at[slot], 1, place, self.clip_peer)
        elif stage == 2:

            @pl.loop(0, 8)
            def _(block):
                i, j, k = block // 4, (block // 2) % 2, block % 2
                b1[slot, i, j, k] = add_halves(
                    b1[slot, i, j, k], got0[place, i, j, k, :, self.mine]
                )

            self.send(b1.at[slot, :, :, 1 - self.x], b2.at[slot], 2, place, self.x_peer)
        elif stage == 3:

            @pl.loop(0, 4)
            def _(block):
                i, j = block // 2, block % 2
                b2[slot, i, j] = add_halves(b2[slot, i, j], b1[slot, i, j, self.x])

            self.send(b2.at[slot, :, 1 - self.low], b3.at[slot], 3, place, self.low_peer)
        elif stage == 4:

            @pl.loop(0, 2)
            def _(i):
                b3[slot, i] = add_halves(b3[slot, i], b2[slot, i, self.low])

            self.send(b3.at[slot, 1 - self.high], b4.at[slot], 4, place, self.high_peer)
        elif stage == 5:
            b4[slot] = add_halves(b4[slot], b3[slot, self.high])
            self.send(b4.at[slot], b5.at[slot], 5, place, self.clip_peer)
        else:
            self.emit(UNIT_ORDER[place], self.mine, b4[slot].astype(WIDE))
            self.emit(UNIT_ORDER[place], self.other, b5[slot].astype(WIDE))

    def gain_step(self, number):
        if number > 0:
            self.gain_copies[number - 1].wait_recv()
            self.gain_sum[number] = self.gain_sum[number - 1] + self.gain_got[number - 1]
        if number < len(self.peers):
            copy = pltpu.make_async_remote_copy(
                src_ref=self.gain_sum.at[number],
                dst_ref=self.gain_got.at[number],
                send_sem=self.gain_send.at[number],
                recv_sem=self.gain_recv.at[number],
                device_id=self.peers[number],
                device_id_type=MESH,
            )
            copy.start()
            self.started.append(copy)
            self.gain_copies[number] = copy

    def leave(self, place):
        self.copies[0, place].wait_send()
        self.left.add(self.places[0, place])

    def finish(self):
        for number, copy in enumerate(self.started):
            if number not in self.left:
                copy.wait_send()


class BackIn(NamedTuple):
    length: Any
    x2: Any
    hidden: Any
    hidden_t: Any
    b3: Any
    x1: Any
    x: Any
    encoded_t: Any
    gain_mlp: Any
    gain_cross: Any
    gain_self: Any
    expand_w: Any
    narrow_w: Any
    cross: Layer
    own: Layer
    cross_w: Weights
    own_w: Weights


class BackOut(NamedTuple):
    output: Any
    input_grad: Any
    state_grad: Any
    summed: Any
    gains: Any


class Room(NamedTuple):
    x1: Any
    encoded_t: Any
    cross: Layer
    own: Layer
    weight: Any
    raised: Any
    ot: Any
    delta: Any
    g: Any
    x3: Any
    low: Any
    dov: Any
    dot_t: Any
    dqt: Any
    dk: Any
    dv: Any
    kept: Any
    narrow: Any
    total: Any
    got0: Any
    a1: Any
    a2: Any
    a3: Any
    a4: Any
    b1: Any
    b2: Any
    b3: Any
    b4: Any
    b5: Any
    gain_sum: Any
    gain_got: Any
    fetch_sem: Any
    raised_sem: Any
    out_sem: Any
    send_sem: Any
    recv_sem: Any
    gain_send: Any
    gain_recv: Any


class Once:
    def __init__(self, copy):
        self.copy, self.pending = copy, True
        copy.start()

    def ready(self):
        if self.pending:
            self.copy.wait()
        self.pending = False


def back_kernel(tree, *refs):
    given, out, s = jax.tree.unflatten(tree, refs)
    count = [0]

    def fetch(source, target):
        copy = pltpu.make_async_copy(source, target, s.fetch_sem.at[count[0]])
        count[0] += 1
        return Once(copy)

    def fetch_layer(source, target):
        return {
            field: fetch(getattr(source, field), getattr(target, field))
            for field in Layer._fields
            if getattr(target, field) is not None
        }

    def raised_copy(layer, pair):
        source = layer.raised.at[pl.ds(2 * pair, 2)]
        slot = pair % 2
        return pltpu.make_async_copy(
            source, s.raised.at[slot, :, pl.ds(0, source.shape[1])], s.raised_sem.at[slot]
        )

    def made(place):
        if 4 <= place < 8 or place >= 12:
            return s.narrow, place % 4
        return s.kept, place % 4 + 4 * (place >= 8)

    def keep(place, at, width, values):
        buffer, number = made(place)
        buffer[:, :, :, :, number, :, at : at + width] = values.astype(LOW).reshape(
            2, 2, 2, 2, PART, width
        )

    def emit(unit, cols, total):
        s.total[unit, :, cols] = total

    sums = Sums(made, emit, s)
    live = {}
    waits = {}

    def feed(strip, half):
        def run():
            first, second = s.weight[2 * (strip % 2)], s.weight[2 * (strip % 2) + 1]
            for name in ("hidden", "hidden_t", "b3", "x2"):
                waits[name].ready()
            width = D // 2
            at = half * width
            cols = slice(at, at + width)
            waits["first", strip].ready()
            active, slope = gelu_both(dot(s.dk[...], first[:, cols]))
            active = active.astype(LOW)
            waits["second", strip].ready()
            grad = (slope * dot_back(s.low[...], second[cols, :])).astype(LOW)
            keep(strip, at, width, dot(s.dot_t[...], grad))
            s.narrow[strip // 2, strip % 2, half] = (
                dot_rows(active, s.low[...]).astype(LOW).reshape(2, 4, PART, D)
            )
            forward, backward = dot(active, second[cols, :]), dot_back(grad, first[:, cols])
            if strip == 0 and half == 0:
                s.x3[...] = s.x1[...] + forward
                s.g[...] = backward
            else:
                s.x3[...] += forward
                s.g[...] += backward
            if strip < 2 and half:
                fetch_feed(strip + 2)

        return run

    def fetch_feed(strip):
        cols = pl.ds(strip * D, D)
        waits["first", strip] = fetch(given.expand_w.at[:, cols], s.weight[2 * (strip % 2)])
        waits["second", strip] = fetch(given.narrow_w.at[cols, :], s.weight[2 * (strip % 2) + 1])

    def feed_end():
        for place, name in enumerate(Weights._fields):
            waits["cross", name] = fetch(getattr(given.cross_w, name), s.weight[place])
        live = lax.broadcasted_iota(jnp.int32, s.x3.shape, 0) < given.length[0]
        s.dv[...] = jnp.where(live, s.x3[...], 0.0).astype(LOW)
        waits["output"] = Once(pltpu.make_async_copy(s.dv, out.output, s.out_sem.at[0]))
        part, gain_part = center_back(s.g[...], s.x1[...], given.gain_mlp[...])
        s.gain_sum[0, 2:3, :] = gain_part
        s.g[...] = s.low[...].astype(WIDE) + part
        waits["x1"] = fetch(given.x1, s.x1)

    def spread(layer, room, name):
        def run():
            waits[name, "output"].ready()
            waits[name]["inverse"].ready()
            s.low[...] = s.g[...].astype(LOW)
            waits[name, "ot"].ready()
            spread_grads(s.low[...], s.weight[0], room.inverse, s.ot, s.delta, s.dov, s.dot_t)
            if name == "cross":
                waits["own", "output"] = fetch(given.own_w.output, s.weight[0])

        return run

    def output_grad(room, name, place):
        def run():
            if name == "own":
                for unit in range(4, 8):
                    sums.leave(unit)
            mixed = s.ot[...].astype(LOW)
            for at, width in strips(D, 256):
                keep(place, at, width, dot(mixed, s.low[:, at : at + width]))
            if name == "cross":
                waits["own", "ot"] = fetch(given.own.ot, s.ot)

        return run

    def attention(layer, room, name, first):
        def run():
            for field in ("q", "kt", "v"):
                waits[name][field].ready()
            waits["output"].ready()
            inner = layer.raised.shape[1]

            @pl.loop(first, first + 2)
            def _(pair):
                raised_copy(layer, pair).wait()
                slot = pair % 2
                attend_pair(
                    pair,
                    room.q,
                    room.kt,
                    room.v,
                    s.raised.at[slot, :, pl.ds(0, inner)],
                    s.delta,
                    s.dot_t,
                    s.dov,
                    s.dqt,
                    s.dk.at[pl.ds(0, inner)],
                    s.dv.at[pl.ds(0, inner)],
                )
                if first < PAIRS - 2:
                    raised_copy(layer, pair + 2).start()
                elif name == "cross":
                    raised_copy(given.own, slot).start()

        return run

    def strip_grads(first_t, second_t, inner, strip, place):
        cols = slice(256 * strip, 256 * (strip + 1))
        part = s.dqt[cols, :].T
        s.low[:, cols] = part
        keep(place, 0, 256, dot(first_t[...], part))
        keep(place, 256, 256, dot(second_t[...], s.dk[0:inner, cols]))
        keep(place, 512, 256, dot(second_t[...], s.dv[0:inner, cols]))

    def cross_grads(strip):
        def run():
            waits["cross"]["ht"].ready()
            waits["encoded_t"].ready()
            strip_grads(s.cross.ht, s.encoded_t, s.encoded_t.shape[1], strip, 9 + strip)

        return run

    def cross_inputs():
        for name in ("query", "key", "value"):
            waits["cross", name].ready()
        waits["x1"].ready()
        frames = s.encoded_t.shape[1]
        for at, width in strips(D, 256):
            cols = slice(at, at + width)
            s.x3[0:frames, cols] = dot_back(s.dk[0:frames, :], s.weight[2][cols, :]) + dot_back(
                s.dv[0:frames, :], s.weight[3][cols, :]
            )
        state = s.x3.at[pl.ds(0, frames)]
        waits["state"] = Once(pltpu.make_async_copy(state, out.state_grad, s.out_sem.at[1]))
        part, gain_part = center_back(
            dot_back(s.low[...], s.weight[1][...]), s.x1[...], given.gain_cross[...]
        )
        s.gain_sum[0, 1:2, :] = gain_part
        s.g[...] += part
        for place, name in enumerate(Weights._fields):
            if place:
                waits["own", name] = fetch(getattr(given.own_w, name), s.weight[place])

    def self_grads(strip):
        def run():
            waits["own"]["ht"].ready()
            strip_grads(s.own.ht, s.own.ht, s.own.ht.shape[1], strip, 13 + strip)
            if strip == 2:
                waits["x"] = fetch(given.x, s.dov)

        return run

    def self_inputs():
        for name in ("query", "key", "value"):
            waits["own", name].ready()
        waits["x"].ready()
        for at, width in strips(D, 256):
            cols = slice(at, at + width)
            s.x1[:, cols] = (
                dot_back(s.low[...], s.weight[1][cols, :])
                + dot_back(s.dk[...], s.weight[2][cols, :])
                + dot_back(s.dv[...], s.weight[3][cols, :])
            )
        part, gain_part = center_back(s.x1[...], s.dov[...].astype(WIDE), given.gain_self[...])
        s.gain_sum[0, 0:1, :] = gain_part
        s.g[...] += part
        waits["input"] = Once(pltpu.make_async_copy(s.g, out.input_grad, s.out_sem.at[2]))

    pieces = [feed(strip, half) for strip in range(4) for half in range(2)]
    pieces += [feed_end, spread(given.cross, s.cross, "cross"), output_grad(s.cross, "cross", 8)]
    for strip in range(3):
        pieces += [attention(given.cross, s.cross, "cross", 2 * strip), cross_grads(strip)]
    pieces += [cross_inputs, spread(given.own, s.own, "own"), output_grad(s.own, "own", 12)]
    for strip in range(3):
        pieces += [attention(given.own, s.own, "own", 2 * strip), self_grads(strip)]
    pieces.append(self_inputs)
    waits["hidden"] = fetch(given.hidden, s.dk)
    fetch_feed(0)
    waits["b3"] = fetch(given.b3, s.low)
    waits["hidden_t"] = fetch(given.hidden_t, s.dot_t)
    waits["x2"] = fetch(given.x2, s.x1)
    fetch_feed(1)
    waits["cross"] = fetch_layer(given.cross, s.cross)
    waits["cross", "ot"] = fetch(given.cross.ot, s.ot)
    raised_copy(given.cross, 0).start()
    raised_copy(given.cross, 1).start()
    waits["encoded_t"] = fetch(given.encoded_t, s.encoded_t)
    waits["own"] = fetch_layer(given.own, s.own)
    s.gain_sum[0] = jnp.zeros(s.gain_sum.shape[1:], WIDE)
    met = False
    for code in STEPS:
        if code < 1000:
            if not met:
                sums.meet()
                met = True
            if code < UNITS * 8:
                sums.step(code % 8, code // 8)
            else:
                sums.gain_step(code % 8)
        else:
            pieces[code - 1000]()
    out.gains[...] = s.gain_sum[5]
    result = pltpu.make_async_copy(s.total, out.summed, s.out_sem.at[3])
    result.start()
    sums.finish()
    waits["state"].ready()
    waits["input"].ready()
    result.wait()


def room_for(given):
    rows, frames = given.x.shape[0], given.encoded_t.shape[1]
    split = (2, 2, 2, 2)
    thin = LETTERS.count("B")
    thick = UNITS - thin
    half = D // 2

    def low(*shape):
        return pltpu.VMEM(shape, LOW)

    def wide(*shape):
        return pltpu.VMEM(shape, WIDE)

    def like(array):
        return pltpu.VMEM(array.shape, array.dtype)

    def layer(source):
        return jax.tree.map(like, source)._replace(raised=None, ot=None)

    plain, turned = (rows, D), (D, rows)
    dma = pltpu.SemaphoreType.DMA
    return Room(
        x1=like(given.x1), encoded_t=like(given.encoded_t),
        cross=layer(given.cross), own=layer(given.own),
        weight=[low(D, D)] * 4, raised=low(2, 2, rows, rows), ot=wide(*turned),
        delta=like(given.own.inverse),
        g=wide(*plain), x3=wide(*plain), low=low(*plain), dov=low(*plain), dot_t=low(*turned),
        dqt=low(*turned), dk=low(*plain), dv=low(*plain),
        kept=low(*split, 8, PART, D), narrow=low(*split, 4, PART, D),
        total=wide(UNITS, PART, D), got0=low(UNITS, 2, 2, 2, PART, D),
        a1=low(thick, 2, 2, PART, D), a2=low(thick, 2, PART, D), a3=low(thick, PART, D),
        a4=low(thick, PART, D), b1=low(thin, 2, 2, 2, PART, half), b2=low(thin, 2, 2, PART, half),
        b3=low(thin, 2, PART, half), b4=low(thin, PART, half), b5=low(thin, PART, half),
        gain_sum=wide(6, 8, D), gain_got=wide(5, 8, D),
        fetch_sem=dma((40,)), raised_sem=dma((2,)), out_sem=dma((4,)),
        send_sem=dma((6, UNITS)), recv_sem=dma((6, UNITS)), gain_send=dma((5,)),
        gain_recv=dma((5,)),
    )


def backward_and_sum(given):
    rows, frames = given.x.shape[0], given.encoded_t.shape[1]
    outs = BackOut(
        output=shape_of((rows, D)), input_grad=shape_of((rows, D), WIDE),
        state_grad=shape_of((frames, D), WIDE), summed=shape_of((UNITS, PART, D), WIDE),
        gains=shape_of((8, D), WIDE),
    )
    room = room_for(given)
    places = jax.tree.map(lambda _: FAR, given)._replace(
        length=NUMBERS, gain_mlp=INSIDE, gain_cross=INSIDE, gain_self=INSIDE
    )
    results = pl.pallas_call(
        functools.partial(back_kernel, jax.tree.structure((given, outs, room))),
        out_shape=tuple(outs),
        in_specs=jax.tree.leaves(places),
        out_specs=(FAR,) * 4 + (INSIDE,),
        scratch_shapes=jax.tree.leaves(room),
        compiler_params=pltpu.CompilerParams(
            collective_id=0, has_side_effects=True, vmem_limit_bytes=63 * 2**20
        ),
    )(*jax.tree.leaves(given))
    return BackOut(*results)


def cut(matrix, strip):
    return matrix.at[:, pl.ds(256 * strip, 256)]


def finish_kernel(output, input_grad, state_grad, summed, *refs):
    outs, (rows_low, rows_wide, frames_wide, blocks, taken, given) = refs[:13], refs[13:]
    parts = [
        (summed.at[pl.ds(0, 8)], blocks.at[pl.ds(0, 8)]),
        (summed.at[pl.ds(8, 8)], blocks.at[pl.ds(8, 8)]),
        (input_grad, rows_wide),
        (state_grad, frames_wide),
        (output, rows_low),
    ]
    results = [
        [(blocks.at[3], outs[6]), (blocks.at[7], outs[10])]
        + [
            (blocks.at[4 * layer + k, :, pl.ds(256 * m, 256)], cut(outs[3 + 4 * layer + m], k))
            for layer in range(2)
            for k in range(3)
            for m in range(3)
        ],
        [(blocks.at[pl.ds(12, 4)], outs[12])]
        + [(blocks.at[8 + k], outs[11].at[:, pl.ds(k * D, D)]) for k in range(4)],
        [(rows_wide, outs[1])],
        [(frames_wide, outs[2])],
        [(rows_low, outs[0])],
    ]
    arriving = [
        pltpu.make_async_copy(*pair, taken.at[place]) for place, pair in enumerate(parts)
    ]
    for copy in arriving:
        copy.start()
    leaving = []
    for copy, pairs in zip(arriving, results):
        copy.wait()
        for pair in pairs:
            leaving.append(pltpu.make_async_copy(*pair, given.at[len(leaving)]))
            leaving[-1].start()
    for copy in leaving:
        copy.wait()


def finish(made):
    outs = [shape_of(made[k].shape, made[k].dtype) for k in range(3)]
    outs += [shape_of((PART, D), WIDE)] * 8
    outs += [shape_of((PART, 4 * D), WIDE), shape_of((4, PART, D), WIDE)]
    *results, narrow = pl.pallas_call(
        finish_kernel,
        out_shape=tuple(outs),
        in_specs=[FAR] * 4,
        out_specs=(FAR,) * len(outs),
        scratch_shapes=[pltpu.VMEM(array.shape, array.dtype) for array in made[:4]]
        + [pltpu.SemaphoreType.DMA((5,)), pltpu.SemaphoreType.DMA((28,))],
        compiler_params=parameters(62),
    )(*made[:4])
    return *results, narrow.reshape(4 * PART, D)


def body(
    members,
    groups,
    mel_frames,
    conv_first,
    conv_second,
    enc_projection,
    enc_output,
    enc_expand,
    enc_narrow,
    dec_input,
    lengths,
    self_query,
    self_key,
    self_value,
    self_output,
    cross_query,
    cross_key,
    cross_value,
    cross_output,
    mlp_expand,
    mlp_narrow,
    gain_self,
    gain_cross,
    gain_mlp,
    cotangent,
):
    inputs, length = dec_input[0, 0], lengths[0]
    own_w = Weights(self_output, self_query, self_key, self_value)
    x1, own, mel = self_forward(length, inputs, gain_self, mel_frames[:, 0], members, own_w)
    encoded, encoded_t = encode(
        mel, conv_first, conv_second, enc_projection, enc_output, enc_expand, enc_narrow
    )
    cross_w = Weights(cross_output, cross_query, cross_key, cross_value)
    x2, hidden, hidden_t, b3, cross = cross_forward(
        length, x1, encoded, cotangent[0, 0], gain_cross, gain_mlp, cross_w
    )
    if (members, groups) == (16, 2):
        made = backward_and_sum(
            BackIn(
                length, x2, hidden, hidden_t, b3, x1, inputs, encoded_t,
                gain_mlp, gain_cross, gain_self, mlp_expand, mlp_narrow,
                cross, own, cross_w, own_w,
            )
        )
        dec_output, dec_input_grad, enc_state_grad, *totals = finish(made)
        gains = made.gains
    else:
        dec_output, g2, g_gain_mlp, g_expand, g_narrow = feed_both(
            length, x2, hidden, hidden_t, b3, gain_mlp, mlp_expand, mlp_narrow
        )
        g1, g_gain_cross, enc_state_grad, *cross_grads = cross_backward(
            (g2, x1, gain_cross) + tuple(cross) + (encoded_t,), cross_w
        )
        dec_input_grad, g_gain_self, *self_grads = self_backward(
            (g1, inputs, gain_self) + tuple(own), own_w
        )
        gains = jnp.concatenate([g_gain_self, g_gain_cross, g_gain_mlp, jnp.zeros((5, D), WIDE)])
        totals, gains = sum_plain(
            self_grads + cross_grads + [g_expand, g_narrow], gains, members, groups
        )
    part = D // members
    gains = lax.dynamic_slice_in_dim(gains, lax.axis_index("tm") * part, part, 1)
    return (
        encoded[None, None],
        dec_output[None, None],
        dec_input_grad[None, None],
        enc_state_grad[None, None],
        *totals,
        gains[0],
        gains[1],
        gains[2],
    )


def solution(mesh):
    placed = (
        P("tm", "clip", None, None),
        P(),
        P(),
        P(),
        P(),
        P(),
        P(),
        P("clip", "tm", None, None),
        P("clip", "tm"),
        P(),
        P(),
        P(),
        P(),
        P(),
        P(),
        P(),
        P(),
        P(),
        P(),
        P(),
        P(),
        P(),
        P("clip", "tm", None, None),
    )
    return jax.shard_map(
        functools.partial(body, mesh.shape["tm"], mesh.shape["clip"]),
        mesh=mesh,
        in_specs=placed,
        out_specs=(
            P("clip", "tm", None, None),
            P("clip", "tm", None, None),
            P("clip", "tm", None, None),
            P("clip", "tm", None, None),
            P("tm", None),
            P("tm", None),
            P("tm", None),
            P("tm", None),
            P("tm", None),
            P("tm", None),
            P("tm", None),
            P("tm", None),
            P("tm", None),
            P("tm", None),
            P("tm"),
            P("tm"),
            P("tm"),
        ),
        check_vma=False,
    )
```

```python
import functools
import math
from typing import Any, NamedTuple

import jax
import jax.numpy as jnp
import numpy as np
from jax import lax
from jax.experimental import pallas as pl
from jax.experimental.pallas import tpu as pltpu
from jax.sharding import PartitionSpec as P

D = 768
HEADS = 12
HD = 64
PAIRS = HEADS // 2
LANES = 2 * HD
SCALE = HD ** (-0.5)
LOW = jnp.bfloat16
WIDE = jnp.float32
INSIDE = pl.BlockSpec(memory_space=pltpu.VMEM)
FAR = pl.BlockSpec(memory_space=pltpu.HBM)
MESH = pl.DeviceIdType.MESH
NUMBERS = pl.BlockSpec(memory_space=pltpu.SMEM)


def shape_of(shape, kind=LOW):
    return jax.ShapeDtypeStruct(shape, kind)


def parameters(megabytes=58):
    return pltpu.CompilerParams(vmem_limit_bytes=megabytes * 2**20)


def center(values):
    shifted = values - jnp.mean(values, axis=-1, keepdims=True)
    spread = jnp.mean(shifted * shifted, axis=-1, keepdims=True)
    root = lax.rsqrt(spread + 1e-05)
    return shifted * root, root


def center_back(gradient, values, gain):
    normed, root = center(values)
    inner = gradient * gain
    first = jnp.mean(inner, axis=-1, keepdims=True)
    second = jnp.mean(inner * normed, axis=-1, keepdims=True)
    gain_part = jnp.sum(gradient * normed, axis=0, keepdims=True)
    return root * (inner - first - normed * second), gain_part


def gelu(values):
    return values * (0.5 + 0.5 * lax.erf(values * 2**-0.5))


def gelu_both(values):
    area = 0.5 + 0.5 * lax.erf(values * 2**-0.5)
    slope = area + values * ((2 * math.pi) ** -0.5 * jnp.exp(-0.5 * values * values))
    return values * area, slope


def dot(left, right):
    return jnp.dot(left, right, preferred_element_type=WIDE)


def dot_back(left, right):
    return lax.dot_general(left, right, (((1,), (1,)), ((), ())), preferred_element_type=WIDE)


def dot_rows(left, right):
    return lax.dot_general(left, right, (((0,), (0,)), ((), ())), preferred_element_type=WIDE)


def strips(total, width):
    return [(at, min(width, total - at)) for at in range(0, total, width)]


class Fetch:
    def __init__(self, sources, targets, semaphores):
        self.copies = [
            pltpu.make_async_copy(source, target, semaphores.at[place])
            for place, (source, target) in enumerate(zip(sources, targets))
        ]
        for copy in self.copies:
            copy.start()

    def wait(self, place):
        self.copies[place].wait()


def pair_lanes(pair):
    return pl.ds(pl.multiple_of(pair * LANES, LANES), LANES)


def head_rows(pair, side):
    return pl.ds(pl.multiple_of(pair * LANES + side * HD, HD), HD)


def attend(
    q_ref, k_ref, vt_ref, bias_ref, ot_ref, inverse_ref=None, raised_ref=None, leave=None
):
    ones = jnp.ones((16, vt_ref.shape[1]), LOW)

    @pl.loop(0, PAIRS, step=2)
    def _(first):
        heads = [(first + more, side) for more in range(2) for side in range(2)]
        cuts = [slice(side * HD, (side + 1) * HD) for _, side in heads]
        queries = [q_ref[:, pair_lanes(first + more)] for more in range(2)]
        keys = [k_ref[:, pair_lanes(first + more)] for more in range(2)]
        scores = [dot_back(keys[k // 2][:, cuts[k]], queries[k // 2][:, cuts[k]]) for k in range(4)]
        if bias_ref is not None:
            scores = [part + bias_ref[...] for part in scores]
        raised = [
            jnp.exp(part - jnp.max(part, axis=0, keepdims=True)).astype(LOW) for part in scores
        ]
        rows = [head_rows(pair, side) for pair, side in heads]
        mixed = [
            dot(jnp.concatenate([vt_ref[rows[k], :], ones], axis=0), raised[k]) for k in range(4)
        ]
        for k, (pair, side) in enumerate(heads):
            inverse = 1.0 / mixed[k][HD : HD + 1]
            ot_ref[rows[k], :] = mixed[k][:HD] * inverse
            if raised_ref is not None:
                raised_ref[2 * pair + side] = raised[k]
                inverse_ref[2 * pair + side] = jnp.broadcast_to(inverse, inverse_ref.shape[1:])
        if leave is not None:
            leave(first)
            leave(first + 1)


def attend_pair(
    pair, q_ref, kt_ref, v_ref, raised_ref, delta_ref, dot_ref, dov_ref, dqt_ref, dk_ref, dv_ref
):
    lanes = pair_lanes(pair)
    queries, values, grads = q_ref[:, lanes], v_ref[:, lanes], dov_ref[:, lanes]
    sides = range(2)
    rows = [head_rows(pair, side) for side in sides]
    cuts = [slice(side * HD, (side + 1) * HD) for side in sides]
    products = [dot(values[:, cuts[side]], dot_ref[rows[side], :]) for side in sides]
    value_sides = [dot(raised_ref[side], grads[:, cuts[side]]) for side in sides]
    score_grads = [
        (
            raised_ref[side].astype(WIDE)
            * (products[side] - delta_ref[2 * pair + side, 0:1, :])
        ).astype(LOW)
        for side in sides
    ]
    key_sides = [dot(score_grads[side], queries[:, cuts[side]]) for side in sides]
    query_sides = [dot(kt_ref[rows[side], :], score_grads[side]) for side in sides]
    for side in sides:
        dqt_ref[rows[side], :] = (query_sides[side] * SCALE).astype(LOW)
    dk_ref[:, lanes] = jnp.concatenate(key_sides, axis=1).astype(LOW)
    dv_ref[:, lanes] = jnp.concatenate(value_sides, axis=1).astype(LOW)


def attend_back(q_ref, kt_ref, v_ref, raised_ref, *rest):
    @pl.loop(0, PAIRS)
    def _(pair):
        attend_pair(pair, q_ref, kt_ref, v_ref, raised_ref.at[pl.ds(2 * pair, 2)], *rest)


def encoder_kernel(
    mel_ref, position_ref, first_h, second_h, joint_h, output_h, expand_h, narrow_h,
    out_ref, out_t_ref,
    first_w, second_w, joint_w, output_w, expand_w, narrow_w,
    even, odd, state, hidden, q, k, vt, mixed_t, semaphores,
):
    length = out_ref.shape[0]
    fetch = Fetch(
        (first_h, second_h, joint_h, output_h, expand_h, narrow_h),
        (first_w, second_w, joint_w, output_w, expand_w, narrow_w),
        semaphores,
    )
    taps = [mel_ref[pl.ds(7 + tap, length, stride=2), :].astype(LOW) for tap in range(4)]
    fetch.wait(0)
    for at, width in strips(D, 256):
        cols = pl.ds(at, width)
        for start, target in ((0, even), (1, odd)):
            total = sum(dot(taps[start + o], first_w[o, :, cols]) for o in range(3))
            target[:, cols] = gelu(total).astype(LOW)
    fetch.wait(1)
    ranks = lax.broadcasted_iota(jnp.int32, (length, 256), 0)
    for at, width in strips(D, 256):
        cols = pl.ds(at, width)
        before = pltpu.roll(dot(odd[...], second_w[0, :, cols]), 1, 0)
        total = dot(even[...], second_w[1, :, cols]) + dot(odd[...], second_w[2, :, cols])
        total = total + jnp.where(ranks == 0, 0.0, before)
        state[:, cols] = gelu(total) + position_ref[:, cols]
    hidden[...] = center(state[...])[0].astype(LOW)
    fetch.wait(2)
    for at, width in strips(D, 256):
        cols = pl.ds(at, width)
        q[:, cols] = (dot(hidden[...], joint_w[:, cols]).astype(LOW) * SCALE).astype(LOW)
        k[:, cols] = dot(hidden[...], joint_w[:, pl.ds(D + at, width)]).astype(LOW)
        vt[cols, :] = dot(hidden[...], joint_w[:, pl.ds(2 * D + at, width)]).astype(LOW).T
    attend(q, k, vt, None, mixed_t)
    fetch.wait(3)
    mixed = mixed_t[...].astype(LOW).T
    for at, width in strips(D, 256):
        cols = pl.ds(at, width)
        state[:, cols] += dot(mixed, output_w[:, cols])
    hidden[...] = center(state[...])[0].astype(LOW)
    fetch.wait(4)
    fetch.wait(5)

    @pl.loop(0, expand_w.shape[1] // 1024)
    def _(strip):
        parts = [pl.ds(pl.multiple_of(strip * 1024 + at, 512), 512) for at in (0, 512)]
        widened = [gelu(dot(hidden[...], expand_w[:, cols])).astype(LOW) for cols in parts]
        first, second = [dot(part, narrow_w[cols, :]) for part, cols in zip(widened, parts)]
        state[...] += first + second

    encoded = center(state[...])[0].astype(LOW)
    out_ref[...] = encoded
    out_t_ref[...] = encoded.T


def encode(mel, conv_first, conv_second, enc_projection, enc_output, enc_expand, enc_narrow):
    length = (mel.shape[0] - 16) // 2
    weights = (conv_first, conv_second, enc_projection, enc_output, enc_expand, enc_narrow)
    return pl.pallas_call(
        encoder_kernel,
        out_shape=(shape_of((length, D)), shape_of((D, length))),
        in_specs=[INSIDE] * 2 + [FAR] * 6,
        out_specs=(INSIDE, INSIDE),
        scratch_shapes=[pltpu.VMEM(weight.shape, LOW) for weight in weights]
        + [
            pltpu.VMEM((length, D), LOW),
            pltpu.VMEM((length, D), LOW),
            pltpu.VMEM((length, D), WIDE),
            pltpu.VMEM((length, D), LOW),
            pltpu.VMEM((length, D), LOW),
            pltpu.VMEM((length, D), LOW),
            pltpu.VMEM((D, length), LOW),
            pltpu.VMEM((D, length), WIDE),
            pltpu.SemaphoreType.DMA((6,)),
        ],
        compiler_params=parameters(),
    )(mel, sinusoids(length, D), *weights)


def sinusoids(length, features):
    halfway = features // 2
    inverse = np.exp(-math.log(10000.0) / (halfway - 1) * np.arange(halfway)).astype(np.float32)
    angles = np.arange(length, dtype=np.float32)[:, None] * inverse[None, :]
    angles = angles.astype(np.float64)
    return jnp.asarray(np.concatenate([np.sin(angles), np.cos(angles)], axis=1).astype(np.float32))


class Layer(NamedTuple):
    ht: Any
    q: Any
    kt: Any
    v: Any
    raised: Any
    inverse: Any
    ot: Any


class Weights(NamedTuple):
    output: Any
    query: Any
    key: Any
    value: Any


class Leave:
    def __init__(self, held, targets, semaphores):
        self.pairs, self.semaphores, self.started = list(zip(held, targets)), semaphores, []

    def __call__(self, *places):
        for place in places:
            copy = pltpu.make_async_copy(*self.pairs[place], self.semaphores.at[place])
            copy.start()
            self.started.append(copy)

    def scores(self, place, first):
        def copy(pair):
            held, target = self.pairs[place]
            heads = pl.ds(2 * pair, 2)
            return pltpu.make_async_copy(
                held.at[heads], target.at[heads], self.semaphores.at[first + pair]
            )

        self.started += [copy(pair) for pair in range(PAIRS)]
        return lambda pair: copy(pair).start()

    def finish(self):
        for copy in self.started:
            copy.wait()


def self_kernel(
    members, length_ref, x_ref, gain_ref, mel_h, output_h, query_h, key_h, value_h, *refs
):
    outs, held = refs[:9], refs[9:18]
    output_w, query_w, key_w, value_w, hidden, k, vt, bias = refs[18:26]
    semaphores, out_sem, own_sem, send_sem, recv_sem = refs[26:]
    x1, ht, q, kt, v, raised, inverse, ot, mel = held
    leave = Leave(held, outs, out_sem)
    tm, clip = lax.axis_index("tm"), lax.axis_index("clip")
    barrier = pltpu.get_barrier_semaphore()

    @pl.loop(1, members)
    def _(step):
        peer = (lax.rem(tm + step, members), clip)
        pl.semaphore_signal(barrier, inc=1, device_id=peer, device_id_type=MESH)

    fetch = Fetch(
        (query_h, key_h, value_h, output_h), (query_w, key_w, value_w, output_w), semaphores
    )
    rows = x_ref.shape[0]
    hidden[...] = (center(x_ref[...].astype(WIDE))[0] * gain_ref[...]).astype(LOW)
    keys = lax.broadcasted_iota(jnp.int32, (rows, rows), 0)
    queries = lax.broadcasted_iota(jnp.int32, (rows, rows), 1)
    allowed = (keys <= queries) & (keys < length_ref[0])
    bias[...] = jnp.where(allowed, 0.0, -1e30)
    fetch.wait(0)
    fetch.wait(1)
    fetch.wait(2)
    for at, width in strips(D, 256):
        cols = pl.ds(at, width)
        q[:, cols] = (dot(hidden[...], query_w[:, cols]).astype(LOW) * SCALE).astype(LOW)
        part = dot(hidden[...], key_w[:, cols]).astype(LOW)
        k[:, cols] = part
        kt[cols, :] = part.T
        part = dot(hidden[...], value_w[:, cols]).astype(LOW)
        v[:, cols] = part
        vt[cols, :] = part.T
    ht[...] = hidden[...].T
    leave(1, 2, 3, 4)
    pl.semaphore_wait(barrier, members - 1)
    frames = mel_h.shape[1]
    place = pl.ds(pl.multiple_of(8 + tm * frames, 8), frames)

    def pass_on(step):
        peer = lax.rem(tm + step, members)
        return pltpu.make_async_remote_copy(
            src_ref=mel_h.at[peer],
            dst_ref=mel.at[place],
            send_sem=send_sem.at[step],
            recv_sem=recv_sem.at[step],
            device_id=(peer, clip),
            device_id_type=MESH,
        )

    @pl.loop(1, members)
    def _(step):
        pass_on(step).start()

    stay = pltpu.make_async_copy(mel_h.at[tm], mel.at[place], own_sem)
    stay.start()
    mel[0:8, :] = jnp.zeros((8, mel.shape[1]), WIDE)
    mel[mel.shape[0] - 8 :, :] = jnp.zeros((8, mel.shape[1]), WIDE)
    attend(q, k, vt, bias, ot, inverse, raised, leave.scores(5, 9))
    leave(6, 7)
    fetch.wait(3)
    mixed = ot[...].astype(LOW).T
    for at, width in strips(D, 256):
        cols = pl.ds(at, width)
        x1[:, cols] = x_ref[:, cols].astype(WIDE) + dot(mixed, output_w[:, cols])
    leave(0)

    @pl.loop(1, members)
    def _(step):
        pass_on(step).wait()

    stay.wait()
    leave(8)
    leave.finish()


def held_like(shapes):
    return [pltpu.VMEM(shape.shape, shape.dtype) for shape in shapes]


def self_forward(lengths, inputs, gain, mel_frames, members, weights):
    rows = inputs.shape[0]
    mel = jnp.transpose(mel_frames.astype(WIDE), (1, 0, 2))
    arrived = (members * mel.shape[1] + 16, mel.shape[2])
    plain, turned = (rows, D), (D, rows)
    outs = (
        shape_of(plain, WIDE), shape_of(turned), shape_of(plain), shape_of(turned),
        shape_of(plain), shape_of((HEADS, rows, rows)), shape_of((HEADS, 8, rows), WIDE),
        shape_of(turned, WIDE), shape_of(arrived, WIDE),
    )
    x1, *layer, arrived = pl.pallas_call(
        functools.partial(self_kernel, members),
        out_shape=outs,
        in_specs=[NUMBERS, INSIDE, INSIDE] + [FAR] * 5,
        out_specs=(FAR,) * 9,
        scratch_shapes=held_like(outs)
        + [pltpu.VMEM((D, D), LOW)] * 4
        + [
            pltpu.VMEM(plain, LOW),
            pltpu.VMEM(plain, LOW),
            pltpu.VMEM(turned, LOW),
            pltpu.VMEM((rows, rows), WIDE),
            pltpu.SemaphoreType.DMA((4,)),
            pltpu.SemaphoreType.DMA((9 + PAIRS,)),
            pltpu.SemaphoreType.DMA(()),
            pltpu.SemaphoreType.DMA((members,)),
            pltpu.SemaphoreType.DMA((members,)),
        ],
        compiler_params=pltpu.CompilerParams(
            collective_id=1, has_side_effects=True, vmem_limit_bytes=58 * 2**20
        ),
    )(lengths, inputs, gain, mel, *weights)
    return x1, Layer(*layer), arrived


def cross_kernel(
    length_ref, x1_ref, encoded_ref, cotangent_ref, gain_cross_ref, gain_mlp_ref,
    output_h, query_h, key_h, value_h, *refs
):
    outs, held = refs[:11], refs[11:22]
    output_w, query_w, key_w, value_w, k, vt, semaphores, out_sem = refs[22:]
    x2, hidden, hidden_t, b3, ht, q, kt, v, raised, inverse, ot = held
    leave = Leave(held, outs, out_sem)
    fetch = Fetch(
        (query_h, key_h, value_h, output_h), (query_w, key_w, value_w, output_w), semaphores
    )
    rows = x1_ref.shape[0]
    hidden[...] = (center(x1_ref[...])[0] * gain_cross_ref[...]).astype(LOW)
    fetch.wait(0)
    fetch.wait(1)
    fetch.wait(2)
    for at, width in strips(D, 256):
        cols = pl.ds(at, width)
        q[:, cols] = (dot(hidden[...], query_w[:, cols]).astype(LOW) * SCALE).astype(LOW)
        part = dot(encoded_ref[...], key_w[:, cols]).astype(LOW)
        k[:, cols] = part
        kt[cols, :] = part.T
        part = dot(encoded_ref[...], value_w[:, cols]).astype(LOW)
        v[:, cols] = part
        vt[cols, :] = part.T
    ht[...] = hidden[...].T
    live = lax.broadcasted_iota(jnp.int32, (rows, D), 0) < length_ref[0]
    b3[...] = jnp.where(live, cotangent_ref[...].astype(WIDE), 0.0).astype(LOW)
    leave(3, 4, 5, 6, 7)
    attend(q, k, vt, None, ot, inverse, raised, leave.scores(8, 11))
    leave(9, 10)
    fetch.wait(3)
    mixed = ot[...].astype(LOW).T
    for at, width in strips(D, 256):
        cols = pl.ds(at, width)
        x2[:, cols] = x1_ref[:, cols] + dot(mixed, output_w[:, cols])
    leave(0)
    hidden[...] = (center(x2[...])[0] * gain_mlp_ref[...]).astype(LOW)
    leave(1)
    hidden_t[...] = hidden[...].T
    leave(2)
    leave.finish()


def cross_forward(lengths, x1, encoded, cotangent, gain_cross, gain_mlp, weights):
    rows, frames = x1.shape[0], encoded.shape[0]
    plain, turned = (rows, D), (D, rows)
    outs = (
        shape_of(plain, WIDE), shape_of(plain), shape_of(turned), shape_of(plain),
        shape_of(turned), shape_of(plain), shape_of((D, frames)), shape_of((frames, D)),
        shape_of((HEADS, frames, rows)), shape_of((HEADS, 8, rows), WIDE),
        shape_of(turned, WIDE),
    )
    x2, hidden, hidden_t, b3, *layer = pl.pallas_call(
        cross_kernel,
        out_shape=outs,
        in_specs=[NUMBERS] + [INSIDE] * 5 + [FAR] * 4,
        out_specs=(FAR,) * 11,
        scratch_shapes=held_like(outs)
        + [pltpu.VMEM(weight.shape, LOW) for weight in weights]
        + [
            pltpu.VMEM((frames, D), LOW),
            pltpu.VMEM((D, frames), LOW),
            pltpu.SemaphoreType.DMA((4,)),
            pltpu.SemaphoreType.DMA((11 + PAIRS,)),
        ],
        compiler_params=parameters(),
    )(lengths, x1, encoded, cotangent, gain_cross, gain_mlp, *weights)
    return x2, hidden, hidden_t, b3, Layer(*layer)


def feed_kernel(
    length_ref, x2_ref, hidden, hidden_t, b3, gain_ref, expand_h, narrow_h,
    out_ref, g2_ref, gain_grad_ref, expand_grad_ref, narrow_grad_ref,
    expand_w, narrow_w, x3, back, semaphores,
):
    fetch = Fetch((expand_h, narrow_h), (expand_w, narrow_w), semaphores)
    x3[...] = x2_ref[...]
    back[...] = jnp.zeros_like(back)
    fetch.wait(0)
    fetch.wait(1)

    @pl.loop(0, expand_w.shape[1] // 512)
    def _(strip):
        cols = pl.ds(pl.multiple_of(strip * 512, 512), 512)
        active, slope = gelu_both(dot(hidden[...], expand_w[:, cols]))
        active = active.astype(LOW)
        grad = (slope * dot_back(b3[...], narrow_w[cols, :])).astype(LOW)
        x3[...] += dot(active, narrow_w[cols, :])
        narrow_grad_ref[cols, :] = dot_rows(active, b3[...]).astype(LOW)
        expand_grad_ref[:, cols] = dot(hidden_t[...], grad).astype(LOW)
        back[...] += dot_back(grad, expand_w[:, cols])

    live = lax.broadcasted_iota(jnp.int32, x3.shape, 0) < length_ref[0]
    out_ref[...] = jnp.where(live, x3[...], 0.0).astype(LOW)
    part, gain_part = center_back(back[...], x2_ref[...], gain_ref[...])
    gain_grad_ref[...] = gain_part
    g2_ref[...] = b3[...].astype(WIDE) + part


def feed_both(lengths, x2, hidden, hidden_t, b3, gain_mlp, expand, narrow):
    plain = x2.shape
    return pl.pallas_call(
        feed_kernel,
        out_shape=(
            shape_of(plain), shape_of(plain, WIDE), shape_of((1, D), WIDE),
            shape_of(expand.shape), shape_of(narrow.shape),
        ),
        in_specs=[NUMBERS] + [INSIDE] * 5 + [FAR] * 2,
        out_specs=(INSIDE,) * 5,
        scratch_shapes=[
            pltpu.VMEM(expand.shape, LOW),
            pltpu.VMEM(narrow.shape, LOW),
            pltpu.VMEM(plain, WIDE),
            pltpu.VMEM(plain, WIDE),
            pltpu.SemaphoreType.DMA((2,)),
        ],
        compiler_params=parameters(),
    )(lengths, x2, hidden, hidden_t, b3, gain_mlp, expand, narrow)


def spread_grads(out_grad, output_w, inverse_ref, ot_ref, delta_ref, dov, dot_t):
    for at, width in strips(D, 256):
        part = dot_back(out_grad, output_w[at : at + width, :]).astype(LOW).T
        sides = []
        for number in range(width // HD):
            head = at // HD + number
            side = part[number * HD : (number + 1) * HD, :].astype(WIDE)
            side = (side * inverse_ref[head, 0:1, :]).astype(LOW)
            mixed = ot_ref[head * HD : (head + 1) * HD, :]
            delta = jnp.sum(mixed * side.astype(WIDE), axis=0, keepdims=True)
            delta_ref[head] = jnp.broadcast_to(delta, delta_ref.shape[1:])
            sides.append(side)
        part = jnp.concatenate(sides, axis=0)
        dot_t[at : at + width, :] = part
        dov[:, at : at + width] = part.T


def cross_back_kernel(
    g2_ref, x1_ref, gain_ref, ht_ref, q_ref, kt_ref, v_ref, raised_ref, inverse_ref, ot_ref,
    encoded_t_ref, output_h, query_h, key_h, value_h,
    g1_ref, gain_grad_ref, state_grad_ref, query_g, key_g, value_g, output_g,
    output_w, query_w, key_w, value_w, dov, dot_t, dqt, dk, dv, delta, semaphores,
):
    fetch = Fetch(
        (output_h, query_h, key_h, value_h), (output_w, query_w, key_w, value_w), semaphores
    )
    b2 = g2_ref[...].astype(LOW)
    fetch.wait(0)
    spread_grads(b2, output_w, inverse_ref, ot_ref, delta, dov, dot_t)
    mixed = ot_ref[...].astype(LOW)
    for at, width in strips(D, 256):
        output_g[:, at : at + width] = dot(mixed, b2[:, at : at + width]).astype(LOW)
    attend_back(q_ref, kt_ref, v_ref, raised_ref, delta, dot_t, dov, dqt, dk, dv)
    dq = dqt[...].T
    for place in range(1, 4):
        fetch.wait(place)
    for at, width in strips(D, 256):
        cols = slice(at, at + width)
        query_g[:, cols] = dot(ht_ref[...], dq[:, cols]).astype(LOW)
        key_g[:, cols] = dot(encoded_t_ref[...], dk[:, cols]).astype(LOW)
        value_g[:, cols] = dot(encoded_t_ref[...], dv[:, cols]).astype(LOW)
        state_grad_ref[:, cols] = dot_back(dk[...], key_w[cols, :]) + dot_back(
            dv[...], value_w[cols, :]
        )
    part, gain_part = center_back(dot_back(dq, query_w[...]), x1_ref[...], gain_ref[...])
    gain_grad_ref[...] = gain_part
    g1_ref[...] = g2_ref[...] + part


def cross_backward(operands, weights):
    rows, frames = operands[0].shape[0], operands[10].shape[1]
    plain, turned, square = (rows, D), (D, rows), shape_of((D, D))
    return pl.pallas_call(
        cross_back_kernel,
        out_shape=(
            shape_of(plain, WIDE), shape_of((1, D), WIDE), shape_of((frames, D), WIDE),
            square, square, square, square,
        ),
        in_specs=[INSIDE] * 11 + [FAR] * 4,
        out_specs=(INSIDE,) * 7,
        scratch_shapes=[pltpu.VMEM((D, D), LOW)] * 4
        + [
            pltpu.VMEM(plain, LOW),
            pltpu.VMEM(turned, LOW),
            pltpu.VMEM(turned, LOW),
            pltpu.VMEM((frames, D), LOW),
            pltpu.VMEM((frames, D), LOW),
            pltpu.VMEM((HEADS, 8, rows), WIDE),
            pltpu.SemaphoreType.DMA((4,)),
        ],
        compiler_params=parameters(),
    )(*operands, *weights)


def self_back_kernel(
    g1_ref, x_ref, gain_ref, ht_ref, q_ref, kt_ref, v_ref, raised_ref, inverse_ref, ot_ref,
    output_h, query_h, key_h, value_h,
    input_grad_ref, gain_grad_ref, query_g, key_g, value_g, output_g,
    output_w, query_w, key_w, value_w, dov, dot_t, dqt, dk, dv, delta, semaphores,
):
    fetch = Fetch(
        (output_h, query_h, key_h, value_h), (output_w, query_w, key_w, value_w), semaphores
    )
    b1 = g1_ref[...].astype(LOW)
    fetch.wait(0)
    spread_grads(b1, output_w, inverse_ref, ot_ref, delta, dov, dot_t)
    mixed = ot_ref[...].astype(LOW)
    for at, width in strips(D, 256):
        output_g[:, at : at + width] = dot(mixed, b1[:, at : at + width]).astype(LOW)
    attend_back(q_ref, kt_ref, v_ref, raised_ref, delta, dot_t, dov, dqt, dk, dv)
    dq = dqt[...].T
    for place in range(1, 4):
        fetch.wait(place)
    for at, width in strips(D, 256):
        cols = slice(at, at + width)
        query_g[:, cols] = dot(ht_ref[...], dq[:, cols]).astype(LOW)
        key_g[:, cols] = dot(ht_ref[...], dk[:, cols]).astype(LOW)
        value_g[:, cols] = dot(ht_ref[...], dv[:, cols]).astype(LOW)
        input_grad_ref[:, cols] = (
            dot_back(dq, query_w[cols, :])
            + dot_back(dk[...], key_w[cols, :])
            + dot_back(dv[...], value_w[cols, :])
        )
    part, gain_part = center_back(
        input_grad_ref[...], x_ref[...].astype(WIDE), gain_ref[...]
    )
    gain_grad_ref[...] = gain_part
    input_grad_ref[...] = g1_ref[...] + part


def self_backward(operands, weights):
    rows = operands[0].shape[0]
    plain, turned, square = (rows, D), (D, rows), shape_of((D, D))
    return pl.pallas_call(
        self_back_kernel,
        out_shape=(shape_of(plain, WIDE), shape_of((1, D), WIDE), square, square, square, square),
        in_specs=[INSIDE] * 10 + [FAR] * 4,
        out_specs=(INSIDE,) * 6,
        scratch_shapes=[pltpu.VMEM((D, D), LOW)] * 4
        + [
            pltpu.VMEM(plain, LOW),
            pltpu.VMEM(turned, LOW),
            pltpu.VMEM(turned, LOW),
            pltpu.VMEM(plain, LOW),
            pltpu.VMEM(plain, LOW),
            pltpu.VMEM((HEADS, 8, rows), WIDE),
            pltpu.SemaphoreType.DMA((4,)),
        ],
        compiler_params=parameters(),
    )(*operands, *weights)


def trade(values, axis, size, bit):
    return lax.ppermute(values, axis, [(i, i ^ bit) for i in range(size)])


def add_rounded(left, right):
    return (left.astype(jnp.float32) + right.astype(jnp.float32)).astype(jnp.bfloat16)


def halve(values, dim, axis, size, bit):
    mine = (lax.axis_index(axis) // bit) % 2
    kept = lax.dynamic_index_in_dim(values, mine, dim, keepdims=False)
    sent = lax.dynamic_index_in_dim(values, 1 - mine, dim, keepdims=False)
    return add_rounded(kept, trade(sent, axis, size, bit))


def bits_of(size):
    return [1 << k for k in range(size.bit_length() - 1)]


def members_first(values, members, groups):
    for bit in bits_of(members):
        values = halve(values, len(values.shape) - 3, "tm", members, bit)
    for bit in bits_of(groups):
        values = add_rounded(values, trade(values, "clip", groups, bit))
    return values.astype(jnp.float32)


def groups_first(values, members, groups):
    values = halve(values, len(values.shape) - 3, "tm", members, 1)
    lead = values.shape[:-2]
    rows, columns = values.shape[-2:]
    for bit in bits_of(groups):
        values = values.reshape(lead + (2, values.shape[-2] // 2, columns))
        values = halve(values, len(lead), "clip", groups, bit)
    for bit in bits_of(members)[1:]:
        values = halve(values, len(values.shape) - 3, "tm", members, bit)
    for bit in bits_of(groups)[::-1]:
        mine = (lax.axis_index("clip") // bit) % 2
        other = trade(values, "clip", groups, bit)
        values = jnp.where(
            mine == 0, jnp.concatenate([values, other]), jnp.concatenate([other, values])
        )
    return values.astype(jnp.float32)


def sum_plain(matrices, gains, members, groups):
    split = (2,) * (members.bit_length() - 1)
    totals = []
    for place, matrix in enumerate(matrices):
        blocks = matrix.reshape(split + (matrix.shape[0] // members, matrix.shape[1]))
        totals.append((members_first, groups_first)[place % 2](blocks, members, groups))
    return tuple(totals), lax.psum(gains, ("tm", "clip"))


PART = 48
UNITS = 16
UNIT_ORDER = (8, 9, 10, 11, 12, 13, 14, 15, 7, 4, 5, 6, 3, 0, 1, 2)
LETTERS = "ABCBABAACBBBABBB"
STEPS = (
    1000, 1001, 0, 1002, 1003, 8, 1004, 1, 1005, 1006, 1007, 9, 1008, 1009, 16, 1010,
    1011, 24, 1012, 2, 17, 1013, 1014, 1015, 10, 56, 25, 32, 40, 1016, 48, 1017,
    57, 3, 33, 1018, 64, 41, 11, 1019, 1020, 72, 18, 65, 49, 1021, 12, 1022,
    80, 4, 73, 58, 1023, 42, 1024, 88, 81, 5, 1025, 34, 26, 1026, 66, 89,
    19, 1027, 96, 1028, 50, 97, 59, 13, 1029, 104, 1030, 43, 105, 35, 82, 1031,
    112, 27, 1032, 51, 113, 74, 1033, 120, 14, 90, 1034, 128, 98, 44, 121, 67,
    28, 129, 106, 83, 99, 75, 60, 20, 114, 91, 36, 84, 29, 130, 45, 52,
    76, 68, 107, 92, 122, 100, 131, 61, 85, 115, 108, 21, 77, 37, 123, 30,
    93, 46, 132, 116, 53, 124, 109, 69, 101, 117, 86, 78, 94, 125, 133, 110,
    118, 126,
)


def add_halves(left, right):
    return left + right


class Sums:
    def __init__(self, made, emit, s):
        self.made, self.emit = made, emit
        self.got0, self.a, self.b = s.got0, (s.a1, s.a2, s.a3, s.a4), (s.b1, s.b2, s.b3, s.b4, s.b5)
        self.send_sem, self.recv_sem = s.send_sem, s.recv_sem
        self.gain_send, self.gain_recv = s.gain_send, s.gain_recv
        self.gain_sum, self.gain_got = s.gain_sum, s.gain_got
        tm, clip = lax.axis_index("tm"), lax.axis_index("clip")
        self.core, self.x, self.low, self.high = tm % 2, (tm // 2) % 2, (tm // 4) % 2, tm // 8
        self.core_peer = (tm + 1 - 2 * self.core, clip)
        self.x_peer = (tm + 2 - 4 * self.x, clip)
        self.low_peer = (tm + 4 - 8 * self.low, clip)
        self.high_peer = (tm + 8 - 16 * self.high, clip)
        self.clip_peer = (tm, 1 - clip)
        self.peers = (self.core_peer, self.x_peer, self.low_peer, self.high_peer, self.clip_peer)
        half = D // 2
        self.mine = pl.ds(pl.multiple_of(clip * half, half), half)
        self.other = pl.ds(pl.multiple_of((1 - clip) * half, half), half)
        self.copies, self.gain_copies, self.places = {}, {}, {}
        self.started, self.left = [], set()
        self.slots = {
            place: sum((LETTERS[k] == "B") == (LETTERS[place] == "B") for k in range(place))
            for place in range(UNITS)
        }

    def meet(self):
        barrier = pltpu.get_barrier_semaphore()
        for peer in self.peers:
            pl.semaphore_signal(barrier, inc=1, device_id=peer, device_id_type=MESH)
        pl.semaphore_wait(barrier, len(self.peers))

    def send(self, src, dst, stage, place, peer):
        copy = pltpu.make_async_remote_copy(
            src_ref=src,
            dst_ref=dst,
            send_sem=self.send_sem.at[stage, place],
            recv_sem=self.recv_sem.at[stage, place],
            device_id=peer,
            device_id_type=MESH,
        )
        copy.start()
        self.places[stage, place] = len(self.started)
        self.started.append(copy)
        self.copies[stage, place] = copy

    def step(self, stage, place):
        if stage == 0:
            buffer, number = self.made(place)
            source = buffer.at[:, :, :, 1 - self.core, number]
            self.send(source, self.got0.at[place], 0, place, self.core_peer)
            return
        self.copies[stage - 1, place].wait_recv()
        if stage == 1:
            self.add_cores(place)
        step = dict(A=self.step_a, B=self.step_b, C=self.step_c)[LETTERS[place]]
        step(stage, place, self.slots[place])

    def add_cores(self, place):
        got0 = self.got0
        buffer, number = self.made(place)

        @pl.loop(0, 8)
        def _(block):
            i, j, k = block // 4, (block // 2) % 2, block % 2
            mine = buffer[i, j, k, self.core, number]
            got0[place, i, j, k] = add_halves(got0[place, i, j, k], mine)

    def step_a(self, stage, place, slot):
        got0, (a1, a2, a3, a4) = self.got0, self.a
        if stage == 1:
            source = got0.at[place, :, :, 1 - self.x]
            self.send(source, a1.at[slot], 1, place, self.x_peer)
        elif stage == 2:

            @pl.loop(0, 4)
            def _(block):
                i, j = block // 2, block % 2
                a1[slot, i, j] = add_halves(a1[slot, i, j], got0[place, i, j, self.x])

            self.send(a1.at[slot, :, 1 - self.low], a2.at[slot], 2, place, self.low_peer)
        elif stage == 3:

            @pl.loop(0, 2)
            def _(i):
                a2[slot, i] = add_halves(a2[slot, i], a1[slot, i, self.low])

            self.send(a2.at[slot, 1 - self.high], a3.at[slot], 3, place, self.high_peer)
        else:
            self.last_two(stage, place, slot, self.high)

    def step_c(self, stage, place, slot):
        got0, (a1, a2, a3, a4) = self.got0, self.a
        if stage == 1:
            source = got0.at[place, :, 1 - self.low]
            self.send(source, a1.at[slot], 1, place, self.low_peer)
        elif stage == 2:

            @pl.loop(0, 4)
            def _(block):
                i, j = block // 2, block % 2
                a1[slot, i, j] = add_halves(a1[slot, i, j], got0[place, i, self.low, j])

            self.send(a1.at[slot, 1 - self.high], a2.at[slot], 2, place, self.high_peer)
        elif stage == 3:

            @pl.loop(0, 2)
            def _(i):
                a2[slot, i] = add_halves(a2[slot, i], a1[slot, self.high, i])

            self.send(a2.at[slot, 1 - self.x], a3.at[slot], 3, place, self.x_peer)
        else:
            self.last_two(stage, place, slot, self.x)

    def last_two(self, stage, place, slot, side):
        a1, a2, a3, a4 = self.a
        if stage == 4:
            a3[slot] = add_halves(a3[slot], a2[slot, side])
            self.send(a3.at[slot], a4.at[slot], 4, place, self.clip_peer)
        else:
            total = a3[slot].astype(WIDE) + a4[slot].astype(WIDE)
            self.emit(UNIT_ORDER[place], slice(0, D), total)

    def step_b(self, stage, place, slot):
        got0, (b1, b2, b3, b4, b5) = self.got0, self.b
        if stage == 1:
            source = got0.at[place, :, :, :, :, self.other]
            self.send(source, b1.at[slot], 1, place, self.clip_peer)
        elif stage == 2:

            @pl.loop(0, 8)
            def _(block):
                i, j, k = block // 4, (block // 2) % 2, block % 2
                b1[slot, i, j, k] = add_halves(
                    b1[slot, i, j, k], got0[place, i, j, k, :, self.mine]
                )

            self.send(b1.at[slot, :, :, 1 - self.x], b2.at[slot], 2, place, self.x_peer)
        elif stage == 3:

            @pl.loop(0, 4)
            def _(block):
                i, j = block // 2, block % 2
                b2[slot, i, j] = add_halves(b2[slot, i, j], b1[slot, i, j, self.x])

            self.send(b2.at[slot, :, 1 - self.low], b3.at[slot], 3, place, self.low_peer)
        elif stage == 4:

            @pl.loop(0, 2)
            def _(i):
                b3[slot, i] = add_halves(b3[slot, i], b2[slot, i, self.low])

            self.send(b3.at[slot, 1 - self.high], b4.at[slot], 4, place, self.high_peer)
        elif stage == 5:
            b4[slot] = add_halves(b4[slot], b3[slot, self.high])
            self.send(b4.at[slot], b5.at[slot], 5, place, self.clip_peer)
        else:
            self.emit(UNIT_ORDER[place], self.mine, b4[slot].astype(WIDE))
            self.emit(UNIT_ORDER[place], self.other, b5[slot].astype(WIDE))

    def gain_step(self, number):
        if number > 0:
            self.gain_copies[number - 1].wait_recv()
            self.gain_sum[number] = self.gain_sum[number - 1] + self.gain_got[number - 1]
        if number < len(self.peers):
            copy = pltpu.make_async_remote_copy(
                src_ref=self.gain_sum.at[number],
                dst_ref=self.gain_got.at[number],
                send_sem=self.gain_send.at[number],
                recv_sem=self.gain_recv.at[number],
                device_id=self.peers[number],
                device_id_type=MESH,
            )
            copy.start()
            self.started.append(copy)
            self.gain_copies[number] = copy

    def leave(self, place):
        self.copies[0, place].wait_send()
        self.left.add(self.places[0, place])

    def finish(self):
        for number, copy in enumerate(self.started):
            if number not in self.left:
                copy.wait_send()


class BackIn(NamedTuple):
    length: Any
    x2: Any
    hidden: Any
    hidden_t: Any
    b3: Any
    x1: Any
    x: Any
    encoded_t: Any
    gain_mlp: Any
    gain_cross: Any
    gain_self: Any
    expand_w: Any
    narrow_w: Any
    cross: Layer
    own: Layer
    cross_w: Weights
    own_w: Weights


class BackOut(NamedTuple):
    output: Any
    input_grad: Any
    state_grad: Any
    summed: Any
    gains: Any


class Room(NamedTuple):
    x1: Any
    encoded_t: Any
    cross: Layer
    own: Layer
    weight: Any
    raised: Any
    ot: Any
    delta: Any
    g: Any
    x3: Any
    low: Any
    dov: Any
    dot_t: Any
    dqt: Any
    dk: Any
    dv: Any
    kept: Any
    narrow: Any
    total: Any
    got0: Any
    a1: Any
    a2: Any
    a3: Any
    a4: Any
    b1: Any
    b2: Any
    b3: Any
    b4: Any
    b5: Any
    gain_sum: Any
    gain_got: Any
    fetch_sem: Any
    raised_sem: Any
    out_sem: Any
    send_sem: Any
    recv_sem: Any
    gain_send: Any
    gain_recv: Any


class Once:
    def __init__(self, copy):
        self.copy, self.pending = copy, True
        copy.start()

    def ready(self):
        if self.pending:
            self.copy.wait()
        self.pending = False


def back_kernel(tree, *refs):
    given, out, s = jax.tree.unflatten(tree, refs)
    count = [0]

    def fetch(source, target):
        copy = pltpu.make_async_copy(source, target, s.fetch_sem.at[count[0]])
        count[0] += 1
        return Once(copy)

    def fetch_layer(source, target):
        return {
            field: fetch(getattr(source, field), getattr(target, field))
            for field in Layer._fields
            if getattr(target, field) is not None
        }

    def raised_copy(layer, pair):
        source = layer.raised.at[pl.ds(2 * pair, 2)]
        slot = pair % 2
        return pltpu.make_async_copy(
            source, s.raised.at[slot, :, pl.ds(0, source.shape[1])], s.raised_sem.at[slot]
        )

    def made(place):
        if 4 <= place < 8 or place >= 12:
            return s.narrow, place % 4
        return s.kept, place % 4 + 4 * (place >= 8)

    def keep(place, at, width, values):
        buffer, number = made(place)
        buffer[:, :, :, :, number, :, at : at + width] = values.astype(LOW).reshape(
            2, 2, 2, 2, PART, width
        )

    def emit(unit, cols, total):
        s.total[unit, :, cols] = total

    sums = Sums(made, emit, s)
    live = {}
    waits = {}

    def feed_room(strip, half):
        cols = pl.ds(half * (D // 2), D // 2)
        if strip % 2 == 0:
            return s.dov.at[:, cols], s.dv.at[:, cols]
        cols = pl.ds(0, D // 2)
        return s.raised.at[0, half, :, cols], s.raised.at[1, half, :, cols]

    def feed_first(strip, half):
        def run():
            first, second = s.weight[2 * (strip % 2)], s.weight[2 * (strip % 2) + 1]
            for name in ("hidden", "hidden_t", "b3", "x2"):
                waits[name].ready()
            width = D // 2
            cols = slice(half * width, (half + 1) * width)
            waits["first", strip].ready()
            active, slope = gelu_both(dot(s.dk[...], first[:, cols]))
            waits["second", strip].ready()
            grad = (slope * dot_back(s.low[...], second[cols, :])).astype(LOW)
            keep(strip, half * width, width, dot(s.dot_t[...], grad))
            active_ref, grad_ref = feed_room(strip, half)
            active_ref[...] = active.astype(LOW)
            grad_ref[...] = grad

        return run

    def feed_second(strip, half):
        def run():
            first, second = s.weight[2 * (strip % 2)], s.weight[2 * (strip % 2) + 1]
            cols = slice(half * (D // 2), (half + 1) * (D // 2))
            active, grad = [part[...] for part in feed_room(strip, half)]
            s.narrow[strip // 2, strip % 2, half] = (
                dot_rows(active, s.low[...]).astype(LOW).reshape(2, 4, PART, D)
            )
            forward, backward = dot(active, second[cols, :]), dot_back(grad, first[:, cols])
            if strip == 0 and half == 0:
                s.x3[...] = s.x1[...] + forward
                s.g[...] = backward
            else:
                s.x3[...] += forward
                s.g[...] += backward
            if strip < 2 and half:
                fetch_feed(strip + 2)

        return run

    def fetch_feed(strip):
        cols = pl.ds(strip * D, D)
        waits["first", strip] = fetch(given.expand_w.at[:, cols], s.weight[2 * (strip % 2)])
        waits["second", strip] = fetch(given.narrow_w.at[cols, :], s.weight[2 * (strip % 2) + 1])

    def feed_end():
        raised_copy(given.cross, 0).start()
        raised_copy(given.cross, 1).start()
        for place, name in enumerate(Weights._fields):
            waits["cross", name] = fetch(getattr(given.cross_w, name), s.weight[place])
        live = lax.broadcasted_iota(jnp.int32, s.x3.shape, 0) < given.length[0]
        s.dv[...] = jnp.where(live, s.x3[...], 0.0).astype(LOW)
        waits["output"] = Once(pltpu.make_async_copy(s.dv, out.output, s.out_sem.at[0]))
        part, gain_part = center_back(s.g[...], s.x1[...], given.gain_mlp[...])
        s.gain_sum[0, 2:3, :] = gain_part
        s.g[...] = s.low[...].astype(WIDE) + part
        waits["x1"] = fetch(given.x1, s.x1)

    def spread(layer, room, name):
        def run():
            waits[name, "output"].ready()
            waits[name]["inverse"].ready()
            s.low[...] = s.g[...].astype(LOW)
            waits[name, "ot"].ready()
            spread_grads(s.low[...], s.weight[0], room.inverse, s.ot, s.delta, s.dov, s.dot_t)
            if name == "cross":
                waits["own", "output"] = fetch(given.own_w.output, s.weight[0])

        return run

    def output_grad(room, name, place):
        def run():
            if name == "own":
                for unit in range(4, 8):
                    sums.leave(unit)
            mixed = s.ot[...].astype(LOW)
            for at, width in strips(D, 256):
                keep(place, at, width, dot(mixed, s.low[:, at : at + width]))
            if name == "cross":
                waits["own", "ot"] = fetch(given.own.ot, s.ot)

        return run

    def attention(layer, room, name, first):
        def run():
            for field in ("q", "kt", "v"):
                waits[name][field].ready()
            waits["output"].ready()
            inner = layer.raised.shape[1]

            @pl.loop(first, first + 2)
            def _(pair):
                raised_copy(layer, pair).wait()
                slot = pair % 2
                attend_pair(
                    pair,
                    room.q,
                    room.kt,
                    room.v,
                    s.raised.at[slot, :, pl.ds(0, inner)],
                    s.delta,
                    s.dot_t,
                    s.dov,
                    s.dqt,
                    s.dk.at[pl.ds(0, inner)],
                    s.dv.at[pl.ds(0, inner)],
                )
                if first < PAIRS - 2:
                    raised_copy(layer, pair + 2).start()
                elif name == "cross":
                    raised_copy(given.own, slot).start()

        return run

    def strip_grads(first_t, second_t, inner, strip, place):
        cols = slice(256 * strip, 256 * (strip + 1))
        part = s.dqt[cols, :].T
        s.low[:, cols] = part
        keep(place, 0, 256, dot(first_t[...], part))
        keep(place, 256, 256, dot(second_t[...], s.dk[0:inner, cols]))
        keep(place, 512, 256, dot(second_t[...], s.dv[0:inner, cols]))

    def cross_grads(strip):
        def run():
            waits["cross"]["ht"].ready()
            waits["encoded_t"].ready()
            strip_grads(s.cross.ht, s.encoded_t, s.encoded_t.shape[1], strip, 9 + strip)

        return run

    def cross_inputs():
        for name in ("query", "key", "value"):
            waits["cross", name].ready()
        waits["x1"].ready()
        frames = s.encoded_t.shape[1]
        for at, width in strips(D, 256):
            cols = slice(at, at + width)
            s.x3[0:frames, cols] = dot_back(s.dk[0:frames, :], s.weight[2][cols, :]) + dot_back(
                s.dv[0:frames, :], s.weight[3][cols, :]
            )
        state = s.x3.at[pl.ds(0, frames)]
        waits["state"] = Once(pltpu.make_async_copy(state, out.state_grad, s.out_sem.at[1]))
        part, gain_part = center_back(
            dot_back(s.low[...], s.weight[1][...]), s.x1[...], given.gain_cross[...]
        )
        s.gain_sum[0, 1:2, :] = gain_part
        s.g[...] += part
        for place, name in enumerate(Weights._fields):
            if place:
                waits["own", name] = fetch(getattr(given.own_w, name), s.weight[place])

    def self_grads(strip):
        def run():
            waits["own"]["ht"].ready()
            strip_grads(s.own.ht, s.own.ht, s.own.ht.shape[1], strip, 13 + strip)
            if strip == 2:
                waits["x"] = fetch(given.x, s.dov)

        return run

    def self_inputs():
        for name in ("query", "key", "value"):
            waits["own", name].ready()
        waits["x"].ready()
        for at, width in strips(D, 256):
            cols = slice(at, at + width)
            s.x1[:, cols] = (
                dot_back(s.low[...], s.weight[1][cols, :])
                + dot_back(s.dk[...], s.weight[2][cols, :])
                + dot_back(s.dv[...], s.weight[3][cols, :])
            )
        part, gain_part = center_back(s.x1[...], s.dov[...].astype(WIDE), given.gain_self[...])
        s.gain_sum[0, 0:1, :] = gain_part
        s.g[...] += part
        waits["input"] = Once(pltpu.make_async_copy(s.g, out.input_grad, s.out_sem.at[2]))

    pieces = [
        part(strip, half)
        for strips_now in ((0, 1), (2, 3))
        for part in (feed_first, feed_second)
        for strip in strips_now
        for half in range(2)
    ]
    pieces += [feed_end, spread(given.cross, s.cross, "cross"), output_grad(s.cross, "cross", 8)]
    for strip in range(3):
        pieces += [attention(given.cross, s.cross, "cross", 2 * strip), cross_grads(strip)]
    pieces += [cross_inputs, spread(given.own, s.own, "own"), output_grad(s.own, "own", 12)]
    for strip in range(3):
        pieces += [attention(given.own, s.own, "own", 2 * strip), self_grads(strip)]
    pieces.append(self_inputs)
    waits["hidden"] = fetch(given.hidden, s.dk)
    fetch_feed(0)
    waits["b3"] = fetch(given.b3, s.low)
    waits["hidden_t"] = fetch(given.hidden_t, s.dot_t)
    waits["x2"] = fetch(given.x2, s.x1)
    fetch_feed(1)
    waits["cross"] = fetch_layer(given.cross, s.cross)
    waits["cross", "ot"] = fetch(given.cross.ot, s.ot)
    waits["encoded_t"] = fetch(given.encoded_t, s.encoded_t)
    waits["own"] = fetch_layer(given.own, s.own)
    s.gain_sum[0] = jnp.zeros(s.gain_sum.shape[1:], WIDE)
    met = False
    for code in STEPS:
        if code < 1000:
            if not met:
                sums.meet()
                met = True
            if code < UNITS * 8:
                sums.step(code % 8, code // 8)
            else:
                sums.gain_step(code % 8)
        else:
            pieces[code - 1000]()
    out.gains[...] = s.gain_sum[5]
    result = pltpu.make_async_copy(s.total, out.summed, s.out_sem.at[3])
    result.start()
    sums.finish()
    waits["state"].ready()
    waits["input"].ready()
    result.wait()


def room_for(given):
    rows, frames = given.x.shape[0], given.encoded_t.shape[1]
    split = (2, 2, 2, 2)
    thin = LETTERS.count("B")
    thick = UNITS - thin
    half = D // 2

    def low(*shape):
        return pltpu.VMEM(shape, LOW)

    def wide(*shape):
        return pltpu.VMEM(shape, WIDE)

    def like(array):
        return pltpu.VMEM(array.shape, array.dtype)

    def layer(source):
        return jax.tree.map(like, source)._replace(raised=None, ot=None)

    plain, turned = (rows, D), (D, rows)
    dma = pltpu.SemaphoreType.DMA
    return Room(
        x1=like(given.x1), encoded_t=like(given.encoded_t),
        cross=layer(given.cross), own=layer(given.own),
        weight=[low(D, D)] * 4, raised=low(2, 2, rows, rows), ot=wide(*turned),
        delta=like(given.own.inverse),
        g=wide(*plain), x3=wide(*plain), low=low(*plain), dov=low(*plain), dot_t=low(*turned),
        dqt=low(*turned), dk=low(*plain), dv=low(*plain),
        kept=low(*split, 8, PART, D), narrow=low(*split, 4, PART, D),
        total=wide(UNITS, PART, D), got0=low(UNITS, 2, 2, 2, PART, D),
        a1=low(thick, 2, 2, PART, D), a2=low(thick, 2, PART, D), a3=low(thick, PART, D),
        a4=low(thick, PART, D), b1=low(thin, 2, 2, 2, PART, half), b2=low(thin, 2, 2, PART, half),
        b3=low(thin, 2, PART, half), b4=low(thin, PART, half), b5=low(thin, PART, half),
        gain_sum=wide(6, 8, D), gain_got=wide(5, 8, D),
        fetch_sem=dma((40,)), raised_sem=dma((2,)), out_sem=dma((4,)),
        send_sem=dma((6, UNITS)), recv_sem=dma((6, UNITS)), gain_send=dma((5,)),
        gain_recv=dma((5,)),
    )


def backward_and_sum(given):
    rows, frames = given.x.shape[0], given.encoded_t.shape[1]
    outs = BackOut(
        output=shape_of((rows, D)), input_grad=shape_of((rows, D), WIDE),
        state_grad=shape_of((frames, D), WIDE), summed=shape_of((UNITS, PART, D), WIDE),
        gains=shape_of((8, D), WIDE),
    )
    room = room_for(given)
    places = jax.tree.map(lambda _: FAR, given)._replace(
        length=NUMBERS, gain_mlp=INSIDE, gain_cross=INSIDE, gain_self=INSIDE
    )
    results = pl.pallas_call(
        functools.partial(back_kernel, jax.tree.structure((given, outs, room))),
        out_shape=tuple(outs),
        in_specs=jax.tree.leaves(places),
        out_specs=(FAR,) * 4 + (INSIDE,),
        scratch_shapes=jax.tree.leaves(room),
        compiler_params=pltpu.CompilerParams(
            collective_id=0, has_side_effects=True, vmem_limit_bytes=63 * 2**20
        ),
    )(*jax.tree.leaves(given))
    return BackOut(*results)


def cut(matrix, strip):
    return matrix.at[:, pl.ds(256 * strip, 256)]


def finish_kernel(output, input_grad, state_grad, summed, *refs):
    outs, (rows_low, rows_wide, frames_wide, blocks, taken, given) = refs[:13], refs[13:]
    parts = [
        (summed.at[pl.ds(0, 8)], blocks.at[pl.ds(0, 8)]),
        (summed.at[pl.ds(8, 8)], blocks.at[pl.ds(8, 8)]),
        (input_grad, rows_wide),
        (state_grad, frames_wide),
        (output, rows_low),
    ]
    results = [
        [(blocks.at[3], outs[6]), (blocks.at[7], outs[10])]
        + [
            (blocks.at[4 * layer + k, :, pl.ds(256 * m, 256)], cut(outs[3 + 4 * layer + m], k))
            for layer in range(2)
            for k in range(3)
            for m in range(3)
        ],
        [(blocks.at[pl.ds(12, 4)], outs[12])]
        + [(blocks.at[8 + k], outs[11].at[:, pl.ds(k * D, D)]) for k in range(4)],
        [(rows_wide, outs[1])],
        [(frames_wide, outs[2])],
        [(rows_low, outs[0])],
    ]
    arriving = [
        pltpu.make_async_copy(*pair, taken.at[place]) for place, pair in enumerate(parts)
    ]
    for copy in arriving:
        copy.start()
    leaving = []
    for copy, pairs in zip(arriving, results):
        copy.wait()
        for pair in pairs:
            leaving.append(pltpu.make_async_copy(*pair, given.at[len(leaving)]))
            leaving[-1].start()
    for copy in leaving:
        copy.wait()


def finish(made):
    outs = [shape_of(made[k].shape, made[k].dtype) for k in range(3)]
    outs += [shape_of((PART, D), WIDE)] * 8
    outs += [shape_of((PART, 4 * D), WIDE), shape_of((4, PART, D), WIDE)]
    *results, narrow = pl.pallas_call(
        finish_kernel,
        out_shape=tuple(outs),
        in_specs=[FAR] * 4,
        out_specs=(FAR,) * len(outs),
        scratch_shapes=[pltpu.VMEM(array.shape, array.dtype) for array in made[:4]]
        + [pltpu.SemaphoreType.DMA((5,)), pltpu.SemaphoreType.DMA((28,))],
        compiler_params=parameters(62),
    )(*made[:4])
    return *results, narrow.reshape(4 * PART, D)


def body(
    members,
    groups,
    mel_frames,
    conv_first,
    conv_second,
    enc_projection,
    enc_output,
    enc_expand,
    enc_narrow,
    dec_input,
    lengths,
    self_query,
    self_key,
    self_value,
    self_output,
    cross_query,
    cross_key,
    cross_value,
    cross_output,
    mlp_expand,
    mlp_narrow,
    gain_self,
    gain_cross,
    gain_mlp,
    cotangent,
):
    inputs, length = dec_input[0, 0], lengths[0]
    own_w = Weights(self_output, self_query, self_key, self_value)
    x1, own, mel = self_forward(length, inputs, gain_self, mel_frames[:, 0], members, own_w)
    encoded, encoded_t = encode(
        mel, conv_first, conv_second, enc_projection, enc_output, enc_expand, enc_narrow
    )
    cross_w = Weights(cross_output, cross_query, cross_key, cross_value)
    x2, hidden, hidden_t, b3, cross = cross_forward(
        length, x1, encoded, cotangent[0, 0], gain_cross, gain_mlp, cross_w
    )
    if (members, groups) == (16, 2):
        made = backward_and_sum(
            BackIn(
                length, x2, hidden, hidden_t, b3, x1, inputs, encoded_t,
                gain_mlp, gain_cross, gain_self, mlp_expand, mlp_narrow,
                cross, own, cross_w, own_w,
            )
        )
        dec_output, dec_input_grad, enc_state_grad, *totals = finish(made)
        gains = made.gains
    else:
        dec_output, g2, g_gain_mlp, g_expand, g_narrow = feed_both(
            length, x2, hidden, hidden_t, b3, gain_mlp, mlp_expand, mlp_narrow
        )
        g1, g_gain_cross, enc_state_grad, *cross_grads = cross_backward(
            (g2, x1, gain_cross) + tuple(cross) + (encoded_t,), cross_w
        )
        dec_input_grad, g_gain_self, *self_grads = self_backward(
            (g1, inputs, gain_self) + tuple(own), own_w
        )
        gains = jnp.concatenate([g_gain_self, g_gain_cross, g_gain_mlp, jnp.zeros((5, D), WIDE)])
        totals, gains = sum_plain(
            self_grads + cross_grads + [g_expand, g_narrow], gains, members, groups
        )
    part = D // members
    gains = lax.dynamic_slice_in_dim(gains, lax.axis_index("tm") * part, part, 1)
    return (
        encoded[None, None],
        dec_output[None, None],
        dec_input_grad[None, None],
        enc_state_grad[None, None],
        *totals,
        gains[0],
        gains[1],
        gains[2],
    )


def solution(mesh):
    placed = (
        P("tm", "clip", None, None),
        P(),
        P(),
        P(),
        P(),
        P(),
        P(),
        P("clip", "tm", None, None),
        P("clip", "tm"),
        P(),
        P(),
        P(),
        P(),
        P(),
        P(),
        P(),
        P(),
        P(),
        P(),
        P(),
        P(),
        P(),
        P("clip", "tm", None, None),
    )
    return jax.shard_map(
        functools.partial(body, mesh.shape["tm"], mesh.shape["clip"]),
        mesh=mesh,
        in_specs=placed,
        out_specs=(
            P("clip", "tm", None, None),
            P("clip", "tm", None, None),
            P("clip", "tm", None, None),
            P("clip", "tm", None, None),
            P("tm", None),
            P("tm", None),
            P("tm", None),
            P("tm", None),
            P("tm", None),
            P("tm", None),
            P("tm", None),
            P("tm", None),
            P("tm", None),
            P("tm", None),
            P("tm"),
            P("tm"),
            P("tm"),
        ),
        check_vma=False,
    )
```

```python
import functools
import math
from typing import Any, NamedTuple

import jax
import jax.numpy as jnp
import numpy as np
from jax import lax
from jax.experimental import pallas as pl
from jax.experimental.pallas import tpu as pltpu
from jax.sharding import PartitionSpec as P

D = 768
HEADS = 12
HD = 64
PAIRS = HEADS // 2
LANES = 2 * HD
SCALE = HD ** (-0.5)
LOW = jnp.bfloat16
WIDE = jnp.float32
INSIDE = pl.BlockSpec(memory_space=pltpu.VMEM)
FAR = pl.BlockSpec(memory_space=pltpu.HBM)
MESH = pl.DeviceIdType.MESH
NUMBERS = pl.BlockSpec(memory_space=pltpu.SMEM)


def shape_of(shape, kind=LOW):
    return jax.ShapeDtypeStruct(shape, kind)


def parameters(megabytes=58):
    return pltpu.CompilerParams(vmem_limit_bytes=megabytes * 2**20)


def center(values):
    shifted = values - jnp.mean(values, axis=-1, keepdims=True)
    spread = jnp.mean(shifted * shifted, axis=-1, keepdims=True)
    root = lax.rsqrt(spread + 1e-05)
    return shifted * root, root


def center_back(gradient, values, gain):
    normed, root = center(values)
    inner = gradient * gain
    first = jnp.mean(inner, axis=-1, keepdims=True)
    second = jnp.mean(inner * normed, axis=-1, keepdims=True)
    gain_part = jnp.sum(gradient * normed, axis=0, keepdims=True)
    return root * (inner - first - normed * second), gain_part


def gelu(values):
    return values * (0.5 + 0.5 * lax.erf(values * 2**-0.5))


def gelu_both(values):
    area = 0.5 + 0.5 * lax.erf(values * 2**-0.5)
    slope = area + values * ((2 * math.pi) ** -0.5 * jnp.exp(-0.5 * values * values))
    return values * area, slope


def dot(left, right):
    return jnp.dot(left, right, preferred_element_type=WIDE)


def dot_back(left, right):
    return lax.dot_general(left, right, (((1,), (1,)), ((), ())), preferred_element_type=WIDE)


def dot_rows(left, right):
    return lax.dot_general(left, right, (((0,), (0,)), ((), ())), preferred_element_type=WIDE)


def strips(total, width):
    return [(at, min(width, total - at)) for at in range(0, total, width)]


class Fetch:
    def __init__(self, sources, targets, semaphores):
        self.copies = [
            pltpu.make_async_copy(source, target, semaphores.at[place])
            for place, (source, target) in enumerate(zip(sources, targets))
        ]
        for copy in self.copies:
            copy.start()

    def wait(self, place):
        self.copies[place].wait()


def pair_lanes(pair):
    return pl.ds(pl.multiple_of(pair * LANES, LANES), LANES)


def head_rows(pair, side):
    return pl.ds(pl.multiple_of(pair * LANES + side * HD, HD), HD)


def attend(
    q_ref, k_ref, vt_ref, bias_ref, ot_ref, inverse_ref=None, raised_ref=None, leave=None
):
    ones = jnp.ones((16, vt_ref.shape[1]), LOW)

    @pl.loop(0, PAIRS, step=3)
    def _(first):
        heads = [(first + more, side) for more in range(3) for side in range(2)]
        cuts = [slice(side * HD, (side + 1) * HD) for _, side in heads]
        queries = [q_ref[:, pair_lanes(first + more)] for more in range(3)]
        keys = [k_ref[:, pair_lanes(first + more)] for more in range(3)]
        scores = [dot_back(keys[k // 2][:, cuts[k]], queries[k // 2][:, cuts[k]]) for k in range(6)]
        if bias_ref is not None:
            scores = [part + bias_ref[...] for part in scores]
        raised = [
            jnp.exp(part - jnp.max(part, axis=0, keepdims=True)).astype(LOW) for part in scores
        ]
        rows = [head_rows(pair, side) for pair, side in heads]
        mixed = [
            dot(jnp.concatenate([vt_ref[rows[k], :], ones], axis=0), raised[k]) for k in range(6)
        ]
        for k, (pair, side) in enumerate(heads):
            inverse = 1.0 / mixed[k][HD : HD + 1]
            ot_ref[rows[k], :] = mixed[k][:HD] * inverse
            if raised_ref is not None:
                raised_ref[2 * pair + side] = raised[k]
                inverse_ref[2 * pair + side] = jnp.broadcast_to(inverse, inverse_ref.shape[1:])
        if leave is not None:
            leave(first)
            leave(first + 1)
            leave(first + 2)


def attend_pair(
    pair, q_ref, kt_ref, v_ref, raised_ref, delta_ref, dot_ref, dov_ref, dqt_ref, dk_ref, dv_ref
):
    lanes = pair_lanes(pair)
    queries, values, grads = q_ref[:, lanes], v_ref[:, lanes], dov_ref[:, lanes]
    sides = range(2)
    rows = [head_rows(pair, side) for side in sides]
    cuts = [slice(side * HD, (side + 1) * HD) for side in sides]
    products = [dot(values[:, cuts[side]], dot_ref[rows[side], :]) for side in sides]
    value_sides = [dot(raised_ref[side], grads[:, cuts[side]]) for side in sides]
    score_grads = [
        (
            raised_ref[side].astype(WIDE)
            * (products[side] - delta_ref[2 * pair + side, 0:1, :])
        ).astype(LOW)
        for side in sides
    ]
    key_sides = [dot(score_grads[side], queries[:, cuts[side]]) for side in sides]
    query_sides = [dot(kt_ref[rows[side], :], score_grads[side]) for side in sides]
    for side in sides:
        dqt_ref[rows[side], :] = (query_sides[side] * SCALE).astype(LOW)
    dk_ref[:, lanes] = jnp.concatenate(key_sides, axis=1).astype(LOW)
    dv_ref[:, lanes] = jnp.concatenate(value_sides, axis=1).astype(LOW)


def attend_back(q_ref, kt_ref, v_ref, raised_ref, *rest):
    @pl.loop(0, PAIRS)
    def _(pair):
        attend_pair(pair, q_ref, kt_ref, v_ref, raised_ref.at[pl.ds(2 * pair, 2)], *rest)


def encoder_kernel(
    mel_ref, position_ref, first_h, second_h, joint_h, output_h, expand_h, narrow_h,
    out_ref, out_t_ref,
    first_w, second_w, joint_w, output_w, expand_w, narrow_w,
    even, odd, state, hidden, q, k, vt, mixed_t, semaphores,
):
    length = out_ref.shape[0]
    fetch = Fetch(
        (first_h, second_h, joint_h, output_h, expand_h, narrow_h),
        (first_w, second_w, joint_w, output_w, expand_w, narrow_w),
        semaphores,
    )
    taps = [mel_ref[pl.ds(7 + tap, length, stride=2), :].astype(LOW) for tap in range(4)]
    fetch.wait(0)
    for at, width in strips(D, 256):
        cols = pl.ds(at, width)
        for start, target in ((0, even), (1, odd)):
            total = sum(dot(taps[start + o], first_w[o, :, cols]) for o in range(3))
            target[:, cols] = gelu(total).astype(LOW)
    fetch.wait(1)
    ranks = lax.broadcasted_iota(jnp.int32, (length, 256), 0)
    for at, width in strips(D, 256):
        cols = pl.ds(at, width)
        before = pltpu.roll(dot(odd[...], second_w[0, :, cols]), 1, 0)
        total = dot(even[...], second_w[1, :, cols]) + dot(odd[...], second_w[2, :, cols])
        total = total + jnp.where(ranks == 0, 0.0, before)
        state[:, cols] = gelu(total) + position_ref[:, cols]
    hidden[...] = center(state[...])[0].astype(LOW)
    fetch.wait(2)
    for at, width in strips(D, 256):
        cols = pl.ds(at, width)
        q[:, cols] = (dot(hidden[...], joint_w[:, cols]).astype(LOW) * SCALE).astype(LOW)
        k[:, cols] = dot(hidden[...], joint_w[:, pl.ds(D + at, width)]).astype(LOW)
        vt[cols, :] = dot(hidden[...], joint_w[:, pl.ds(2 * D + at, width)]).astype(LOW).T
    attend(q, k, vt, None, mixed_t)
    fetch.wait(3)
    mixed = mixed_t[...].astype(LOW).T
    for at, width in strips(D, 256):
        cols = pl.ds(at, width)
        state[:, cols] += dot(mixed, output_w[:, cols])
    hidden[...] = center(state[...])[0].astype(LOW)
    fetch.wait(4)
    fetch.wait(5)

    @pl.loop(0, expand_w.shape[1] // 1024)
    def _(strip):
        parts = [pl.ds(pl.multiple_of(strip * 1024 + at, 512), 512) for at in (0, 512)]
        widened = [gelu(dot(hidden[...], expand_w[:, cols])).astype(LOW) for cols in parts]
        first, second = [dot(part, narrow_w[cols, :]) for part, cols in zip(widened, parts)]
        state[...] += first + second

    encoded = center(state[...])[0].astype(LOW)
    out_ref[...] = encoded
    out_t_ref[...] = encoded.T


def encode(mel, conv_first, conv_second, enc_projection, enc_output, enc_expand, enc_narrow):
    length = (mel.shape[0] - 16) // 2
    weights = (conv_first, conv_second, enc_projection, enc_output, enc_expand, enc_narrow)
    return pl.pallas_call(
        encoder_kernel,
        out_shape=(shape_of((length, D)), shape_of((D, length))),
        in_specs=[INSIDE] * 2 + [FAR] * 6,
        out_specs=(INSIDE, INSIDE),
        scratch_shapes=[pltpu.VMEM(weight.shape, LOW) for weight in weights]
        + [
            pltpu.VMEM((length, D), LOW),
            pltpu.VMEM((length, D), LOW),
            pltpu.VMEM((length, D), WIDE),
            pltpu.VMEM((length, D), LOW),
            pltpu.VMEM((length, D), LOW),
            pltpu.VMEM((length, D), LOW),
            pltpu.VMEM((D, length), LOW),
            pltpu.VMEM((D, length), WIDE),
            pltpu.SemaphoreType.DMA((6,)),
        ],
        compiler_params=parameters(),
    )(mel, sinusoids(length, D), *weights)


def sinusoids(length, features):
    halfway = features // 2
    inverse = np.exp(-math.log(10000.0) / (halfway - 1) * np.arange(halfway)).astype(np.float32)
    angles = np.arange(length, dtype=np.float32)[:, None] * inverse[None, :]
    angles = angles.astype(np.float64)
    return jnp.asarray(np.concatenate([np.sin(angles), np.cos(angles)], axis=1).astype(np.float32))


class Layer(NamedTuple):
    ht: Any
    q: Any
    kt: Any
    v: Any
    raised: Any
    inverse: Any
    ot: Any


class Weights(NamedTuple):
    output: Any
    query: Any
    key: Any
    value: Any


class Leave:
    def __init__(self, held, targets, semaphores):
        self.pairs, self.semaphores, self.started = list(zip(held, targets)), semaphores, []

    def __call__(self, *places):
        for place in places:
            copy = pltpu.make_async_copy(*self.pairs[place], self.semaphores.at[place])
            copy.start()
            self.started.append(copy)

    def scores(self, place, first):
        def copy(pair):
            held, target = self.pairs[place]
            heads = pl.ds(2 * pair, 2)
            return pltpu.make_async_copy(
                held.at[heads], target.at[heads], self.semaphores.at[first + pair]
            )

        self.started += [copy(pair) for pair in range(PAIRS)]
        return lambda pair: copy(pair).start()

    def finish(self):
        for copy in self.started:
            copy.wait()


def self_kernel(
    members, length_ref, x_ref, gain_ref, mel_h, output_h, query_h, key_h, value_h, *refs
):
    outs, held = refs[:9], refs[9:18]
    output_w, query_w, key_w, value_w, hidden, k, vt, bias = refs[18:26]
    semaphores, out_sem, own_sem, send_sem, recv_sem = refs[26:]
    x1, ht, q, kt, v, raised, inverse, ot, mel = held
    leave = Leave(held, outs, out_sem)
    tm, clip = lax.axis_index("tm"), lax.axis_index("clip")
    barrier = pltpu.get_barrier_semaphore()

    @pl.loop(1, members)
    def _(step):
        peer = (lax.rem(tm + step, members), clip)
        pl.semaphore_signal(barrier, inc=1, device_id=peer, device_id_type=MESH)

    fetch = Fetch(
        (query_h, key_h, value_h, output_h), (query_w, key_w, value_w, output_w), semaphores
    )
    rows = x_ref.shape[0]
    hidden[...] = (center(x_ref[...].astype(WIDE))[0] * gain_ref[...]).astype(LOW)
    keys = lax.broadcasted_iota(jnp.int32, (rows, rows), 0)
    queries = lax.broadcasted_iota(jnp.int32, (rows, rows), 1)
    allowed = (keys <= queries) & (keys < length_ref[0])
    bias[...] = jnp.where(allowed, 0.0, -1e30)
    fetch.wait(0)
    fetch.wait(1)
    fetch.wait(2)
    for at, width in strips(D, 256):
        cols = pl.ds(at, width)
        q[:, cols] = (dot(hidden[...], query_w[:, cols]).astype(LOW) * SCALE).astype(LOW)
        part = dot(hidden[...], key_w[:, cols]).astype(LOW)
        k[:, cols] = part
        kt[cols, :] = part.T
        part = dot(hidden[...], value_w[:, cols]).astype(LOW)
        v[:, cols] = part
        vt[cols, :] = part.T
    ht[...] = hidden[...].T
    leave(1, 2, 3, 4)
    pl.semaphore_wait(barrier, members - 1)
    frames = mel_h.shape[1]
    place = pl.ds(pl.multiple_of(8 + tm * frames, 8), frames)

    def pass_on(step):
        peer = lax.rem(tm + step, members)
        return pltpu.make_async_remote_copy(
            src_ref=mel_h.at[peer],
            dst_ref=mel.at[place],
            send_sem=send_sem.at[step],
            recv_sem=recv_sem.at[step],
            device_id=(peer, clip),
            device_id_type=MESH,
        )

    @pl.loop(1, members)
    def _(step):
        pass_on(step).start()

    stay = pltpu.make_async_copy(mel_h.at[tm], mel.at[place], own_sem)
    stay.start()
    mel[0:8, :] = jnp.zeros((8, mel.shape[1]), WIDE)
    mel[mel.shape[0] - 8 :, :] = jnp.zeros((8, mel.shape[1]), WIDE)
    attend(q, k, vt, bias, ot, inverse, raised, leave.scores(5, 9))
    leave(6, 7)
    fetch.wait(3)
    mixed = ot[...].astype(LOW).T
    for at, width in strips(D, 256):
        cols = pl.ds(at, width)
        x1[:, cols] = x_ref[:, cols].astype(WIDE) + dot(mixed, output_w[:, cols])
    leave(0)

    @pl.loop(1, members)
    def _(step):
        pass_on(step).wait()

    stay.wait()
    leave(8)
    leave.finish()


def held_like(shapes):
    return [pltpu.VMEM(shape.shape, shape.dtype) for shape in shapes]


def self_forward(lengths, inputs, gain, mel_frames, members, weights):
    rows = inputs.shape[0]
    mel = jnp.transpose(mel_frames.astype(WIDE), (1, 0, 2))
    arrived = (members * mel.shape[1] + 16, mel.shape[2])
    plain, turned = (rows, D), (D, rows)
    outs = (
        shape_of(plain, WIDE), shape_of(turned), shape_of(plain), shape_of(turned),
        shape_of(plain), shape_of((HEADS, rows, rows)), shape_of((HEADS, 8, rows), WIDE),
        shape_of(turned, WIDE), shape_of(arrived, WIDE),
    )
    x1, *layer, arrived = pl.pallas_call(
        functools.partial(self_kernel, members),
        out_shape=outs,
        in_specs=[NUMBERS, INSIDE, INSIDE] + [FAR] * 5,
        out_specs=(FAR,) * 9,
        scratch_shapes=held_like(outs)
        + [pltpu.VMEM((D, D), LOW)] * 4
        + [
            pltpu.VMEM(plain, LOW),
            pltpu.VMEM(plain, LOW),
            pltpu.VMEM(turned, LOW),
            pltpu.VMEM((rows, rows), WIDE),
            pltpu.SemaphoreType.DMA((4,)),
            pltpu.SemaphoreType.DMA((9 + PAIRS,)),
            pltpu.SemaphoreType.DMA(()),
            pltpu.SemaphoreType.DMA((members,)),
            pltpu.SemaphoreType.DMA((members,)),
        ],
        compiler_params=pltpu.CompilerParams(
            collective_id=1, has_side_effects=True, vmem_limit_bytes=58 * 2**20
        ),
    )(lengths, inputs, gain, mel, *weights)
    return x1, Layer(*layer), arrived


def cross_kernel(
    length_ref, x1_ref, encoded_ref, cotangent_ref, gain_cross_ref, gain_mlp_ref,
    output_h, query_h, key_h, value_h, *refs
):
    outs, held = refs[:11], refs[11:22]
    output_w, query_w, key_w, value_w, k, vt, semaphores, out_sem = refs[22:]
    x2, hidden, hidden_t, b3, ht, q, kt, v, raised, inverse, ot = held
    leave = Leave(held, outs, out_sem)
    fetch = Fetch(
        (query_h, key_h, value_h, output_h), (query_w, key_w, value_w, output_w), semaphores
    )
    rows = x1_ref.shape[0]
    hidden[...] = (center(x1_ref[...])[0] * gain_cross_ref[...]).astype(LOW)
    fetch.wait(0)
    fetch.wait(1)
    fetch.wait(2)
    for at, width in strips(D, 256):
        cols = pl.ds(at, width)
        q[:, cols] = (dot(hidden[...], query_w[:, cols]).astype(LOW) * SCALE).astype(LOW)
        part = dot(encoded_ref[...], key_w[:, cols]).astype(LOW)
        k[:, cols] = part
        kt[cols, :] = part.T
        part = dot(encoded_ref[...], value_w[:, cols]).astype(LOW)
        v[:, cols] = part
        vt[cols, :] = part.T
    ht[...] = hidden[...].T
    live = lax.broadcasted_iota(jnp.int32, (rows, D), 0) < length_ref[0]
    b3[...] = jnp.where(live, cotangent_ref[...].astype(WIDE), 0.0).astype(LOW)
    leave(3, 4, 5, 6, 7)
    attend(q, k, vt, None, ot, inverse, raised, leave.scores(8, 11))
    leave(9, 10)
    fetch.wait(3)
    mixed = ot[...].astype(LOW).T
    for at, width in strips(D, 256):
        cols = pl.ds(at, width)
        x2[:, cols] = x1_ref[:, cols] + dot(mixed, output_w[:, cols])
    leave(0)
    hidden[...] = (center(x2[...])[0] * gain_mlp_ref[...]).astype(LOW)
    leave(1)
    hidden_t[...] = hidden[...].T
    leave(2)
    leave.finish()


def cross_forward(lengths, x1, encoded, cotangent, gain_cross, gain_mlp, weights):
    rows, frames = x1.shape[0], encoded.shape[0]
    plain, turned = (rows, D), (D, rows)
    outs = (
        shape_of(plain, WIDE), shape_of(plain), shape_of(turned), shape_of(plain),
        shape_of(turned), shape_of(plain), shape_of((D, frames)), shape_of((frames, D)),
        shape_of((HEADS, frames, rows)), shape_of((HEADS, 8, rows), WIDE),
        shape_of(turned, WIDE),
    )
    x2, hidden, hidden_t, b3, *layer = pl.pallas_call(
        cross_kernel,
        out_shape=outs,
        in_specs=[NUMBERS] + [INSIDE] * 5 + [FAR] * 4,
        out_specs=(FAR,) * 11,
        scratch_shapes=held_like(outs)
        + [pltpu.VMEM(weight.shape, LOW) for weight in weights]
        + [
            pltpu.VMEM((frames, D), LOW),
            pltpu.VMEM((D, frames), LOW),
            pltpu.SemaphoreType.DMA((4,)),
            pltpu.SemaphoreType.DMA((11 + PAIRS,)),
        ],
        compiler_params=parameters(),
    )(lengths, x1, encoded, cotangent, gain_cross, gain_mlp, *weights)
    return x2, hidden, hidden_t, b3, Layer(*layer)


def feed_kernel(
    length_ref, x2_ref, hidden, hidden_t, b3, gain_ref, expand_h, narrow_h,
    out_ref, g2_ref, gain_grad_ref, expand_grad_ref, narrow_grad_ref,
    expand_w, narrow_w, x3, back, semaphores,
):
    fetch = Fetch((expand_h, narrow_h), (expand_w, narrow_w), semaphores)
    x3[...] = x2_ref[...]
    back[...] = jnp.zeros_like(back)
    fetch.wait(0)
    fetch.wait(1)

    @pl.loop(0, expand_w.shape[1] // 512)
    def _(strip):
        cols = pl.ds(pl.multiple_of(strip * 512, 512), 512)
        active, slope = gelu_both(dot(hidden[...], expand_w[:, cols]))
        active = active.astype(LOW)
        grad = (slope * dot_back(b3[...], narrow_w[cols, :])).astype(LOW)
        x3[...] += dot(active, narrow_w[cols, :])
        narrow_grad_ref[cols, :] = dot_rows(active, b3[...]).astype(LOW)
        expand_grad_ref[:, cols] = dot(hidden_t[...], grad).astype(LOW)
        back[...] += dot_back(grad, expand_w[:, cols])

    live = lax.broadcasted_iota(jnp.int32, x3.shape, 0) < length_ref[0]
    out_ref[...] = jnp.where(live, x3[...], 0.0).astype(LOW)
    part, gain_part = center_back(back[...], x2_ref[...], gain_ref[...])
    gain_grad_ref[...] = gain_part
    g2_ref[...] = b3[...].astype(WIDE) + part


def feed_both(lengths, x2, hidden, hidden_t, b3, gain_mlp, expand, narrow):
    plain = x2.shape
    return pl.pallas_call(
        feed_kernel,
        out_shape=(
            shape_of(plain), shape_of(plain, WIDE), shape_of((1, D), WIDE),
            shape_of(expand.shape), shape_of(narrow.shape),
        ),
        in_specs=[NUMBERS] + [INSIDE] * 5 + [FAR] * 2,
        out_specs=(INSIDE,) * 5,
        scratch_shapes=[
            pltpu.VMEM(expand.shape, LOW),
            pltpu.VMEM(narrow.shape, LOW),
            pltpu.VMEM(plain, WIDE),
            pltpu.VMEM(plain, WIDE),
            pltpu.SemaphoreType.DMA((2,)),
        ],
        compiler_params=parameters(),
    )(lengths, x2, hidden, hidden_t, b3, gain_mlp, expand, narrow)


def spread_grads(out_grad, output_w, inverse_ref, ot_ref, delta_ref, dov, dot_t):
    for at, width in strips(D, 256):
        part = dot_back(out_grad, output_w[at : at + width, :]).astype(LOW).T
        sides = []
        for number in range(width // HD):
            head = at // HD + number
            side = part[number * HD : (number + 1) * HD, :].astype(WIDE)
            side = (side * inverse_ref[head, 0:1, :]).astype(LOW)
            mixed = ot_ref[head * HD : (head + 1) * HD, :]
            delta = jnp.sum(mixed * side.astype(WIDE), axis=0, keepdims=True)
            delta_ref[head] = jnp.broadcast_to(delta, delta_ref.shape[1:])
            sides.append(side)
        part = jnp.concatenate(sides, axis=0)
        dot_t[at : at + width, :] = part
        dov[:, at : at + width] = part.T


def cross_back_kernel(
    g2_ref, x1_ref, gain_ref, ht_ref, q_ref, kt_ref, v_ref, raised_ref, inverse_ref, ot_ref,
    encoded_t_ref, output_h, query_h, key_h, value_h,
    g1_ref, gain_grad_ref, state_grad_ref, query_g, key_g, value_g, output_g,
    output_w, query_w, key_w, value_w, dov, dot_t, dqt, dk, dv, delta, semaphores,
):
    fetch = Fetch(
        (output_h, query_h, key_h, value_h), (output_w, query_w, key_w, value_w), semaphores
    )
    b2 = g2_ref[...].astype(LOW)
    fetch.wait(0)
    spread_grads(b2, output_w, inverse_ref, ot_ref, delta, dov, dot_t)
    mixed = ot_ref[...].astype(LOW)
    for at, width in strips(D, 256):
        output_g[:, at : at + width] = dot(mixed, b2[:, at : at + width]).astype(LOW)
    attend_back(q_ref, kt_ref, v_ref, raised_ref, delta, dot_t, dov, dqt, dk, dv)
    dq = dqt[...].T
    for place in range(1, 4):
        fetch.wait(place)
    for at, width in strips(D, 256):
        cols = slice(at, at + width)
        query_g[:, cols] = dot(ht_ref[...], dq[:, cols]).astype(LOW)
        key_g[:, cols] = dot(encoded_t_ref[...], dk[:, cols]).astype(LOW)
        value_g[:, cols] = dot(encoded_t_ref[...], dv[:, cols]).astype(LOW)
        state_grad_ref[:, cols] = dot_back(dk[...], key_w[cols, :]) + dot_back(
            dv[...], value_w[cols, :]
        )
    part, gain_part = center_back(dot_back(dq, query_w[...]), x1_ref[...], gain_ref[...])
    gain_grad_ref[...] = gain_part
    g1_ref[...] = g2_ref[...] + part


def cross_backward(operands, weights):
    rows, frames = operands[0].shape[0], operands[10].shape[1]
    plain, turned, square = (rows, D), (D, rows), shape_of((D, D))
    return pl.pallas_call(
        cross_back_kernel,
        out_shape=(
            shape_of(plain, WIDE), shape_of((1, D), WIDE), shape_of((frames, D), WIDE),
            square, square, square, square,
        ),
        in_specs=[INSIDE] * 11 + [FAR] * 4,
        out_specs=(INSIDE,) * 7,
        scratch_shapes=[pltpu.VMEM((D, D), LOW)] * 4
        + [
            pltpu.VMEM(plain, LOW),
            pltpu.VMEM(turned, LOW),
            pltpu.VMEM(turned, LOW),
            pltpu.VMEM((frames, D), LOW),
            pltpu.VMEM((frames, D), LOW),
            pltpu.VMEM((HEADS, 8, rows), WIDE),
            pltpu.SemaphoreType.DMA((4,)),
        ],
        compiler_params=parameters(),
    )(*operands, *weights)


def self_back_kernel(
    g1_ref, x_ref, gain_ref, ht_ref, q_ref, kt_ref, v_ref, raised_ref, inverse_ref, ot_ref,
    output_h, query_h, key_h, value_h,
    input_grad_ref, gain_grad_ref, query_g, key_g, value_g, output_g,
    output_w, query_w, key_w, value_w, dov, dot_t, dqt, dk, dv, delta, semaphores,
):
    fetch = Fetch(
        (output_h, query_h, key_h, value_h), (output_w, query_w, key_w, value_w), semaphores
    )
    b1 = g1_ref[...].astype(LOW)
    fetch.wait(0)
    spread_grads(b1, output_w, inverse_ref, ot_ref, delta, dov, dot_t)
    mixed = ot_ref[...].astype(LOW)
    for at, width in strips(D, 256):
        output_g[:, at : at + width] = dot(mixed, b1[:, at : at + width]).astype(LOW)
    attend_back(q_ref, kt_ref, v_ref, raised_ref, delta, dot_t, dov, dqt, dk, dv)
    dq = dqt[...].T
    for place in range(1, 4):
        fetch.wait(place)
    for at, width in strips(D, 256):
        cols = slice(at, at + width)
        query_g[:, cols] = dot(ht_ref[...], dq[:, cols]).astype(LOW)
        key_g[:, cols] = dot(ht_ref[...], dk[:, cols]).astype(LOW)
        value_g[:, cols] = dot(ht_ref[...], dv[:, cols]).astype(LOW)
        input_grad_ref[:, cols] = (
            dot_back(dq, query_w[cols, :])
            + dot_back(dk[...], key_w[cols, :])
            + dot_back(dv[...], value_w[cols, :])
        )
    part, gain_part = center_back(
        input_grad_ref[...], x_ref[...].astype(WIDE), gain_ref[...]
    )
    gain_grad_ref[...] = gain_part
    input_grad_ref[...] = g1_ref[...] + part


def self_backward(operands, weights):
    rows = operands[0].shape[0]
    plain, turned, square = (rows, D), (D, rows), shape_of((D, D))
    return pl.pallas_call(
        self_back_kernel,
        out_shape=(shape_of(plain, WIDE), shape_of((1, D), WIDE), square, square, square, square),
        in_specs=[INSIDE] * 10 + [FAR] * 4,
        out_specs=(INSIDE,) * 6,
        scratch_shapes=[pltpu.VMEM((D, D), LOW)] * 4
        + [
            pltpu.VMEM(plain, LOW),
            pltpu.VMEM(turned, LOW),
            pltpu.VMEM(turned, LOW),
            pltpu.VMEM(plain, LOW),
            pltpu.VMEM(plain, LOW),
            pltpu.VMEM((HEADS, 8, rows), WIDE),
            pltpu.SemaphoreType.DMA((4,)),
        ],
        compiler_params=parameters(),
    )(*operands, *weights)


def trade(values, axis, size, bit):
    return lax.ppermute(values, axis, [(i, i ^ bit) for i in range(size)])


def add_rounded(left, right):
    return (left.astype(jnp.float32) + right.astype(jnp.float32)).astype(jnp.bfloat16)


def halve(values, dim, axis, size, bit):
    mine = (lax.axis_index(axis) // bit) % 2
    kept = lax.dynamic_index_in_dim(values, mine, dim, keepdims=False)
    sent = lax.dynamic_index_in_dim(values, 1 - mine, dim, keepdims=False)
    return add_rounded(kept, trade(sent, axis, size, bit))


def bits_of(size):
    return [1 << k for k in range(size.bit_length() - 1)]


def members_first(values, members, groups):
    for bit in bits_of(members):
        values = halve(values, len(values.shape) - 3, "tm", members, bit)
    for bit in bits_of(groups):
        values = add_rounded(values, trade(values, "clip", groups, bit))
    return values.astype(jnp.float32)


def groups_first(values, members, groups):
    values = halve(values, len(values.shape) - 3, "tm", members, 1)
    lead = values.shape[:-2]
    rows, columns = values.shape[-2:]
    for bit in bits_of(groups):
        values = values.reshape(lead + (2, values.shape[-2] // 2, columns))
        values = halve(values, len(lead), "clip", groups, bit)
    for bit in bits_of(members)[1:]:
        values = halve(values, len(values.shape) - 3, "tm", members, bit)
    for bit in bits_of(groups)[::-1]:
        mine = (lax.axis_index("clip") // bit) % 2
        other = trade(values, "clip", groups, bit)
        values = jnp.where(
            mine == 0, jnp.concatenate([values, other]), jnp.concatenate([other, values])
        )
    return values.astype(jnp.float32)


def sum_plain(matrices, gains, members, groups):
    split = (2,) * (members.bit_length() - 1)
    totals = []
    for place, matrix in enumerate(matrices):
        blocks = matrix.reshape(split + (matrix.shape[0] // members, matrix.shape[1]))
        totals.append((members_first, groups_first)[place % 2](blocks, members, groups))
    return tuple(totals), lax.psum(gains, ("tm", "clip"))


PART = 48
UNITS = 16
UNIT_ORDER = (8, 9, 10, 11, 12, 13, 14, 15, 7, 4, 5, 6, 3, 0, 1, 2)
LETTERS = "ABCBABAACBBBABBB"
STEPS = (
    1000, 1001, 0, 1002, 1003, 8, 1004, 1, 1005, 1006, 1007, 9, 1008, 1009, 16, 1010,
    1011, 24, 1012, 2, 17, 1013, 1014, 1015, 10, 56, 25, 32, 40, 1016, 48, 1017,
    57, 3, 33, 1018, 64, 41, 11, 1019, 1020, 72, 18, 65, 49, 1021, 12, 1022,
    80, 4, 73, 58, 1023, 42, 1024, 88, 81, 5, 1025, 34, 26, 1026, 66, 89,
    19, 1027, 96, 1028, 50, 97, 59, 13, 1029, 104, 1030, 43, 105, 35, 82, 1031,
    112, 27, 1032, 51, 113, 74, 1033, 120, 14, 90, 1034, 128, 98, 44, 121, 67,
    28, 129, 106, 83, 99, 75, 60, 20, 114, 91, 36, 84, 29, 130, 45, 52,
    76, 68, 107, 92, 122, 100, 131, 61, 85, 115, 108, 21, 77, 37, 123, 30,
    93, 46, 132, 116, 53, 124, 109, 69, 101, 117, 86, 78, 94, 125, 133, 110,
    118, 126,
)


def add_halves(left, right):
    return left + right


class Sums:
    def __init__(self, made, emit, s):
        self.made, self.emit = made, emit
        self.got0, self.a, self.b = s.got0, (s.a1, s.a2, s.a3, s.a4), (s.b1, s.b2, s.b3, s.b4, s.b5)
        self.send_sem, self.recv_sem = s.send_sem, s.recv_sem
        self.gain_send, self.gain_recv = s.gain_send, s.gain_recv
        self.gain_sum, self.gain_got = s.gain_sum, s.gain_got
        tm, clip = lax.axis_index("tm"), lax.axis_index("clip")
        self.core, self.x, self.low, self.high = tm % 2, (tm // 2) % 2, (tm // 4) % 2, tm // 8
        self.core_peer = (tm + 1 - 2 * self.core, clip)
        self.x_peer = (tm + 2 - 4 * self.x, clip)
        self.low_peer = (tm + 4 - 8 * self.low, clip)
        self.high_peer = (tm + 8 - 16 * self.high, clip)
        self.clip_peer = (tm, 1 - clip)
        self.peers = (self.core_peer, self.x_peer, self.low_peer, self.high_peer, self.clip_peer)
        half = D // 2
        self.mine = pl.ds(pl.multiple_of(clip * half, half), half)
        self.other = pl.ds(pl.multiple_of((1 - clip) * half, half), half)
        self.copies, self.gain_copies, self.places = {}, {}, {}
        self.started, self.left = [], set()
        self.slots = {
            place: sum((LETTERS[k] == "B") == (LETTERS[place] == "B") for k in range(place))
            for place in range(UNITS)
        }

    def meet(self):
        barrier = pltpu.get_barrier_semaphore()
        for peer in self.peers:
            pl.semaphore_signal(barrier, inc=1, device_id=peer, device_id_type=MESH)
        pl.semaphore_wait(barrier, len(self.peers))

    def send(self, src, dst, stage, place, peer):
        copy = pltpu.make_async_remote_copy(
            src_ref=src,
            dst_ref=dst,
            send_sem=self.send_sem.at[stage, place],
            recv_sem=self.recv_sem.at[stage, place],
            device_id=peer,
            device_id_type=MESH,
        )
        copy.start()
        self.places[stage, place] = len(self.started)
        self.started.append(copy)
        self.copies[stage, place] = copy

    def step(self, stage, place):
        if stage == 0:
            buffer, number = self.made(place)
            source = buffer.at[:, :, :, 1 - self.core, number]
            self.send(source, self.got0.at[place], 0, place, self.core_peer)
            return
        self.copies[stage - 1, place].wait_recv()
        if stage == 1:
            self.add_cores(place)
        step = dict(A=self.step_a, B=self.step_b, C=self.step_c)[LETTERS[place]]
        step(stage, place, self.slots[place])

    def add_cores(self, place):
        got0 = self.got0
        buffer, number = self.made(place)

        @pl.loop(0, 8)
        def _(block):
            i, j, k = block // 4, (block // 2) % 2, block % 2
            mine = buffer[i, j, k, self.core, number]
            got0[place, i, j, k] = add_halves(got0[place, i, j, k], mine)

    def step_a(self, stage, place, slot):
        got0, (a1, a2, a3, a4) = self.got0, self.a
        if stage == 1:
            source = got0.at[place, :, :, 1 - self.x]
            self.send(source, a1.at[slot], 1, place, self.x_peer)
        elif stage == 2:

            @pl.loop(0, 4)
            def _(block):
                i, j = block // 2, block % 2
                a1[slot, i, j] = add_halves(a1[slot, i, j], got0[place, i, j, self.x])

            self.send(a1.at[slot, :, 1 - self.low], a2.at[slot], 2, place, self.low_peer)
        elif stage == 3:

            @pl.loop(0, 2)
            def _(i):
                a2[slot, i] = add_halves(a2[slot, i], a1[slot, i, self.low])

            self.send(a2.at[slot, 1 - self.high], a3.at[slot], 3, place, self.high_peer)
        else:
            self.last_two(stage, place, slot, self.high)

    def step_c(self, stage, place, slot):
        got0, (a1, a2, a3, a4) = self.got0, self.a
        if stage == 1:
            source = got0.at[place, :, 1 - self.low]
            self.send(source, a1.at[slot], 1, place, self.low_peer)
        elif stage == 2:

            @pl.loop(0, 4)
            def _(block):
                i, j = block // 2, block % 2
                a1[slot, i, j] = add_halves(a1[slot, i, j], got0[place, i, self.low, j])

            self.send(a1.at[slot, 1 - self.high], a2.at[slot], 2, place, self.high_peer)
        elif stage == 3:

            @pl.loop(0, 2)
            def _(i):
                a2[slot, i] = add_halves(a2[slot, i], a1[slot, self.high, i])

            self.send(a2.at[slot, 1 - self.x], a3.at[slot], 3, place, self.x_peer)
        else:
            self.last_two(stage, place, slot, self.x)

    def last_two(self, stage, place, slot, side):
        a1, a2, a3, a4 = self.a
        if stage == 4:
            a3[slot] = add_halves(a3[slot], a2[slot, side])
            self.send(a3.at[slot], a4.at[slot], 4, place, self.clip_peer)
        else:
            total = a3[slot].astype(WIDE) + a4[slot].astype(WIDE)
            self.emit(UNIT_ORDER[place], slice(0, D), total)

    def step_b(self, stage, place, slot):
        got0, (b1, b2, b3, b4, b5) = self.got0, self.b
        if stage == 1:
            source = got0.at[place, :, :, :, :, self.other]
            self.send(source, b1.at[slot], 1, place, self.clip_peer)
        elif stage == 2:

            @pl.loop(0, 8)
            def _(block):
                i, j, k = block // 4, (block // 2) % 2, block % 2
                b1[slot, i, j, k] = add_halves(
                    b1[slot, i, j, k], got0[place, i, j, k, :, self.mine]
                )

            self.send(b1.at[slot, :, :, 1 - self.x], b2.at[slot], 2, place, self.x_peer)
        elif stage == 3:

            @pl.loop(0, 4)
            def _(block):
                i, j = block // 2, block % 2
                b2[slot, i, j] = add_halves(b2[slot, i, j], b1[slot, i, j, self.x])

            self.send(b2.at[slot, :, 1 - self.low], b3.at[slot], 3, place, self.low_peer)
        elif stage == 4:

            @pl.loop(0, 2)
            def _(i):
                b3[slot, i] = add_halves(b3[slot, i], b2[slot, i, self.low])

            self.send(b3.at[slot, 1 - self.high], b4.at[slot], 4, place, self.high_peer)
        elif stage == 5:
            b4[slot] = add_halves(b4[slot], b3[slot, self.high])
            self.send(b4.at[slot], b5.at[slot], 5, place, self.clip_peer)
        else:
            self.emit(UNIT_ORDER[place], self.mine, b4[slot].astype(WIDE))
            self.emit(UNIT_ORDER[place], self.other, b5[slot].astype(WIDE))

    def gain_step(self, number):
        if number > 0:
            self.gain_copies[number - 1].wait_recv()
            self.gain_sum[number] = self.gain_sum[number - 1] + self.gain_got[number - 1]
        if number < len(self.peers):
            copy = pltpu.make_async_remote_copy(
                src_ref=self.gain_sum.at[number],
                dst_ref=self.gain_got.at[number],
                send_sem=self.gain_send.at[number],
                recv_sem=self.gain_recv.at[number],
                device_id=self.peers[number],
                device_id_type=MESH,
            )
            copy.start()
            self.started.append(copy)
            self.gain_copies[number] = copy

    def leave(self, place):
        self.copies[0, place].wait_send()
        self.left.add(self.places[0, place])

    def finish(self):
        for number, copy in enumerate(self.started):
            if number not in self.left:
                copy.wait_send()


class BackIn(NamedTuple):
    length: Any
    x2: Any
    hidden: Any
    hidden_t: Any
    b3: Any
    x1: Any
    x: Any
    encoded_t: Any
    gain_mlp: Any
    gain_cross: Any
    gain_self: Any
    expand_w: Any
    narrow_w: Any
    cross: Layer
    own: Layer
    cross_w: Weights
    own_w: Weights


class BackOut(NamedTuple):
    output: Any
    input_grad: Any
    state_grad: Any
    summed: Any
    gains: Any


class Room(NamedTuple):
    x1: Any
    encoded_t: Any
    cross: Layer
    own: Layer
    weight: Any
    raised: Any
    ot: Any
    delta: Any
    g: Any
    x3: Any
    low: Any
    dov: Any
    dot_t: Any
    dqt: Any
    dk: Any
    dv: Any
    kept: Any
    narrow: Any
    total: Any
    got0: Any
    a1: Any
    a2: Any
    a3: Any
    a4: Any
    b1: Any
    b2: Any
    b3: Any
    b4: Any
    b5: Any
    gain_sum: Any
    gain_got: Any
    fetch_sem: Any
    raised_sem: Any
    out_sem: Any
    send_sem: Any
    recv_sem: Any
    gain_send: Any
    gain_recv: Any


class Once:
    def __init__(self, copy):
        self.copy, self.pending = copy, True
        copy.start()

    def ready(self):
        if self.pending:
            self.copy.wait()
        self.pending = False


def back_kernel(tree, *refs):
    given, out, s = jax.tree.unflatten(tree, refs)
    count = [0]

    def fetch(source, target):
        copy = pltpu.make_async_copy(source, target, s.fetch_sem.at[count[0]])
        count[0] += 1
        return Once(copy)

    def fetch_layer(source, target):
        return {
            field: fetch(getattr(source, field), getattr(target, field))
            for field in Layer._fields
            if getattr(target, field) is not None
        }

    def raised_copy(layer, pair):
        source = layer.raised.at[pl.ds(2 * pair, 2)]
        slot = pair % 2
        return pltpu.make_async_copy(
            source, s.raised.at[slot, :, pl.ds(0, source.shape[1])], s.raised_sem.at[slot]
        )

    def made(place):
        if 4 <= place < 8 or place >= 12:
            return s.narrow, place % 4
        return s.kept, place % 4 + 4 * (place >= 8)

    def keep(place, at, width, values):
        buffer, number = made(place)
        buffer[:, :, :, :, number, :, at : at + width] = values.astype(LOW).reshape(
            2, 2, 2, 2, PART, width
        )

    def emit(unit, cols, total):
        s.total[unit, :, cols] = total

    sums = Sums(made, emit, s)
    live = {}
    waits = {}

    def feed_room(strip, half):
        cols = pl.ds(half * (D // 2), D // 2)
        if strip % 2 == 0:
            return s.dov.at[:, cols], s.dv.at[:, cols]
        cols = pl.ds(0, D // 2)
        return s.raised.at[0, half, :, cols], s.raised.at[1, half, :, cols]

    def feed_first(strip, half):
        def run():
            first, second = s.weight[2 * (strip % 2)], s.weight[2 * (strip % 2) + 1]
            for name in ("hidden", "hidden_t", "b3", "x2"):
                waits[name].ready()
            width = D // 2
            cols = slice(half * width, (half + 1) * width)
            waits["first", strip].ready()
            active, slope = gelu_both(dot(s.dk[...], first[:, cols]))
            waits["second", strip].ready()
            grad = (slope * dot_back(s.low[...], second[cols, :])).astype(LOW)
            keep(strip, half * width, width, dot(s.dot_t[...], grad))
            active_ref, grad_ref = feed_room(strip, half)
            active_ref[...] = active.astype(LOW)
            grad_ref[...] = grad

        return run

    def feed_second(strip, half):
        def run():
            first, second = s.weight[2 * (strip % 2)], s.weight[2 * (strip % 2) + 1]
            cols = slice(half * (D // 2), (half + 1) * (D // 2))
            active, grad = [part[...] for part in feed_room(strip, half)]
            s.narrow[strip // 2, strip % 2, half] = (
                dot_rows(active, s.low[...]).astype(LOW).reshape(2, 4, PART, D)
            )
            forward, backward = dot(active, second[cols, :]), dot_back(grad, first[:, cols])
            if strip == 0 and half == 0:
                s.x3[...] = s.x1[...] + forward
                s.g[...] = backward
            else:
                s.x3[...] += forward
                s.g[...] += backward
            if strip < 2 and half:
                fetch_feed(strip + 2)

        return run

    def fetch_feed(strip):
        cols = pl.ds(strip * D, D)
        waits["first", strip] = fetch(given.expand_w.at[:, cols], s.weight[2 * (strip % 2)])
        waits["second", strip] = fetch(given.narrow_w.at[cols, :], s.weight[2 * (strip % 2) + 1])

    def feed_end():
        raised_copy(given.cross, 0).start()
        raised_copy(given.cross, 1).start()
        for place, name in enumerate(Weights._fields):
            waits["cross", name] = fetch(getattr(given.cross_w, name), s.weight[place])
        live = lax.broadcasted_iota(jnp.int32, s.x3.shape, 0) < given.length[0]
        s.dv[...] = jnp.where(live, s.x3[...], 0.0).astype(LOW)
        waits["output"] = Once(pltpu.make_async_copy(s.dv, out.output, s.out_sem.at[0]))
        part, gain_part = center_back(s.g[...], s.x1[...], given.gain_mlp[...])
        s.gain_sum[0, 2:3, :] = gain_part
        s.g[...] = s.low[...].astype(WIDE) + part
        waits["x1"] = fetch(given.x1, s.x1)

    def spread(layer, room, name):
        def run():
            waits[name, "output"].ready()
            waits[name]["inverse"].ready()
            s.low[...] = s.g[...].astype(LOW)
            waits[name, "ot"].ready()
            spread_grads(s.low[...], s.weight[0], room.inverse, s.ot, s.delta, s.dov, s.dot_t)
            if name == "cross":
                waits["own", "output"] = fetch(given.own_w.output, s.weight[0])

        return run

    def output_grad(room, name, place):
        def run():
            if name == "own":
                for unit in range(4, 8):
                    sums.leave(unit)
            mixed = s.ot[...].astype(LOW)
            for at, width in strips(D, 256):
                keep(place, at, width, dot(mixed, s.low[:, at : at + width]))
            if name == "cross":
                waits["own", "ot"] = fetch(given.own.ot, s.ot)

        return run

    def attention(layer, room, name, first):
        def run():
            for field in ("q", "kt", "v"):
                waits[name][field].ready()
            waits["output"].ready()
            inner = layer.raised.shape[1]

            @pl.loop(first, first + 2)
            def _(pair):
                raised_copy(layer, pair).wait()
                slot = pair % 2
                attend_pair(
                    pair,
                    room.q,
                    room.kt,
                    room.v,
                    s.raised.at[slot, :, pl.ds(0, inner)],
                    s.delta,
                    s.dot_t,
                    s.dov,
                    s.dqt,
                    s.dk.at[pl.ds(0, inner)],
                    s.dv.at[pl.ds(0, inner)],
                )
                if first < PAIRS - 2:
                    raised_copy(layer, pair + 2).start()
                elif name == "cross":
                    raised_copy(given.own, slot).start()

        return run

    def strip_grads(first_t, second_t, inner, strip, place):
        cols = slice(256 * strip, 256 * (strip + 1))
        part = s.dqt[cols, :].T
        s.low[:, cols] = part
        keep(place, 0, 256, dot(first_t[...], part))
        keep(place, 256, 256, dot(second_t[...], s.dk[0:inner, cols]))
        keep(place, 512, 256, dot(second_t[...], s.dv[0:inner, cols]))

    def cross_grads(strip):
        def run():
            waits["cross"]["ht"].ready()
            waits["encoded_t"].ready()
            strip_grads(s.cross.ht, s.encoded_t, s.encoded_t.shape[1], strip, 9 + strip)

        return run

    def cross_inputs():
        for name in ("query", "key", "value"):
            waits["cross", name].ready()
        waits["x1"].ready()
        frames = s.encoded_t.shape[1]
        for at, width in strips(D, 256):
            cols = slice(at, at + width)
            s.x3[0:frames, cols] = dot_back(s.dk[0:frames, :], s.weight[2][cols, :]) + dot_back(
                s.dv[0:frames, :], s.weight[3][cols, :]
            )
        state = s.x3.at[pl.ds(0, frames)]
        waits["state"] = Once(pltpu.make_async_copy(state, out.state_grad, s.out_sem.at[1]))
        part, gain_part = center_back(
            dot_back(s.low[...], s.weight[1][...]), s.x1[...], given.gain_cross[...]
        )
        s.gain_sum[0, 1:2, :] = gain_part
        s.g[...] += part
        for place, name in enumerate(Weights._fields):
            if place:
                waits["own", name] = fetch(getattr(given.own_w, name), s.weight[place])

    def self_grads(strip):
        def run():
            waits["own"]["ht"].ready()
            strip_grads(s.own.ht, s.own.ht, s.own.ht.shape[1], strip, 13 + strip)
            if strip == 2:
                waits["x"] = fetch(given.x, s.dov)

        return run

    def self_inputs():
        for name in ("query", "key", "value"):
            waits["own", name].ready()
        waits["x"].ready()
        for at, width in strips(D, 256):
            cols = slice(at, at + width)
            s.x1[:, cols] = (
                dot_back(s.low[...], s.weight[1][cols, :])
                + dot_back(s.dk[...], s.weight[2][cols, :])
                + dot_back(s.dv[...], s.weight[3][cols, :])
            )
        part, gain_part = center_back(s.x1[...], s.dov[...].astype(WIDE), given.gain_self[...])
        s.gain_sum[0, 0:1, :] = gain_part
        s.g[...] += part
        waits["input"] = Once(pltpu.make_async_copy(s.g, out.input_grad, s.out_sem.at[2]))

    pieces = [
        part(strip, half)
        for strips_now in ((0, 1), (2, 3))
        for part in (feed_first, feed_second)
        for strip in strips_now
        for half in range(2)
    ]
    pieces += [feed_end, spread(given.cross, s.cross, "cross"), output_grad(s.cross, "cross", 8)]
    for strip in range(3):
        pieces += [attention(given.cross, s.cross, "cross", 2 * strip), cross_grads(strip)]
    pieces += [cross_inputs, spread(given.own, s.own, "own"), output_grad(s.own, "own", 12)]
    for strip in range(3):
        pieces += [attention(given.own, s.own, "own", 2 * strip), self_grads(strip)]
    pieces.append(self_inputs)
    waits["hidden"] = fetch(given.hidden, s.dk)
    fetch_feed(0)
    waits["b3"] = fetch(given.b3, s.low)
    waits["hidden_t"] = fetch(given.hidden_t, s.dot_t)
    waits["x2"] = fetch(given.x2, s.x1)
    fetch_feed(1)
    waits["cross"] = fetch_layer(given.cross, s.cross)
    waits["cross", "ot"] = fetch(given.cross.ot, s.ot)
    waits["encoded_t"] = fetch(given.encoded_t, s.encoded_t)
    waits["own"] = fetch_layer(given.own, s.own)
    s.gain_sum[0] = jnp.zeros(s.gain_sum.shape[1:], WIDE)
    met = False
    for code in STEPS:
        if code < 1000:
            if not met:
                sums.meet()
                met = True
            if code < UNITS * 8:
                sums.step(code % 8, code // 8)
            else:
                sums.gain_step(code % 8)
        else:
            pieces[code - 1000]()
    out.gains[...] = s.gain_sum[5]
    result = pltpu.make_async_copy(s.total, out.summed, s.out_sem.at[3])
    result.start()
    sums.finish()
    waits["state"].ready()
    waits["input"].ready()
    result.wait()


def room_for(given):
    rows, frames = given.x.shape[0], given.encoded_t.shape[1]
    split = (2, 2, 2, 2)
    thin = LETTERS.count("B")
    thick = UNITS - thin
    half = D // 2

    def low(*shape):
        return pltpu.VMEM(shape, LOW)

    def wide(*shape):
        return pltpu.VMEM(shape, WIDE)

    def like(array):
        return pltpu.VMEM(array.shape, array.dtype)

    def layer(source):
        return jax.tree.map(like, source)._replace(raised=None, ot=None)

    plain, turned = (rows, D), (D, rows)
    dma = pltpu.SemaphoreType.DMA
    return Room(
        x1=like(given.x1), encoded_t=like(given.encoded_t),
        cross=layer(given.cross), own=layer(given.own),
        weight=[low(D, D)] * 4, raised=low(2, 2, rows, rows), ot=wide(*turned),
        delta=like(given.own.inverse),
        g=wide(*plain), x3=wide(*plain), low=low(*plain), dov=low(*plain), dot_t=low(*turned),
        dqt=low(*turned), dk=low(*plain), dv=low(*plain),
        kept=low(*split, 8, PART, D), narrow=low(*split, 4, PART, D),
        total=wide(UNITS, PART, D), got0=low(UNITS, 2, 2, 2, PART, D),
        a1=low(thick, 2, 2, PART, D), a2=low(thick, 2, PART, D), a3=low(thick, PART, D),
        a4=low(thick, PART, D), b1=low(thin, 2, 2, 2, PART, half), b2=low(thin, 2, 2, PART, half),
        b3=low(thin, 2, PART, half), b4=low(thin, PART, half), b5=low(thin, PART, half),
        gain_sum=wide(6, 8, D), gain_got=wide(5, 8, D),
        fetch_sem=dma((40,)), raised_sem=dma((2,)), out_sem=dma((4,)),
        send_sem=dma((6, UNITS)), recv_sem=dma((6, UNITS)), gain_send=dma((5,)),
        gain_recv=dma((5,)),
    )


def backward_and_sum(given):
    rows, frames = given.x.shape[0], given.encoded_t.shape[1]
    outs = BackOut(
        output=shape_of((rows, D)), input_grad=shape_of((rows, D), WIDE),
        state_grad=shape_of((frames, D), WIDE), summed=shape_of((UNITS, PART, D), WIDE),
        gains=shape_of((8, D), WIDE),
    )
    room = room_for(given)
    places = jax.tree.map(lambda _: FAR, given)._replace(
        length=NUMBERS, gain_mlp=INSIDE, gain_cross=INSIDE, gain_self=INSIDE
    )
    results = pl.pallas_call(
        functools.partial(back_kernel, jax.tree.structure((given, outs, room))),
        out_shape=tuple(outs),
        in_specs=jax.tree.leaves(places),
        out_specs=(FAR,) * 4 + (INSIDE,),
        scratch_shapes=jax.tree.leaves(room),
        compiler_params=pltpu.CompilerParams(
            collective_id=0, has_side_effects=True, vmem_limit_bytes=63 * 2**20
        ),
    )(*jax.tree.leaves(given))
    return BackOut(*results)


def cut(matrix, strip):
    return matrix.at[:, pl.ds(256 * strip, 256)]


def finish_kernel(output, input_grad, state_grad, summed, *refs):
    outs, (rows_low, rows_wide, frames_wide, blocks, taken, given) = refs[:13], refs[13:]
    parts = [
        (summed.at[pl.ds(0, 8)], blocks.at[pl.ds(0, 8)]),
        (summed.at[pl.ds(8, 8)], blocks.at[pl.ds(8, 8)]),
        (input_grad, rows_wide),
        (state_grad, frames_wide),
        (output, rows_low),
    ]
    results = [
        [(blocks.at[3], outs[6]), (blocks.at[7], outs[10])]
        + [
            (blocks.at[4 * layer + k, :, pl.ds(256 * m, 256)], cut(outs[3 + 4 * layer + m], k))
            for layer in range(2)
            for k in range(3)
            for m in range(3)
        ],
        [(blocks.at[pl.ds(12, 4)], outs[12])]
        + [(blocks.at[8 + k], outs[11].at[:, pl.ds(k * D, D)]) for k in range(4)],
        [(rows_wide, outs[1])],
        [(frames_wide, outs[2])],
        [(rows_low, outs[0])],
    ]
    arriving = [
        pltpu.make_async_copy(*pair, taken.at[place]) for place, pair in enumerate(parts)
    ]
    for copy in arriving:
        copy.start()
    leaving = []
    for copy, pairs in zip(arriving, results):
        copy.wait()
        for pair in pairs:
            leaving.append(pltpu.make_async_copy(*pair, given.at[len(leaving)]))
            leaving[-1].start()
    for copy in leaving:
        copy.wait()


def finish(made):
    outs = [shape_of(made[k].shape, made[k].dtype) for k in range(3)]
    outs += [shape_of((PART, D), WIDE)] * 8
    outs += [shape_of((PART, 4 * D), WIDE), shape_of((4, PART, D), WIDE)]
    *results, narrow = pl.pallas_call(
        finish_kernel,
        out_shape=tuple(outs),
        in_specs=[FAR] * 4,
        out_specs=(FAR,) * len(outs),
        scratch_shapes=[pltpu.VMEM(array.shape, array.dtype) for array in made[:4]]
        + [pltpu.SemaphoreType.DMA((5,)), pltpu.SemaphoreType.DMA((28,))],
        compiler_params=parameters(62),
    )(*made[:4])
    return *results, narrow.reshape(4 * PART, D)


def body(
    members,
    groups,
    mel_frames,
    conv_first,
    conv_second,
    enc_projection,
    enc_output,
    enc_expand,
    enc_narrow,
    dec_input,
    lengths,
    self_query,
    self_key,
    self_value,
    self_output,
    cross_query,
    cross_key,
    cross_value,
    cross_output,
    mlp_expand,
    mlp_narrow,
    gain_self,
    gain_cross,
    gain_mlp,
    cotangent,
):
    inputs, length = dec_input[0, 0], lengths[0]
    own_w = Weights(self_output, self_query, self_key, self_value)
    x1, own, mel = self_forward(length, inputs, gain_self, mel_frames[:, 0], members, own_w)
    encoded, encoded_t = encode(
        mel, conv_first, conv_second, enc_projection, enc_output, enc_expand, enc_narrow
    )
    cross_w = Weights(cross_output, cross_query, cross_key, cross_value)
    x2, hidden, hidden_t, b3, cross = cross_forward(
        length, x1, encoded, cotangent[0, 0], gain_cross, gain_mlp, cross_w
    )
    if (members, groups) == (16, 2):
        made = backward_and_sum(
            BackIn(
                length, x2, hidden, hidden_t, b3, x1, inputs, encoded_t,
                gain_mlp, gain_cross, gain_self, mlp_expand, mlp_narrow,
                cross, own, cross_w, own_w,
            )
        )
        dec_output, dec_input_grad, enc_state_grad, *totals = finish(made)
        gains = made.gains
    else:
        dec_output, g2, g_gain_mlp, g_expand, g_narrow = feed_both(
            length, x2, hidden, hidden_t, b3, gain_mlp, mlp_expand, mlp_narrow
        )
        g1, g_gain_cross, enc_state_grad, *cross_grads = cross_backward(
            (g2, x1, gain_cross) + tuple(cross) + (encoded_t,), cross_w
        )
        dec_input_grad, g_gain_self, *self_grads = self_backward(
            (g1, inputs, gain_self) + tuple(own), own_w
        )
        gains = jnp.concatenate([g_gain_self, g_gain_cross, g_gain_mlp, jnp.zeros((5, D), WIDE)])
        totals, gains = sum_plain(
            self_grads + cross_grads + [g_expand, g_narrow], gains, members, groups
        )
    part = D // members
    gains = lax.dynamic_slice_in_dim(gains, lax.axis_index("tm") * part, part, 1)
    return (
        encoded[None, None],
        dec_output[None, None],
        dec_input_grad[None, None],
        enc_state_grad[None, None],
        *totals,
        gains[0],
        gains[1],
        gains[2],
    )


def solution(mesh):
    placed = (
        P("tm", "clip", None, None),
        P(),
        P(),
        P(),
        P(),
        P(),
        P(),
        P("clip", "tm", None, None),
        P("clip", "tm"),
        P(),
        P(),
        P(),
        P(),
        P(),
        P(),
        P(),
        P(),
        P(),
        P(),
        P(),
        P(),
        P(),
        P("clip", "tm", None, None),
    )
    return jax.shard_map(
        functools.partial(body, mesh.shape["tm"], mesh.shape["clip"]),
        mesh=mesh,
        in_specs=placed,
        out_specs=(
            P("clip", "tm", None, None),
            P("clip", "tm", None, None),
            P("clip", "tm", None, None),
            P("clip", "tm", None, None),
            P("tm", None),
            P("tm", None),
            P("tm", None),
            P("tm", None),
            P("tm", None),
            P("tm", None),
            P("tm", None),
            P("tm", None),
            P("tm", None),
            P("tm", None),
            P("tm"),
            P("tm"),
            P("tm"),
        ),
        check_vma=False,
    )
```
